128 devices in a mesh: gx: 16 (over z, x), gy: 8 (over y, core).
Axes of the slice: x: 4, y: 4, z: 4, core: 2. Of those that a mesh axis runs over, the one named last changes fastest.
Arguments:
- features: bfloat16 [256, 128, 128, 128], P('gx', 'gy'), may hold values from -30 to 30
- occupancy: int32 [256, 128, 128], P('gx', 'gy'), may hold values 0 or 1
- owner_map: int32 [32, 16, 16], P('gx', 'gy'), may hold values from -1 to 255, as said below
- kernel: bfloat16 [27, 128, 128], replicated, may hold values from -0.109375 to 0.109375
- norm_gain: float32 [128], replicated, may hold values from 0.25 to 1.75
- norm_bias: float32 [128], replicated, may hold values from -2.5 to 2.5
Outputs:
- result: bfloat16 [256, 8, 512, 128], P('gx', 'gy')
The draws below stay inside these ranges and needn't reach their ends.
Inputs may be any that keep to these rules, and one draw needn't show every extreme that they name: `owner_map`: A value g >= 0 hands the brick to the device g // 16 along gx in the brick's own gy row, into its slot g % 16. In every gy row each value 0 to 255 occurs exactly once. One device holds at most 32 active bricks and hands at most 2 of them to one owner; both bounds are reached in every row.
All inputs are finite; a program needn't handle non-finite values. No bound on the sum of `occupancy` on one device may be relied on, other than what follows from the above.
Results may differ from the reference program's by a relative error of at most 0.007.
Values may be sent and summed in bfloat16 or wider, within the bound.
No kernel may reach another device: no remote copies, remote signals or barrier semaphores. Data moves between devices by JAX's collectives and lax.ppermute only.
A program may use at most 320 MiB of HBM per device.

```python
import math
import jax
import jax.numpy as jnp
from jax import lax

C = 128
E = 8
BX = 2
BY = 2
BZ = 16
O = 16
NXV = 256
NYV = 128
NZV = 128
N_GX = 16
N_GY = 8


def owner_table(key):
    key = jax.random.fold_in(key, 23)
    places = BX * BY * BZ
    paired = N_GX // 2

    def one_row(row_key):
        subkeys = jax.random.split(row_key, 4)
        surplus = jax.random.randint(subkeys[0], (paired,), 0, O + 1)
        surplus = surplus.at[0].set(O)
        counts = jnp.concatenate([O + surplus, O - surplus])
        shuffle = jax.random.permutation(subkeys[1], N_GX)
        counts = counts[shuffle]
        starts = jnp.cumsum(counts) - counts
        rotation = jax.random.randint(subkeys[2], (), 0, N_GX)
        position_rank = jax.vmap(lambda device_key: jax.random.permutation(device_key, places))(jax.random.split(subkeys[3], N_GX))
        running = starts[:, None] + position_rank
        owner_index = (running + rotation) % N_GX
        owner_slot = running // N_GX
        return jnp.where(position_rank < counts[:, None], owner_index * O + owner_slot, -1).astype(jnp.int32)
    row_table = jax.vmap(one_row)(jax.random.split(key, N_GY))
    row_table = row_table.reshape(N_GY, N_GX, BX, BY, BZ)
    return row_table.transpose(1, 2, 0, 3, 4).reshape(N_GX * BX, N_GY * BY, BZ)


def draw_owner_map(key, part):
    return owner_table(key)


def draw_features(key, part):
    table = owner_table(key)
    key = jax.random.fold_in(key, 11)
    subkeys = jax.random.split(key, 3)
    shape = (N_GX * BX * E, N_GY * BY * E, BZ * E, C)
    owner_fraction = jnp.maximum(table // O, 0).astype(jnp.float32) / (N_GX - 1)
    owner_fraction = jnp.repeat(jnp.repeat(jnp.repeat(owner_fraction, E, axis=0), E, axis=1), E, axis=2)[..., None]
    x_fraction = jnp.arange(shape[0], dtype=jnp.float32)[:, None, None, None] / (shape[0] - 1)
    y_fraction = jnp.arange(shape[1], dtype=jnp.float32)[None, :, None, None] / (shape[1] - 1)
    direction = jax.random.uniform(subkeys[0], (C,), jnp.float32, -1.0, 1.0)
    scale_rows = jnp.exp(jax.random.uniform(subkeys[1], shape[:3] + (1,), jnp.float32, math.log(0.15), math.log(1.0)))
    ramp = (1.0 + 2.0 * x_fraction) * (1.0 + 2.0 * owner_fraction)
    offset = 0.8 + 2.4 * y_fraction
    noise = jax.random.truncated_normal(subkeys[2], -4.0, 4.0, shape, jnp.float32)
    return (ramp * scale_rows * (offset * direction + noise) / 3.0).astype(jnp.bfloat16)


def set_ends(drawn, key, smallest, high):
    longest = drawn.shape.index(max(drawn.shape))
    spots = []
    for shift in (0, 1):
        where = [jax.random.randint(jax.random.fold_in(key, axis), (), 0, length) for axis, length in enumerate(drawn.shape)]
        where[longest] = (where[longest] + shift) % drawn.shape[longest]
        spots.append(tuple(where))
    return drawn.at[spots[0]].set(smallest).at[spots[1]].set(high)


def gaussian(key, extent, spread, limit, held_as=jnp.bfloat16):
    result = spread * jax.random.normal(key, extent, jnp.float32)
    return jnp.clip(result, min=-limit, max=limit).astype(held_as)


def setup_inputs(seed: int = 0) -> dict:
    keys = jax.random.split(jax.random.key(seed), 7)
    return {
        "features": draw_features(jax.random.fold_in(keys[6], 71), 0),
        "occupancy": set_ends((jax.random.randint(keys[1], (NXV, NYV, NZV), 0, 2) < 1).astype(jnp.int32), jax.random.fold_in(keys[1], 1), 0, 1),
        "owner_map": draw_owner_map(jax.random.fold_in(keys[6], 71), 0),
        "kernel": gaussian(keys[3], (27, C, C), (27 * C) ** -0.5, 0.109375),
        "norm_gain": jnp.clip(1.0 + 0.15 * jax.random.normal(keys[4], (C,), jnp.float32), 0.25, 1.75),
        "norm_bias": gaussian(keys[5], (C,), 0.5, 2.5, jnp.float32),
    }


EPSILON = 1e-05

def convolve_window(windows, kernel):
    amount = windows.shape[0]
    rows_all = amount * E * E * E
    summed = jnp.zeros((rows_all, C), jnp.float32)
    for step_x in range(3):
        for step_y in range(3):
            for step_z in range(3):
                tap_slice = windows[:, step_x:step_x + E, step_y:step_y + E, step_z:step_z + E, :].reshape(rows_all, C)
                summed = summed + jnp.dot(tap_slice, kernel[step_x * 9 + step_y * 3 + step_z], preferred_element_type=jnp.float32)
    return summed.reshape(amount, E * E * E, C)

def finish(convolved, centre, occupied_centre, summed, squared, voxels_on, norm_gain, norm_bias):
    mean_value = summed / voxels_on
    variance = squared / voxels_on - mean_value * mean_value
    factor = norm_gain / jnp.sqrt(variance + EPSILON)
    shifted = factor * (convolved.astype(jnp.float32) - mean_value) + norm_bias
    combined = centre.astype(jnp.float32) + occupied_centre[..., None].astype(jnp.float32) * jax.nn.silu(shifted)
    return combined.astype(jnp.bfloat16)

def reference(features, occupancy, owner_map, kernel, norm_gain, norm_bias):
    span_x, span_y, span_z = owner_map.shape
    active = (owner_map >= 0).astype(jnp.int32)
    occupied = (occupancy.reshape(span_x, E, span_y, E, span_z, E) * active[:, None, :, None, :, None]).reshape(occupancy.shape)
    masked = features * occupied[..., None].astype(jnp.bfloat16)
    padded = jnp.pad(masked, ((1, 1), (1, 1), (1, 1), (0, 0)))
    flat_owner = owner_map.reshape(-1)
    place_index = jnp.arange(flat_owner.shape[0], dtype=jnp.int32)
    row_index = place_index // span_z % span_y // BY
    row_slots = N_GX * O
    target = jnp.where(flat_owner >= 0, row_index * row_slots + flat_owner, N_GY * row_slots).astype(jnp.int32)
    inverse = jnp.zeros((N_GY * row_slots + 1,), jnp.int32).at[target].set(place_index)
    inverse = inverse[:N_GY * row_slots].reshape(N_GY, N_GX, O).transpose(1, 2, 0).reshape(N_GX, O * N_GY)

    def cut_window(start_x, start_y, start_z, start_c):
        return lax.dynamic_slice(padded, (start_x, start_y, start_z, start_c), (E + 2, E + 2, E + 2, C))

    def cut_occupied(start_x, start_y, start_z):
        return lax.dynamic_slice(occupied, (start_x, start_y, start_z), (E, E, E)).reshape(E * E * E)

    def per_block(positions):
        along_x = positions // (span_y * span_z) * E
        along_y = positions // span_z % span_y * E
        along_z = positions % span_z * E
        zero_index = jnp.zeros_like(positions)
        windows = jax.vmap(cut_window)(along_x, along_y, along_z, zero_index)
        occupied_centre = jax.vmap(cut_occupied)(along_x, along_y, along_z)
        convolved = (convolve_window(windows, kernel) * occupied_centre[:, :, None].astype(jnp.float32)).astype(jnp.bfloat16)
        centre = windows[:, 1:-1, 1:-1, 1:-1, :].reshape(-1, E * E * E, C)
        return (convolved, centre, occupied_centre)
    convolved, centre, occupied_centre = lax.map(per_block, inverse)
    convolved = convolved.reshape(N_GX * O, N_GY, E * E * E, C)
    centre = centre.reshape(N_GX * O, N_GY, E * E * E, C)
    occupied_centre = occupied_centre.reshape(N_GX * O, N_GY, E * E * E)
    widened = convolved.astype(jnp.float32)
    summed = lax.optimization_barrier(jnp.sum(widened, axis=(0, 1, 2)))
    squared = lax.optimization_barrier(jnp.sum(widened * widened, axis=(0, 1, 2)))
    voxels_on = jnp.sum(occupied_centre.astype(jnp.float32))
    return finish(convolved, centre, occupied_centre, summed, squared, voxels_on, norm_gain, norm_bias)
```

```python
import functools

import jax
import jax.numpy as jnp
from jax import lax
from jax.experimental import pallas as pl
from jax.experimental.pallas import tpu as pltpu
from jax.sharding import PartitionSpec as P

O = 16
E = 8
C = 128
GROUP = 4
ABSENT = -1e30
EPSILON = 1e-05
MIB = 1 << 20


def conv_kernel(
    place_ref,
    count_ref,
    masked_ref,
    x_low_ref,
    x_high_ref,
    y_low_ref,
    y_high_ref,
    corner_ref,
    occupied_ref,
    weight_ref,
    conv_ref,
    centre_ref,
    sums_ref,
    padded,
    shifted,
    total,
    sems,
):
    step = pl.program_id(0)

    @pl.when(step == 0)
    def _():
        copies = [
            pltpu.make_async_copy(
                masked_ref, padded.at[1:17, 1:17, 8:136, :], sems.at[0]
            ),
            pltpu.make_async_copy(x_low_ref, padded.at[0:1, 1:17, 8:136, :], sems.at[1]),
            pltpu.make_async_copy(x_high_ref, padded.at[17:18, 1:17, 8:136, :], sems.at[2]),
            pltpu.make_async_copy(y_low_ref, padded.at[1:17, 0:1, 8:136, :], sems.at[3]),
            pltpu.make_async_copy(y_high_ref, padded.at[1:17, 17:18, 8:136, :], sems.at[4]),
        ]
        for i in range(4):
            copies.append(
                pltpu.make_async_copy(
                    corner_ref.at[i],
                    padded.at[17 * (i // 2), 17 * (i % 2), 8:136, :],
                    sems.at[5 + i],
                )
            )
        for copy in copies:
            copy.start()
        padded[:, :, 0:8, :] = jnp.zeros((18, 18, 8, C), jnp.float32)
        padded[:, :, 136:144, :] = jnp.zeros((18, 18, 8, C), jnp.float32)
        sums_ref[...] = jnp.zeros_like(sums_ref)
        for copy in copies:
            copy.wait()

    @pl.when(step * GROUP < count_ref[0])
    def _():
        row = lax.broadcasted_iota(jnp.int32, (E, C), 0)
        lane = lax.broadcasted_iota(jnp.int32, (E, C), 1)

        def place_of(b):
            place = place_ref[step * GROUP + b]
            return place // 32, place // 16 % 2, place % 16

        def prepare(b, carry):
            bx, by, bz = place_of(b)
            for dz in range(3):
                for xx in range(10):
                    lines = [
                        padded[bx * E + xx, by * E + yy, pl.ds(bz * E + 7 + dz, E), :]
                        for yy in range(10)
                    ]
                    for parity in range(2):
                        for yp in range(5 - parity):
                            pair = jnp.concatenate(
                                [lines[2 * yp + parity], lines[2 * yp + parity + 1]], axis=0
                            )
                            shifted[parity, dz, xx % 2, b, xx // 2, yp] = pair.astype(jnp.bfloat16)
            return carry

        lax.fori_loop(0, GROUP, prepare, 0)

        for dy in range(3):
            parity, first = dy % 2, dy // 2
            parts = []
            for dz in range(3):
                for j in range(4):
                    part = shifted[
                        parity, dz, j % 2, :, j // 2 : j // 2 + 4, first : first + 4, :, :
                    ]
                    parts.append(part.reshape(GROUP * 256, C))
            product = jnp.dot(
                jnp.concatenate(parts, axis=1),
                weight_ref[dy],
                preferred_element_type=jnp.float32,
            )
            if dy == 0:
                total[...] = product
            else:
                total[...] += product

        ones = jnp.ones((C, C), jnp.bfloat16)

        def finish(b, carry):
            bx, by, bz = place_of(b)
            valid = jnp.where(step * GROUP + b < count_ref[0], 1.0, 0.0)
            eye = jnp.where(lane == bz * E + row, valid, 0.0)
            summed = jnp.zeros((E, C), jnp.float32)
            squared = jnp.zeros((E, C), jnp.float32)
            counted = jnp.zeros((E, C), jnp.float32)
            for x in range(E):
                lines = occupied_ref[pl.ds((bx * E + x) * 16 + by * E, E), :]
                spread = (lines[:, None, :] * eye[None, :, :]).reshape(E * E, C)
                live = jnp.dot(
                    spread.astype(jnp.bfloat16), ones, preferred_element_type=jnp.float32
                )
                block = total[pl.ds(b * 256 + (x // 2) * 64, 64), (x % 2) * C : (x % 2 + 1) * C]
                value = (block * live).astype(jnp.bfloat16)
                wide = value.astype(jnp.float32)
                summed += jnp.sum(wide.reshape(E, E, C), axis=0)
                squared += jnp.sum((wide * wide).reshape(E, E, C), axis=0)
                counted += jnp.sum(live.reshape(E, E, C), axis=0)
                conv_ref[b, x * 64 : (x + 1) * 64, :] = jnp.where(
                    live > 0.5, wide, ABSENT
                ).astype(jnp.bfloat16)
                centre_ref[b, x * 64 : (x + 1) * 64, :] = shifted[
                    1, 1, (x + 1) % 2, b, (x + 1) // 2, 0:4
                ].reshape(64, C)
            sums_ref[0] += summed
            sums_ref[1] += squared
            sums_ref[2] += counted
            return carry

        lax.fori_loop(0, GROUP, finish, 0)


def convolve(places, count, masked, halos, occupied, weight):
    any_spec = pl.BlockSpec(memory_space=pl.ANY)
    whole = pl.BlockSpec(memory_space=pltpu.VMEM)
    return pl.pallas_call(
        conv_kernel,
        grid_spec=pltpu.PrefetchScalarGridSpec(
            num_scalar_prefetch=2,
            grid=(32 // GROUP,),
            in_specs=[any_spec] * 6 + [whole, whole],
            out_specs=[
                pl.BlockSpec((GROUP, 512, C), lambda i, *_: (i, 0, 0)),
                pl.BlockSpec((GROUP, 512, C), lambda i, *_: (i, 0, 0)),
                pl.BlockSpec((3, E, C), lambda i, *_: (0, 0, 0)),
            ],
            scratch_shapes=[
                pltpu.VMEM((18, 18, 144, C), jnp.float32),
                pltpu.VMEM((2, 3, 2, GROUP, 5, 5, 16, C), jnp.bfloat16),
                pltpu.VMEM((GROUP * 256, 2 * C), jnp.float32),
                pltpu.SemaphoreType.DMA((9,)),
            ],
        ),
        out_shape=[
            jax.ShapeDtypeStruct((32, 512, C), jnp.bfloat16),
            jax.ShapeDtypeStruct((32, 512, C), jnp.bfloat16),
            jax.ShapeDtypeStruct((3, E, C), jnp.float32),
        ],
        compiler_params=pltpu.CompilerParams(vmem_limit_bytes=56 * MIB),
        cost_estimate=pl.CostEstimate(
            flops=2 * 32 * 256 * 4608 * 256, bytes_accessed=30 * MIB, transcendentals=0
        ),
    )(places, count, masked, *halos, occupied, weight)


def finish_kernel(index_ref, valid_ref, conv_ref, centre_ref, norm_ref, out_ref):
    @pl.when(valid_ref[pl.program_id(0)] > 0)
    def _():
        mean, factor, bias = norm_ref[0:1, :], norm_ref[1:2, :], norm_ref[2:3, :]
        for i in range(0, 512, 64):
            conv = conv_ref[0, i : i + 64, :].astype(jnp.float32)
            scaled = factor * (conv - mean) + bias
            silu = scaled * (0.5 + 0.5 * jnp.tanh(0.5 * scaled))
            silu = jnp.where(conv > 0.5 * ABSENT, silu, 0.0)
            centre = centre_ref[0, i : i + 64, :].astype(jnp.float32)
            out_ref[0, i : i + 64, :] = (centre + silu).astype(jnp.bfloat16)


def finish(index, valid, conv, centre, norm):
    return pl.pallas_call(
        finish_kernel,
        grid_spec=pltpu.PrefetchScalarGridSpec(
            num_scalar_prefetch=2,
            grid=(32,),
            in_specs=[
                pl.BlockSpec((1, 512, C), lambda i, index, valid: (index[i], 0, 0)),
                pl.BlockSpec((1, 512, C), lambda i, index, valid: (index[i], 0, 0)),
                pl.BlockSpec((8, C), lambda i, index, valid: (0, 0)),
            ],
            out_specs=pl.BlockSpec((1, 512, C), lambda i, index, valid: (i, 0, 0)),
        ),
        out_shape=jax.ShapeDtypeStruct((32, 512, C), jnp.bfloat16),
    )(index, valid, conv, centre, norm)


def pick_kernel(index_ref, in_ref, out_ref):
    out_ref[...] = in_ref[...]


def pick(index, received):
    return pl.pallas_call(
        pick_kernel,
        grid_spec=pltpu.PrefetchScalarGridSpec(
            num_scalar_prefetch=1,
            grid=(O,),
            in_specs=[pl.BlockSpec((1, 512, C), lambda i, index: (index[i], 0, 0))],
            out_specs=pl.BlockSpec((1, 512, C), lambda i, index: (i, 0, 0)),
        ),
        out_shape=jax.ShapeDtypeStruct((O, 512, C), jnp.bfloat16),
    )(index, received)


def summed_over(values, axis):
    count = lax.axis_size(axis)
    spread = jnp.broadcast_to(values[None], (count,) + values.shape)
    return jnp.sum(lax.all_to_all(spread, axis, 0, 0, tiled=True), axis=0)


def exchange_faces(features, occupied):
    def face(x, y):
        return features[x, y] * occupied[x, y][..., None]

    gx, gy = lax.axis_size("gx"), lax.axis_size("gy")

    def send(block, dx, dy):
        pairs = [
            (i * gy + j, (i + dx) * gy + j + dy)
            for i in range(gx)
            for j in range(gy)
            if 0 <= i + dx < gx and 0 <= j + dy < gy
        ]
        return lax.ppermute(block, ("gx", "gy"), pairs)

    every, first, last = slice(None), slice(0, 1), slice(15, 16)
    x_low = send(face(last, every), 1, 0)
    x_high = send(face(first, every), -1, 0)
    y_low = send(face(every, last), 0, 1)
    y_high = send(face(every, first), 0, -1)
    corners = jnp.concatenate(
        [
            send(face(last, last), 1, 1),
            send(face(last, first), 1, -1),
            send(face(first, last), -1, 1),
            send(face(first, first), -1, -1),
        ]
    ).reshape(4, 128, C)
    return tuple(h.astype(jnp.float32) for h in (x_low, x_high, y_low, y_high, corners))


def routes(owner_map):
    flat = owner_map.reshape(-1)
    index = jnp.arange(flat.shape[0], dtype=jnp.int32)
    active = flat >= 0
    owner = jnp.where(active, flat // O, -1)
    earlier = (index[None, :] < index[:, None]) & active[None, :]
    rank = jnp.sum(earlier.astype(jnp.int32), axis=1)
    pair_rank = jnp.sum((earlier & (owner[None, :] == owner[:, None])).astype(jnp.int32), axis=1)
    slot = jnp.where(active, owner * 2 + pair_rank, -1)
    slots = jnp.arange(32, dtype=jnp.int32)
    here = slot[None, :] == slots[:, None]
    compact = jnp.sum(jnp.where(here, rank[None, :], 0), axis=1)
    valid = jnp.sum(here.astype(jnp.int32), axis=1)
    sent = jnp.sum(jnp.where(here, (flat % O)[None, :] + 1, 0), axis=1) - 1
    ordered = active[None, :] & (rank[None, :] == slots[:, None])
    places = jnp.sum(jnp.where(ordered, index[None, :], 0), axis=1)
    count = jnp.sum(active.astype(jnp.int32)).reshape(1)
    return places, count, compact, valid, sent


def on_device(features, occupancy, owner_map, kernel, norm_gain, norm_bias):
    active = (owner_map >= 0).astype(jnp.int32)
    occupied_grid = (
        occupancy.reshape(2, E, 2, E, 16, E) * active[:, None, :, None, :, None]
    ).reshape(occupancy.shape)
    occupied = occupied_grid.astype(jnp.bfloat16)
    halos = exchange_faces(features, occupied)
    masked = features.astype(jnp.float32) * occupied_grid.astype(jnp.float32)[..., None]
    places, count, compact, valid, sent = routes(owner_map)
    received_slots = lax.all_to_all(
        sent.reshape(16, 1, 2), "gx", split_axis=0, concat_axis=0, tiled=True
    ).reshape(32)
    taps = kernel.reshape(3, 3, 3, C, C)
    blank = jnp.zeros((1, 3, 3, C, C), kernel.dtype)
    weight = jnp.concatenate(
        [jnp.concatenate([taps, blank]), jnp.concatenate([blank, taps])], axis=4
    )
    weight = weight.transpose(1, 2, 0, 3, 4).reshape(3, 12 * C, 2 * C)
    conv, centre, sums = convolve(
        places, count, masked, halos, occupied_grid.astype(jnp.float32).reshape(256, 128), weight
    )
    sums = jnp.sum(sums, axis=1)
    sums = summed_over(summed_over(jnp.pad(sums, ((0, 5), (0, 0))), "gx"), "gy")
    mean = sums[0] / sums[2]
    variance = sums[1] / sums[2] - mean * mean
    factor = norm_gain / jnp.sqrt(variance + EPSILON)
    norm = jnp.pad(jnp.stack([mean, factor, norm_bias]), ((0, 5), (0, 0)))
    result = finish(compact, valid, conv, centre, norm)
    received = lax.all_to_all(
        result.reshape(16, 2, 512, C), "gx", split_axis=0, concat_axis=0, tiled=True
    ).reshape(32, 512, C)
    slots = jnp.arange(O, dtype=jnp.int32)
    source = jnp.sum(
        jnp.where(
            received_slots[None, :] == slots[:, None], jnp.arange(32, dtype=jnp.int32)[None, :], 0
        ),
        axis=1,
    )
    return pick(source, received).reshape(O, 1, 512, C)


def solution(mesh):
    in_specs = (P("gx", "gy", None, None), P("gx", "gy", None), P("gx", "gy", None), P(), P(), P())
    out_specs = P("gx", "gy", None, None)
    return jax.shard_map(
        on_device, mesh=mesh, in_specs=in_specs, out_specs=out_specs, check_vma=False
    )
```

```python
import functools

import jax
import jax.numpy as jnp
from jax import lax
from jax.experimental import pallas as pl
from jax.experimental.pallas import tpu as pltpu
from jax.sharding import PartitionSpec as P

O = 16
E = 8
C = 128
GROUP = 4
ABSENT = -1e30
EPSILON = 1e-05
MIB = 1 << 20


def shifted_scratch():
    return pltpu.VMEM((2, 3, 2, GROUP, 5, 5, 16, C), jnp.bfloat16)


def conv_kernel(
    place_ref,
    count_ref,
    masked_ref,
    y_low_ref,
    y_high_ref,
    occupied_ref,
    weight_ref,
    conv_ref,
    centre_ref,
    face_ref,
    sums_ref,
    padded,
    shifted_a,
    shifted_b,
    total_a,
    total_b,
    sems,
):
    step = pl.program_id(0)
    count, early, steps = count_ref[0], count_ref[1], count_ref[2]
    halves = [
        pltpu.make_async_copy(
            masked_ref.at[lo:hi], padded.at[1 + lo : 1 + hi, 1:17, 8:136, :], sems.at[i]
        )
        for i, (lo, hi) in enumerate(((0, 9), (9, 16)))
    ]
    row = lax.broadcasted_iota(jnp.int32, (E, C), 0)
    lane = lax.broadcasted_iota(jnp.int32, (E, C), 1)

    def place_of(k):
        place = place_ref[k]
        return place // 32, place // 16 % 2, place % 16

    def prepare(group, shifted):
        for b in range(GROUP):
            bx, by, bz = place_of(group * GROUP + b)
            for dz in range(3):
                for xx in range(10):
                    lines = [
                        padded[bx * E + xx, by * E + yy, pl.ds(bz * E + 7 + dz, E), :]
                        for yy in range(10)
                    ]
                    for parity in range(2):
                        for yp in range(5 - parity):
                            pair = jnp.concatenate(
                                [lines[2 * yp + parity], lines[2 * yp + parity + 1]], axis=0
                            )
                            shifted[parity, dz, xx % 2, b, xx // 2, yp] = pair.astype(jnp.bfloat16)

    def multiply(shifted, total):
        for dy in range(3):
            parity, first = dy % 2, dy // 2
            parts = []
            for dz in range(3):
                for j in range(4):
                    part = shifted[
                        parity, dz, j % 2, :, j // 2 : j // 2 + 4, first : first + 4, :, :
                    ]
                    parts.append(part.reshape(GROUP * 256, C))
            product = jnp.dot(
                jnp.concatenate(parts, axis=1),
                weight_ref[dy],
                preferred_element_type=jnp.float32,
            )
            if dy == 0:
                total[...] = product
            else:
                total[...] += product

    def emit(group, shifted, total, at):
        ones = jnp.ones((C, C), jnp.bfloat16)
        summed = jnp.zeros((E, C), jnp.float32)
        squared = jnp.zeros((E, C), jnp.float32)
        counted = jnp.zeros((E, C), jnp.float32)
        for b in range(GROUP):
            k = group * GROUP + b
            bx, by, bz = place_of(k)
            valid = jnp.where(k < count, 1.0, 0.0)
            eye = jnp.where(lane == bz * E + row, valid, 0.0)
            for x in range(E):
                lines = occupied_ref[pl.ds((bx * E + x) * 16 + by * E, E), :]
                spread = (lines[:, None, :] * eye[None, :, :]).reshape(E * E, C)
                live = jnp.dot(
                    spread.astype(jnp.bfloat16), ones, preferred_element_type=jnp.float32
                )
                block = total[b * 256 + (x // 2) * 64 : b * 256 + (x // 2) * 64 + 64,
                              (x % 2) * C : (x % 2 + 1) * C]
                value = (block * live).astype(jnp.bfloat16)
                wide = value.astype(jnp.float32)
                kept = wide
                if x == 0:
                    kept = wide * jnp.where(bx == 0, 0.0, 1.0)
                    face_low = block
                if x == E - 1:
                    kept = wide * jnp.where(bx == 0, 1.0, 0.0)
                    face_ref[at + b] = jnp.where(bx == 0, face_low, block)
                summed += jnp.sum(kept.reshape(E, E, C), axis=0)
                squared += jnp.sum((kept * kept).reshape(E, E, C), axis=0)
                counted += jnp.sum(live.reshape(E, E, C), axis=0)
                conv_ref[at + b, x * 64 : (x + 1) * 64, :] = jnp.where(
                    live > 0.5, wide, ABSENT
                ).astype(jnp.bfloat16)
                centre_ref[at + b, x * 64 : (x + 1) * 64, :] = shifted[
                    1, 1, (x + 1) % 2, b, (x + 1) // 2, 0:4
                ].reshape(64, C)
        sums_ref[0] += summed
        sums_ref[1] += squared
        sums_ref[2] += counted

    @pl.when(step == 0)
    def _():
        for half in halves:
            half.start()
        edge = jnp.zeros((18, 18, E, C), jnp.float32)
        padded[:, :, 0:8, :] = edge
        padded[:, :, 136:144, :] = edge
        side = jnp.zeros((18, 128, C), jnp.float32)
        padded[0, :, 8:136, :] = side
        padded[17, :, 8:136, :] = side
        padded[1:17, 0, 8:136, :] = y_low_ref[...].reshape(16, 128, C).astype(jnp.float32)
        padded[1:17, 17, 8:136, :] = y_high_ref[...].reshape(16, 128, C).astype(jnp.float32)
        sums_ref[...] = jnp.zeros_like(sums_ref)
        halves[0].wait()

    @pl.when(((step == 0) & (early < 3 * GROUP)) | ((step == 1) & (early >= 3 * GROUP)))
    def _():
        halves[1].wait()

    @pl.when((step == 0) & (steps > 0))
    def _():
        prepare(0, shifted_a)

    @pl.when((step > 0) & (step <= steps))
    def _():
        emit(2 * step - 1, shifted_b, total_b, 0)

    @pl.when(step < steps)
    def _():
        prepare(2 * step + 1, shifted_b)
        multiply(shifted_a, total_a)
        multiply(shifted_b, total_b)
        emit(2 * step, shifted_a, total_a, GROUP)
        prepare(2 * step + 2, shifted_a)


def convolve(places, count, masked, y_low, y_high, occupied, weight):
    any_spec = pl.BlockSpec(memory_space=pl.ANY)
    whole = pl.BlockSpec(memory_space=pltpu.VMEM)

    def block(i, places, count):
        return (jnp.minimum(i, count[2]), 0, 0)

    rows = 2 * GROUP * (16 // GROUP + 1)
    return pl.pallas_call(
        conv_kernel,
        grid_spec=pltpu.PrefetchScalarGridSpec(
            num_scalar_prefetch=2,
            grid=(16 // GROUP + 1,),
            in_specs=[any_spec, whole, whole, whole, whole],
            out_specs=[
                pl.BlockSpec((2 * GROUP, 512, C), block),
                pl.BlockSpec((2 * GROUP, 512, C), block),
                pl.BlockSpec((2 * GROUP, 64, C), block),
                pl.BlockSpec((3, E, C), lambda i, *_: (0, 0, 0)),
            ],
            scratch_shapes=[
                pltpu.VMEM((18, 18, 144, C), jnp.float32),
                shifted_scratch(),
                shifted_scratch(),
                pltpu.VMEM((GROUP * 256, 2 * C), jnp.float32),
                pltpu.VMEM((GROUP * 256, 2 * C), jnp.float32),
                pltpu.SemaphoreType.DMA((2,)),
            ],
        ),
        out_shape=[
            jax.ShapeDtypeStruct((rows, 512, C), jnp.bfloat16),
            jax.ShapeDtypeStruct((rows, 512, C), jnp.bfloat16),
            jax.ShapeDtypeStruct((rows, 64, C), jnp.float32),
            jax.ShapeDtypeStruct((3, E, C), jnp.float32),
        ],
        compiler_params=pltpu.CompilerParams(vmem_limit_bytes=56 * MIB),
        cost_estimate=pl.CostEstimate(
            flops=2 * 32 * 256 * 4608 * 256, bytes_accessed=30 * MIB, transcendentals=0
        ),
    )(places, count, masked, y_low, y_high, occupied, weight)


def face_kernel(
    place_ref,
    count_ref,
    x_low_ref,
    x_high_ref,
    partial_ref,
    sums_ref,
    occupied_ref,
    weight_ref,
    out_ref,
    norm_ref,
    padded,
    shifted,
    added,
):
    count = count_ref[0]
    row = lax.broadcasted_iota(jnp.int32, (E, C), 0)
    lane = lax.broadcasted_iota(jnp.int32, (E, C), 1)
    ones = jnp.ones((C, C), jnp.bfloat16)
    padded[:, 0:8, :] = jnp.zeros((18, E, C), jnp.float32)
    padded[:, 136:144, :] = jnp.zeros((18, E, C), jnp.float32)
    for side, ref in enumerate((x_low_ref, x_high_ref)):
        padded[:, 8:136, :] = ref[0].astype(jnp.float32)
        for dz in range(3):
            shifted[dz] = padded[:, 7 + dz : 135 + dz, :].astype(jnp.bfloat16).reshape(
                9, 2, 128, C
            )
        parts = []
        for dz in range(3):
            for j in range(4):
                parts.append(shifted[dz, j // 2 : j // 2 + 8, j % 2].reshape(1024, C))
        added[side] = jnp.dot(
            jnp.concatenate(parts, axis=1), weight_ref[side], preferred_element_type=jnp.float32
        )

    def one(k, carry):
        summed, squared = carry
        place = place_ref[k]
        bx, by, bz = place // 32, place // 16 % 2, place % 16
        eye = jnp.where(lane == bz * E + row, 1.0, 0.0)
        lines = occupied_ref[pl.ds(bx * 240 + by * E, E), :]
        spread = (lines[:, None, :] * eye[None, :, :]).reshape(E * E, C)
        live = jnp.dot(spread.astype(jnp.bfloat16), ones, preferred_element_type=jnp.float32)
        pieces = []
        for y in range(E):
            start = pl.multiple_of((by * 4 + y // 2) * 128 + bz * E, E)
            pieces.append(added[bx, pl.ds(start, E), (y % 2) * C : (y % 2 + 1) * C])
        block = partial_ref[k + GROUP] + jnp.concatenate(pieces, axis=0)
        wide = (block * live).astype(jnp.bfloat16).astype(jnp.float32)
        out_ref[k] = jnp.where(live > 0.5, wide, ABSENT).astype(jnp.bfloat16)
        summed += jnp.sum(wide.reshape(E, E, C), axis=0)
        squared += jnp.sum((wide * wide).reshape(E, E, C), axis=0)
        return summed, squared

    summed, squared = lax.fori_loop(0, count, one, (sums_ref[0], sums_ref[1]))
    table = jnp.concatenate(
        [
            jnp.sum(summed, axis=0, keepdims=True),
            jnp.sum(squared, axis=0, keepdims=True),
            jnp.sum(sums_ref[2], axis=0, keepdims=True),
            jnp.zeros((5, C), jnp.float32),
        ],
        axis=0,
    )
    norm_ref[...] = jnp.broadcast_to(table[None], norm_ref.shape)


def correct_faces(places, count, x_low, x_high, partial, sums, occupied, weight):
    whole = pl.BlockSpec(memory_space=pltpu.VMEM)
    scalars = pl.BlockSpec(memory_space=pltpu.SMEM)
    return pl.pallas_call(
        face_kernel,
        in_specs=[scalars, scalars] + [whole] * 6,
        out_specs=[whole, whole],
        out_shape=[
            jax.ShapeDtypeStruct((32, 64, C), jnp.bfloat16),
            jax.ShapeDtypeStruct((16, E, C), jnp.float32),
        ],
        scratch_shapes=[
            pltpu.VMEM((18, 144, C), jnp.float32),
            pltpu.VMEM((3, 9, 2, 128, C), jnp.bfloat16),
            pltpu.VMEM((2, 1024, 2 * C), jnp.float32),
        ],
        compiler_params=pltpu.CompilerParams(vmem_limit_bytes=32 * MIB),
    )(places, count, x_low, x_high, partial, sums, occupied, weight)


def finish_kernel(
    slot_ref,
    place_ref,
    count_ref,
    conv_ref,
    centre_ref,
    face_ref,
    sums_ref,
    gain_ref,
    bias_ref,
    out_ref,
    buffer,
    sems,
):
    step = pl.program_id(0)
    count = count_ref[0]

    def copy(k, half, b):
        return pltpu.make_async_copy(
            buffer.at[half, b], out_ref.at[slot_ref[k]], sems.at[half, b]
        )

    def drain(at):
        for b in range(GROUP):
            k = at * GROUP + b

            @pl.when((at >= 0) & (k < count))
            def _():
                copy(k, at % 2, b).wait()

    drain(step - 2)

    @pl.when(step * GROUP < count)
    def _():
        sums = jnp.sum(sums_ref[...], axis=0)
        mean = sums[0:1] / sums[2:3]
        variance = sums[1:2] / sums[2:3] - mean * mean
        factor = gain_ref[...] / jnp.sqrt(variance + EPSILON)
        bias = bias_ref[...]
        for b in range(GROUP):
            k = step * GROUP + b

            @pl.when(k < count)
            def _():
                bx = place_ref[k] // 32
                for x in range(E):
                    conv = conv_ref[b, x * 64 : (x + 1) * 64, :].astype(jnp.float32)
                    if x in (0, E - 1):
                        own = face_ref[b].astype(jnp.float32)
                        conv = jnp.where(bx == (0 if x == 0 else 1), own, conv)
                    scaled = factor * (conv - mean) + bias
                    silu = scaled * (0.5 + 0.5 * jnp.tanh(0.5 * scaled))
                    silu = jnp.where(conv > 0.5 * ABSENT, silu, 0.0)
                    centre = centre_ref[b, x * 64 : (x + 1) * 64, :].astype(jnp.float32)
                    buffer[step % 2, b, x * 64 : (x + 1) * 64, :] = (centre + silu).astype(
                        jnp.bfloat16
                    )
                copy(k, step % 2, b).start()

    @pl.when(step == pl.num_programs(0) - 1)
    def _():
        drain(step - 1)
        drain(step)


def finish(slots, places, count, conv, centre, face, sums, gain, bias):
    whole = pl.BlockSpec(memory_space=pltpu.VMEM)

    def last(i, count):
        return jnp.minimum(i, jnp.maximum((count[0] - 1) // GROUP, 0))

    def shifted_block(i, slots, places, count):
        return (last(i, count) + 1, 0, 0)

    def block(i, slots, places, count):
        return (last(i, count), 0, 0)

    return pl.pallas_call(
        finish_kernel,
        grid_spec=pltpu.PrefetchScalarGridSpec(
            num_scalar_prefetch=3,
            grid=(32 // GROUP,),
            in_specs=[
                pl.BlockSpec((GROUP, 512, C), shifted_block),
                pl.BlockSpec((GROUP, 512, C), shifted_block),
                pl.BlockSpec((GROUP, 64, C), block),
                whole,
                whole,
                whole,
            ],
            out_specs=pl.BlockSpec(memory_space=pl.ANY),
            scratch_shapes=[
                pltpu.VMEM((2, GROUP, 512, C), jnp.bfloat16),
                pltpu.SemaphoreType.DMA((2, GROUP)),
            ],
        ),
        out_shape=jax.ShapeDtypeStruct((32, 512, C), jnp.bfloat16),
        compiler_params=pltpu.CompilerParams(vmem_limit_bytes=24 * MIB),
    )(slots, places, count, conv, centre, face, sums, gain, bias)


def pick_kernel(index_ref, in_ref, out_ref, buffer, sems):
    reads = [
        pltpu.make_async_copy(in_ref.at[index_ref[i]], buffer.at[i], sems.at[0, i])
        for i in range(O)
    ]
    writes = [
        pltpu.make_async_copy(buffer.at[i], out_ref.at[i], sems.at[1, i]) for i in range(O)
    ]
    for read in reads:
        read.start()
    for read, write in zip(reads, writes):
        read.wait()
        write.start()
    for write in writes:
        write.wait()


def pick(index, received):
    return pl.pallas_call(
        pick_kernel,
        in_specs=[pl.BlockSpec(memory_space=pltpu.SMEM), pl.BlockSpec(memory_space=pl.ANY)],
        out_specs=pl.BlockSpec(memory_space=pl.ANY),
        scratch_shapes=[
            pltpu.VMEM((O, 512, C), jnp.bfloat16),
            pltpu.SemaphoreType.DMA((2, O)),
        ],
        out_shape=jax.ShapeDtypeStruct((O, 512, C), jnp.bfloat16),
    )(index, received)


def swap(spread, axis):
    return lax.all_to_all(spread, axis, 0, 0, tiled=True)


def neighbours(low_block, high_block, axis):
    count = lax.axis_size(axis)
    up = [(i, i + 1) for i in range(count - 1)]
    down = [(j, i) for i, j in up]
    return lax.ppermute(high_block, axis, up), lax.ppermute(low_block, axis, down)


def routes(owner_map):
    flat = owner_map.reshape(-1)
    index = jnp.arange(flat.shape[0], dtype=jnp.int32)
    active = flat >= 0
    owner = jnp.where(active, flat // O, -1)
    earlier = (index[None, :] < index[:, None]) & active[None, :]
    rank = jnp.sum(earlier.astype(jnp.int32), axis=1)
    pair_rank = jnp.sum((earlier & (owner[None, :] == owner[:, None])).astype(jnp.int32), axis=1)
    slot = jnp.where(active, owner * 2 + pair_rank, -1)
    slots = jnp.arange(32, dtype=jnp.int32)
    here = slot[None, :] == slots[:, None]
    sent = jnp.sum(jnp.where(here, (flat % O)[None, :] + 1, 0), axis=1) - 1
    order = jnp.arange(48, dtype=jnp.int32)
    ordered = active[None, :] & (rank[None, :] == order[:, None])
    places = jnp.sum(jnp.where(ordered, index[None, :], 0), axis=1)
    slot_of = jnp.sum(jnp.where(ordered, slot[None, :], 0), axis=1)
    count = jnp.sum(active.astype(jnp.int32))
    early = jnp.sum(active[:32].astype(jnp.int32))
    counts = jnp.stack([count, early, (count + 2 * GROUP - 1) // (2 * GROUP)])
    return places, slot_of, counts, sent


def pair_weights(taps):
    blank = jnp.zeros((1,) + taps.shape[1:], taps.dtype)
    return jnp.concatenate(
        [jnp.concatenate([taps, blank]), jnp.concatenate([blank, taps])], axis=-1
    )


def on_device(features, occupancy, owner_map, kernel, norm_gain, norm_bias):
    active = (owner_map >= 0).astype(jnp.int32)
    occupied_grid = (
        occupancy.reshape(2, E, 2, E, 16, E) * active[:, None, :, None, :, None]
    ).reshape(occupancy.shape)
    occupied = occupied_grid.astype(jnp.bfloat16)

    def face(x, y):
        return features[x, y] * occupied[x, y][..., None]

    every, first, last = slice(None), slice(0, 1), slice(15, 16)
    y_low, y_high = neighbours(face(every, first), face(every, last), "gy")
    masked = features.astype(jnp.float32) * occupied_grid.astype(jnp.float32)[..., None]
    places, slot_of, counts, sent = routes(owner_map)
    received_slots = lax.all_to_all(
        sent.reshape(16, 1, 2), "gx", split_axis=0, concat_axis=0, tiled=True
    ).reshape(32)
    owned = jnp.arange(O, dtype=jnp.int32)
    source = jnp.sum(
        jnp.where(
            received_slots[None, :] == owned[:, None], jnp.arange(32, dtype=jnp.int32)[None, :], 0
        ),
        axis=1,
    )
    taps = kernel.reshape(3, 3, 3, C, C)
    weight = pair_weights(taps).transpose(1, 2, 0, 3, 4).reshape(3, 12 * C, 2 * C)
    face_weight = jnp.stack(
        [pair_weights(taps[a]).transpose(1, 0, 2, 3).reshape(12 * C, 2 * C) for a in (0, 2)]
    )
    lines = occupied_grid.astype(jnp.float32).reshape(256, 128)
    x_low, x_high = neighbours(
        jnp.concatenate([y_low[0:1], face(first, every), y_high[0:1]], axis=1),
        jnp.concatenate([y_low[15:16], face(last, every), y_high[15:16]], axis=1),
        "gx",
    )
    places, source = lax.optimization_barrier((places, source))
    conv, centre, partial, sums = convolve(places, counts, masked, y_low, y_high, lines, weight)
    face_conv, spread = correct_faces(
        places, counts, x_low, x_high, partial, sums, lines, face_weight
    )
    partly = jnp.sum(swap(spread, "gx"), axis=0)
    totals = swap(jnp.broadcast_to(partly[None], (8, E, C)), "gy")
    result = finish(
        slot_of,
        places,
        counts,
        conv,
        centre,
        face_conv,
        totals,
        norm_gain.reshape(1, C),
        norm_bias.reshape(1, C),
    )
    received = swap(result.reshape(16, 2, 512, C), "gx").reshape(32, 512, C)
    return pick(source, received).reshape(O, 1, 512, C)


def solution(mesh):
    in_specs = (P("gx", "gy", None, None), P("gx", "gy", None), P("gx", "gy", None), P(), P(), P())
    out_specs = P("gx", "gy", None, None)
    return jax.shard_map(
        on_device, mesh=mesh, in_specs=in_specs, out_specs=out_specs, check_vma=False
    )
```

```python
import functools

import jax
import jax.numpy as jnp
from jax import lax
from jax.experimental import pallas as pl
from jax.experimental.pallas import tpu as pltpu
from jax.sharding import PartitionSpec as P

O = 16
E = 8
C = 128
GROUP = 4
ABSENT = -1e30
EPSILON = 1e-05
MIB = 1 << 20


def pair_taps(weight_ref, taps_ref, index):
    blank = jnp.zeros((C, C), jnp.bfloat16)
    for a in range(weight_ref.shape[0]):
        for dz in range(3):
            for j in range(4):
                at = (dz * 4 + j) * C
                weight_ref[a, at : at + C, 0:C] = (
                    taps_ref[index(a, dz, j)] if j < 3 else blank
                )
                weight_ref[a, at : at + C, C : 2 * C] = (
                    taps_ref[index(a, dz, j - 1)] if j > 0 else blank
                )


def shifted_scratch():
    return pltpu.VMEM((2, 3, 2, GROUP, 5, 5, 16, C), jnp.bfloat16)


def conv_kernel(
    place_ref,
    count_ref,
    features_ref,
    y_low_ref,
    y_high_ref,
    taps_hbm,
    occupied_ref,
    conv_ref,
    centre_ref,
    face_ref,
    sums_ref,
    padded,
    raw,
    margins,
    taps_ref,
    weight_ref,
    shifted_a,
    shifted_b,
    total_a,
    total_b,
    sems,
):
    step = pl.program_id(0)
    count, steps = count_ref[0], count_ref[1]
    chunks = [
        pltpu.make_async_copy(
            features_ref.at[4 * i : 4 * i + 4], raw.at[i % 2], sems.at[i]
        )
        for i in range(4)
    ]
    row = lax.broadcasted_iota(jnp.int32, (E, C), 0)
    lane = lax.broadcasted_iota(jnp.int32, (E, C), 1)

    def place_of(k):
        place = place_ref[k]
        return place // 32, place // 16 % 2, place % 16

    def prepare(group, shifted):
        for b in range(GROUP):
            bx, by, bz = place_of(group * GROUP + b)
            for dz in range(3):
                for xx in range(10):
                    lines = [
                        padded[bx * E + xx, by * E + yy, pl.ds(bz * E + 7 + dz, E), :]
                        for yy in range(10)
                    ]
                    for parity in range(2):
                        for yp in range(5 - parity):
                            pair = jnp.concatenate(
                                [lines[2 * yp + parity], lines[2 * yp + parity + 1]], axis=0
                            )
                            shifted[parity, dz, xx % 2, b, xx // 2, yp] = pair.astype(jnp.bfloat16)

    def multiply(shifted, total):
        for dy in range(3):
            parity, first = dy % 2, dy // 2
            parts = []
            for dz in range(3):
                for j in range(4):
                    part = shifted[
                        parity, dz, j % 2, :, j // 2 : j // 2 + 4, first : first + 4, :, :
                    ]
                    parts.append(part.reshape(GROUP * 256, C))
            product = jnp.dot(
                jnp.concatenate(parts, axis=1),
                weight_ref[dy],
                preferred_element_type=jnp.float32,
            )
            if dy == 0:
                total[...] = product
            else:
                total[...] += product

    def emit(group, shifted, total, at):
        ones = jnp.ones((C, C), jnp.bfloat16)
        summed = jnp.zeros((E, C), jnp.float32)
        squared = jnp.zeros((E, C), jnp.float32)
        counted = jnp.zeros((E, C), jnp.float32)
        for b in range(GROUP):
            k = group * GROUP + b
            bx, by, bz = place_of(k)
            valid = jnp.where(k < count, 1.0, 0.0)
            eye = jnp.where(lane == bz * E + row, valid, 0.0)
            for x in range(E):
                lines = occupied_ref[pl.ds((bx * E + x) * 16 + by * E, E), :]
                spread = (lines[:, None, :] * eye[None, :, :]).reshape(E * E, C)
                live = jnp.dot(
                    spread.astype(jnp.bfloat16), ones, preferred_element_type=jnp.float32
                )
                block = total[b * 256 + (x // 2) * 64 : b * 256 + (x // 2) * 64 + 64,
                              (x % 2) * C : (x % 2 + 1) * C]
                value = (block * live).astype(jnp.bfloat16)
                wide = value.astype(jnp.float32)
                kept = wide
                if x == 0:
                    kept = wide * jnp.where(bx == 0, 0.0, 1.0)
                    face_low = block
                if x == E - 1:
                    kept = wide * jnp.where(bx == 0, 1.0, 0.0)
                    face_ref[at + b] = jnp.where(bx == 0, face_low, block)
                summed += jnp.sum(kept.reshape(E, E, C), axis=0)
                squared += jnp.sum((kept * kept).reshape(E, E, C), axis=0)
                counted += jnp.sum(live.reshape(E, E, C), axis=0)
                conv_ref[at + b, x * 64 : (x + 1) * 64, :] = jnp.where(
                    live > 0.5, wide, ABSENT
                ).astype(jnp.bfloat16)
                centre_ref[at + b, x * 64 : (x + 1) * 64, :] = shifted[
                    1, 1, (x + 1) % 2, b, (x + 1) // 2, 0:4
                ].reshape(64, C)
        sums_ref[0] += summed
        sums_ref[1] += squared
        sums_ref[2] += counted

    @pl.when(step == 0)
    def _():
        extra = [
            pltpu.make_async_copy(y_low_ref, margins.at[0], sems.at[4]),
            pltpu.make_async_copy(y_high_ref, margins.at[1], sems.at[5]),
            pltpu.make_async_copy(taps_hbm, taps_ref, sems.at[6]),
        ]
        for copy in [chunks[0], chunks[1]] + extra:
            copy.start()
        edge = jnp.zeros((18, 18, E, C), jnp.float32)
        padded[:, :, 0:8, :] = edge
        padded[:, :, 136:144, :] = edge
        side = jnp.zeros((18, 128, C), jnp.float32)
        padded[0, :, 8:136, :] = side
        padded[17, :, 8:136, :] = side
        sums_ref[...] = jnp.zeros_like(sums_ref)
        for i in range(4):
            chunks[i].wait()
            columns = jnp.transpose(occupied_ref[i // 2 * 128 : i // 2 * 128 + 128, :])

            def mask_plane(j, carry, i=i, columns=columns):
                near = pltpu.roll(columns, 128 - 64 * (i % 2) - 16 * j, axis=1)
                for y in range(16):
                    live = jnp.broadcast_to(near[:, y : y + 1], (128, C))
                    padded[1 + 4 * i + j, 1 + y, 8:136, :] = (
                        raw[i % 2, j, y].astype(jnp.float32) * live
                    )
                return carry

            lax.fori_loop(0, 4, mask_plane, 0)
            if i < 2:
                chunks[i + 2].start()
        for copy in extra:
            copy.wait()
        for side in range(2):
            padded[1:17, 17 * side, 8:136, :] = (
                margins[side].reshape(16, 128, C).astype(jnp.float32)
            )
        pair_taps(weight_ref, taps_ref, lambda dy, dz, dx: 9 * dx + 3 * dy + dz)

    @pl.when((step == 0) & (steps > 0))
    def _():
        prepare(0, shifted_a)

    @pl.when((step > 0) & (step <= steps))
    def _():
        emit(2 * step - 1, shifted_b, total_b, 0)

    @pl.when(step < steps)
    def _():
        prepare(2 * step + 1, shifted_b)
        multiply(shifted_a, total_a)
        multiply(shifted_b, total_b)
        emit(2 * step, shifted_a, total_a, GROUP)
        prepare(2 * step + 2, shifted_a)


def convolve(places, count, features, y_low, y_high, occupied, taps):
    any_spec = pl.BlockSpec(memory_space=pl.ANY)
    whole = pl.BlockSpec(memory_space=pltpu.VMEM)

    def block(i, places, count):
        return (jnp.minimum(i, count[1]), 0, 0)

    rows = 2 * GROUP * (16 // GROUP + 1)
    return pl.pallas_call(
        conv_kernel,
        grid_spec=pltpu.PrefetchScalarGridSpec(
            num_scalar_prefetch=2,
            grid=(16 // GROUP + 1,),
            in_specs=[any_spec, any_spec, any_spec, any_spec, whole],
            out_specs=[
                pl.BlockSpec((2 * GROUP, 512, C), block),
                pl.BlockSpec((2 * GROUP, 512, C), block),
                pl.BlockSpec((2 * GROUP, 64, C), block),
                pl.BlockSpec((3, E, C), lambda i, *_: (0, 0, 0)),
            ],
            scratch_shapes=[
                pltpu.VMEM((18, 18, 144, C), jnp.float32),
                pltpu.VMEM((2, 4, 16, 128, C), jnp.bfloat16),
                pltpu.VMEM((2, 16, 1, 128, C), jnp.bfloat16),
                pltpu.VMEM((27, C, C), jnp.bfloat16),
                pltpu.VMEM((3, 12 * C, 2 * C), jnp.bfloat16),
                shifted_scratch(),
                shifted_scratch(),
                pltpu.VMEM((GROUP * 256, 2 * C), jnp.float32),
                pltpu.VMEM((GROUP * 256, 2 * C), jnp.float32),
                pltpu.SemaphoreType.DMA((7,)),
            ],
        ),
        out_shape=[
            jax.ShapeDtypeStruct((rows, 512, C), jnp.bfloat16),
            jax.ShapeDtypeStruct((rows, 512, C), jnp.bfloat16),
            jax.ShapeDtypeStruct((rows, 64, C), jnp.float32),
            jax.ShapeDtypeStruct((3, E, C), jnp.float32),
        ],
        compiler_params=pltpu.CompilerParams(vmem_limit_bytes=56 * MIB),
        cost_estimate=pl.CostEstimate(
            flops=2 * 32 * 256 * 4608 * 256, bytes_accessed=30 * MIB, transcendentals=0
        ),
    )(places, count, features, y_low, y_high, taps, occupied)


def face_kernel(
    place_ref,
    count_ref,
    x_low_ref,
    x_high_ref,
    partial_ref,
    sums_ref,
    occupied_ref,
    taps_ref,
    slots_ref,
    out_ref,
    norm_ref,
    padded,
    shifted,
    added,
    weight_ref,
):
    count = count_ref[0]
    pair_taps(weight_ref, taps_ref, lambda side, dz, dy: 18 * side + 3 * dy + dz)
    row = lax.broadcasted_iota(jnp.int32, (E, C), 0)
    lane = lax.broadcasted_iota(jnp.int32, (E, C), 1)
    ones = jnp.ones((C, C), jnp.bfloat16)
    padded[:, 0:8, :] = jnp.zeros((18, E, C), jnp.float32)
    padded[:, 136:144, :] = jnp.zeros((18, E, C), jnp.float32)
    for side, ref in enumerate((x_low_ref, x_high_ref)):
        padded[:, 8:136, :] = ref[0].astype(jnp.float32)
        for dz in range(3):
            shifted[dz] = padded[:, 7 + dz : 135 + dz, :].astype(jnp.bfloat16).reshape(
                9, 2, 128, C
            )
        parts = []
        for dz in range(3):
            for j in range(4):
                parts.append(shifted[dz, j // 2 : j // 2 + 8, j % 2].reshape(1024, C))
        added[side] = jnp.dot(
            jnp.concatenate(parts, axis=1), weight_ref[side], preferred_element_type=jnp.float32
        )

    def one(k, carry):
        summed, squared = carry
        place = place_ref[k]
        bx, by, bz = place // 32, place // 16 % 2, place % 16
        eye = jnp.where(lane == bz * E + row, 1.0, 0.0)
        lines = occupied_ref[pl.ds(bx * 240 + by * E, E), :]
        spread = (lines[:, None, :] * eye[None, :, :]).reshape(E * E, C)
        live = jnp.dot(spread.astype(jnp.bfloat16), ones, preferred_element_type=jnp.float32)
        pieces = []
        for y in range(E):
            start = pl.multiple_of((by * 4 + y // 2) * 128 + bz * E, E)
            pieces.append(added[bx, pl.ds(start, E), (y % 2) * C : (y % 2 + 1) * C])
        block = partial_ref[k + GROUP] + jnp.concatenate(pieces, axis=0)
        wide = (block * live).astype(jnp.bfloat16).astype(jnp.float32)
        out_ref[k] = jnp.where(live > 0.5, wide, ABSENT).astype(jnp.bfloat16)
        summed += jnp.sum(wide.reshape(E, E, C), axis=0)
        squared += jnp.sum((wide * wide).reshape(E, E, C), axis=0)
        return summed, squared

    summed, squared = lax.fori_loop(0, count, one, (sums_ref[0], sums_ref[1]))
    table = jnp.concatenate(
        [
            jnp.sum(summed, axis=0, keepdims=True),
            jnp.sum(squared, axis=0, keepdims=True),
            jnp.sum(sums_ref[2], axis=0, keepdims=True),
            jnp.zeros((5, C), jnp.float32),
        ],
        axis=0,
    )
    norm_ref[...] = jnp.broadcast_to(table[None], norm_ref.shape)
    wide_lane = lax.broadcasted_iota(jnp.int32, (1, C), 1)
    for i in range(16):
        pair = jnp.where(wide_lane == 0, slots_ref[2 * i], slots_ref[2 * i + 1])
        norm_ref[i, 3:4, :] = pair.astype(jnp.float32)


def correct_faces(places, count, x_low, x_high, partial, sums, occupied, taps, sent):
    whole = pl.BlockSpec(memory_space=pltpu.VMEM)
    scalars = pl.BlockSpec(memory_space=pltpu.SMEM)
    return pl.pallas_call(
        face_kernel,
        in_specs=[scalars, scalars] + [whole] * 6 + [scalars],
        out_specs=[whole, whole],
        out_shape=[
            jax.ShapeDtypeStruct((32, 64, C), jnp.bfloat16),
            jax.ShapeDtypeStruct((16, E, C), jnp.float32),
        ],
        scratch_shapes=[
            pltpu.VMEM((18, 144, C), jnp.float32),
            pltpu.VMEM((3, 9, 2, 128, C), jnp.bfloat16),
            pltpu.VMEM((2, 1024, 2 * C), jnp.float32),
            pltpu.VMEM((2, 12 * C, 2 * C), jnp.bfloat16),
        ],
        compiler_params=pltpu.CompilerParams(vmem_limit_bytes=32 * MIB),
    )(places, count, x_low, x_high, partial, sums, occupied, taps, sent)


def finish_kernel(
    slot_ref,
    place_ref,
    count_ref,
    conv_ref,
    centre_ref,
    face_ref,
    sums_ref,
    gain_ref,
    bias_ref,
    out_ref,
    buffer,
    sems,
):
    step = pl.program_id(0)
    count = count_ref[0]

    def copy(k, half, b):
        return pltpu.make_async_copy(
            buffer.at[half, b], out_ref.at[slot_ref[k]], sems.at[half, b]
        )

    def drain(at):
        for b in range(GROUP):
            k = at * GROUP + b

            @pl.when((at >= 0) & (k < count))
            def _():
                copy(k, at % 2, b).wait()

    drain(step - 2)

    @pl.when(step * GROUP < count)
    def _():
        sums = jnp.sum(sums_ref[...], axis=0)
        mean = sums[0:1] / sums[2:3]
        variance = sums[1:2] / sums[2:3] - mean * mean
        factor = gain_ref[...] / jnp.sqrt(variance + EPSILON)
        bias = bias_ref[...]
        for b in range(GROUP):
            k = step * GROUP + b

            @pl.when(k < count)
            def _():
                bx = place_ref[k] // 32
                for x in range(E):
                    conv = conv_ref[b, x * 64 : (x + 1) * 64, :].astype(jnp.float32)
                    if x in (0, E - 1):
                        own = face_ref[b].astype(jnp.float32)
                        conv = jnp.where(bx == (0 if x == 0 else 1), own, conv)
                    scaled = factor * (conv - mean) + bias
                    silu = scaled * (0.5 + 0.5 * jnp.tanh(0.5 * scaled))
                    silu = jnp.where(conv > 0.5 * ABSENT, silu, 0.0)
                    centre = centre_ref[b, x * 64 : (x + 1) * 64, :].astype(jnp.float32)
                    buffer[step % 2, b, x * 64 : (x + 1) * 64, :] = (centre + silu).astype(
                        jnp.bfloat16
                    )
                copy(k, step % 2, b).start()

    @pl.when(step == pl.num_programs(0) - 1)
    def _():
        drain(step - 1)
        drain(step)


def finish(slots, places, count, conv, centre, face, sums, gain, bias):
    whole = pl.BlockSpec(memory_space=pltpu.VMEM)

    def last(i, count):
        return jnp.minimum(i, jnp.maximum((count[0] - 1) // GROUP, 0))

    def shifted_block(i, slots, places, count):
        return (last(i, count) + 1, 0, 0)

    def block(i, slots, places, count):
        return (last(i, count), 0, 0)

    return pl.pallas_call(
        finish_kernel,
        grid_spec=pltpu.PrefetchScalarGridSpec(
            num_scalar_prefetch=3,
            grid=(32 // GROUP,),
            in_specs=[
                pl.BlockSpec((GROUP, 512, C), shifted_block),
                pl.BlockSpec((GROUP, 512, C), shifted_block),
                pl.BlockSpec((GROUP, 64, C), block),
                whole,
                whole,
                whole,
            ],
            out_specs=pl.BlockSpec(memory_space=pl.ANY),
            scratch_shapes=[
                pltpu.VMEM((2, GROUP, 512, C), jnp.bfloat16),
                pltpu.SemaphoreType.DMA((2, GROUP)),
            ],
        ),
        out_shape=jax.ShapeDtypeStruct((32, 512, C), jnp.bfloat16),
        compiler_params=pltpu.CompilerParams(vmem_limit_bytes=56 * MIB),
    )(slots, places, count, conv, centre, face, sums, gain, bias)


def pick_kernel(index_ref, in_ref, out_ref, buffer, sems):
    reads = [
        pltpu.make_async_copy(in_ref.at[index_ref[i]], buffer.at[i], sems.at[0, i])
        for i in range(O)
    ]
    writes = [
        pltpu.make_async_copy(buffer.at[i], out_ref.at[i], sems.at[1, i]) for i in range(O)
    ]
    for read in reads:
        read.start()
    for read, write in zip(reads, writes):
        read.wait()
        write.start()
    for write in writes:
        write.wait()


def pick(index, received):
    return pl.pallas_call(
        pick_kernel,
        in_specs=[pl.BlockSpec(memory_space=pltpu.SMEM), pl.BlockSpec(memory_space=pl.ANY)],
        out_specs=pl.BlockSpec(memory_space=pl.ANY),
        scratch_shapes=[
            pltpu.VMEM((O, 512, C), jnp.bfloat16),
            pltpu.SemaphoreType.DMA((2, O)),
        ],
        out_shape=jax.ShapeDtypeStruct((O, 512, C), jnp.bfloat16),
    )(index, received)


def swap(spread, axis):
    return lax.all_to_all(spread, axis, 0, 0, tiled=True)


def neighbours(low_block, high_block, axis):
    count = lax.axis_size(axis)
    up = [(i, i + 1) for i in range(count - 1)]
    down = [(j, i) for i, j in up]
    return lax.ppermute(high_block, axis, up), lax.ppermute(low_block, axis, down)


def edges_kernel(
    owner_ref,
    active_ref,
    occupancy_ref,
    features_ref,
    lines_ref,
    x_first_ref,
    x_last_ref,
    y_first_ref,
    y_last_ref,
    ends_first_ref,
    ends_last_ref,
    place_ref,
    slot_ref,
    count_ref,
    sent_ref,
    raw,
    met,
    sems,
):
    copies = [
        pltpu.make_async_copy(features_ref.at[0], raw.at[0], sems.at[0]),
        pltpu.make_async_copy(features_ref.at[15], raw.at[1], sems.at[1]),
        pltpu.make_async_copy(features_ref.at[:, 0], raw.at[2], sems.at[2]),
        pltpu.make_async_copy(features_ref.at[:, 15], raw.at[3], sems.at[3]),
    ]
    for copy in copies:
        copy.start()

    for i in range(17):
        met[i] = 0
    for i in range(32):
        sent_ref[i] = -1
    for i in range(48):
        place_ref[i] = 0
        slot_ref[i] = 0

    def route(i, carry):
        owned = owner_ref[i // 32, i // 16 % 2, i % 16]

        @pl.when(owned >= 0)
        def _():
            owner = owned // 16
            slot = 2 * owner + met[owner]
            rank = met[16]
            met[owner] = met[owner] + 1
            met[16] = rank + 1
            place_ref[rank] = i
            slot_ref[rank] = slot
            sent_ref[slot] = owned % 16

        return carry

    lax.fori_loop(0, 64, route, 0)
    count_ref[0] = met[16]
    count_ref[1] = (met[16] + 2 * GROUP - 1) // (2 * GROUP)

    repeat = jnp.where(
        lax.broadcasted_iota(jnp.int32, (16, C), 1) // E
        == lax.broadcasted_iota(jnp.int32, (16, C), 0),
        1.0,
        0.0,
    ).astype(jnp.bfloat16)
    for bx in range(2):
        spread = jnp.dot(
            jnp.where(active_ref[bx] >= 0, 1.0, 0.0).astype(jnp.bfloat16),
            repeat,
            preferred_element_type=jnp.float32,
        )
        for x in range(bx * E, bx * E + E):
            for by in range(2):
                at = x * 16 + by * E
                lines_ref[at : at + E, :] = (
                    occupancy_ref[at : at + E, :].astype(jnp.float32) * spread[by : by + 1, :]
                )
    columns = [jnp.transpose(lines_ref[128 * i : 128 * i + 128, :]) for i in range(2)]

    def masked(source, at, x, y):
        column = x % E * 16 + y
        live = jnp.broadcast_to(columns[x // E][:, column : column + 1], (128, C))
        return (raw[source, at].astype(jnp.float32) * live).astype(jnp.bfloat16)

    for source, ref, ends, y in ((2, y_first_ref, ends_first_ref, 0), (3, y_last_ref, ends_last_ref, 15)):
        copies[source].wait()
        for x in range(16):
            line = masked(source, x, x, y)
            ref[x, 0] = line
            if x in (0, 15):
                ends[x // 15, 0] = line
    for source, ref, x in ((0, x_first_ref, 0), (1, x_last_ref, 15)):
        copies[source].wait()
        for y in range(16):
            ref[0, y] = masked(source, y, x, y)


def find_edges(owner_map, occupancy, features):
    whole = pl.BlockSpec(memory_space=pltpu.VMEM)
    scalars = pl.BlockSpec(memory_space=pltpu.SMEM)
    blocks = [(1, 16), (1, 16), (16, 1), (16, 1), (2, 1), (2, 1)]
    return pl.pallas_call(
        edges_kernel,
        in_specs=[scalars, whole, whole, pl.BlockSpec(memory_space=pl.ANY)],
        out_specs=[whole] * 7 + [scalars] * 4,
        out_shape=[jax.ShapeDtypeStruct((256, 128), jnp.float32)]
        + [jax.ShapeDtypeStruct(block + (128, C), jnp.bfloat16) for block in blocks]
        + [jax.ShapeDtypeStruct((n,), jnp.int32) for n in (48, 48, 2, 32)],
        scratch_shapes=[
            pltpu.VMEM((4, 16, 128, C), jnp.bfloat16),
            pltpu.SMEM((17,), jnp.int32),
            pltpu.SemaphoreType.DMA((4,)),
        ],
        compiler_params=pltpu.CompilerParams(vmem_limit_bytes=56 * MIB),
    )(owner_map, owner_map, occupancy, features)


def widen_kernel(first_ref, last_ref, low_ref, high_ref, first_out, last_out):
    for i, (ref, out) in enumerate(((first_ref, first_out), (last_ref, last_out))):
        out[0, 0:1] = low_ref[i]
        out[0, 1:17] = ref[0]
        out[0, 17:18] = high_ref[i]


def widen(first, last, low, high):
    whole = pl.BlockSpec(memory_space=pltpu.VMEM)
    return pl.pallas_call(
        widen_kernel,
        in_specs=[whole] * 4,
        out_specs=[whole] * 2,
        out_shape=[jax.ShapeDtypeStruct((1, 18, 128, C), jnp.bfloat16)] * 2,
        compiler_params=pltpu.CompilerParams(vmem_limit_bytes=16 * MIB),
    )(first, last, low, high)


def on_device(features, occupancy, owner_map, kernel, norm_gain, norm_bias):
    lines, x_first, x_last, y_first, y_last, ends_first, ends_last, *routes = find_edges(
        owner_map, occupancy.reshape(256, 128), features
    )
    places, slot_of, counts, sent = routes
    line_low, line_high = neighbours(ends_first, ends_last, "gy")
    y_low, y_high = neighbours(y_first, y_last, "gy")
    x_low, x_high = neighbours(*widen(x_first, x_last, line_low, line_high), "gx")
    conv, centre, partial, sums = convolve(places, counts, features, y_low, y_high, lines, kernel)
    face_conv, spread = correct_faces(
        places, counts, x_low, x_high, partial, sums, lines, kernel, sent
    )
    arrived = swap(spread, "gx")
    totals = swap(jnp.broadcast_to(jnp.sum(arrived, axis=0)[None], (8, E, C)), "gy")
    result = finish(
        slot_of,
        places,
        counts,
        conv,
        centre,
        face_conv,
        totals,
        norm_gain.reshape(1, C),
        norm_bias.reshape(1, C),
    )
    received = swap(result.reshape(16, 2, 512, C), "gx").reshape(32, 512, C)
    named = arrived[:, 3, 0:2].reshape(32).astype(jnp.int32)
    owned = jnp.arange(O, dtype=jnp.int32)
    source = jnp.sum(
        jnp.where(named[None, :] == owned[:, None], jnp.arange(32, dtype=jnp.int32)[None, :], 0),
        axis=1,
    )
    return pick(source, received).reshape(O, 1, 512, C)


def solution(mesh):
    in_specs = (P("gx", "gy", None, None), P("gx", "gy", None), P("gx", "gy", None), P(), P(), P())
    out_specs = P("gx", "gy", None, None)
    return jax.shard_map(
        on_device, mesh=mesh, in_specs=in_specs, out_specs=out_specs, check_vma=False
    )
```

```python
import functools

import jax
import jax.numpy as jnp
from jax import lax
from jax.experimental import pallas as pl
from jax.experimental.pallas import tpu as pltpu
from jax.sharding import PartitionSpec as P

O = 16
E = 8
C = 128
GROUP = 4
ABSENT = -1e30
EPSILON = 1e-05
MIB = 1 << 20


def pair_taps(weight_ref, taps_ref, index):
    blank = jnp.zeros((C, C), jnp.bfloat16)
    for a in range(weight_ref.shape[0]):
        for dz in range(3):
            for j in range(4):
                at = (dz * 4 + j) * C
                weight_ref[a, at : at + C, 0:C] = (
                    taps_ref[index(a, dz, j)] if j < 3 else blank
                )
                weight_ref[a, at : at + C, C : 2 * C] = (
                    taps_ref[index(a, dz, j - 1)] if j > 0 else blank
                )


def shifted_scratch():
    return pltpu.VMEM((2, 3, 2, GROUP, 5, 5, 16, C), jnp.bfloat16)


def conv_kernel(
    place_ref,
    count_ref,
    features_ref,
    y_low_ref,
    y_high_ref,
    taps_hbm,
    occupied_ref,
    conv_ref,
    centre_ref,
    face_ref,
    sums_ref,
    stage,
    out_sems,
    padded,
    raw,
    margins,
    columns_ref,
    taps_ref,
    weight_ref,
    shifted_a,
    shifted_b,
    total_a,
    total_b,
    sems,
):
    count, steps = count_ref[0], count_ref[1]
    chunks = [
        pltpu.make_async_copy(
            features_ref.at[4 * i : 4 * i + 4], raw.at[i % 2], sems.at[i]
        )
        for i in range(4)
    ]
    lane = lax.broadcasted_iota(jnp.int32, (E, C), 1)

    def place_of(k):
        place = place_ref[k]
        return place // 32, place // 16 % 2, place % 16

    def prepare(group, shifted):
        for b in range(GROUP):
            bx, by, bz = place_of(group * GROUP + b)
            for dz in range(3):
                for xx in range(10):
                    lines = [
                        padded[bx * E + xx, by * E + yy, pl.ds(bz * E + 7 + dz, E), :]
                        for yy in range(10)
                    ]
                    for parity in range(2):
                        for yp in range(5 - parity):
                            pair = jnp.concatenate(
                                [lines[2 * yp + parity], lines[2 * yp + parity + 1]], axis=0
                            )
                            shifted[parity, dz, xx % 2, b, xx // 2, yp] = pair.astype(jnp.bfloat16)

    def multiply(shifted, total):
        for dy in range(3):
            parity, first = dy % 2, dy // 2
            parts = []
            for dz in range(3):
                for j in range(4):
                    part = shifted[
                        parity, dz, j % 2, :, j // 2 : j // 2 + 4, first : first + 4, :, :
                    ]
                    parts.append(part.reshape(GROUP * 256, C))
            product = jnp.dot(
                jnp.concatenate(parts, axis=1),
                weight_ref[dy],
                preferred_element_type=jnp.float32,
            )
            if dy == 0:
                total[...] = product
            else:
                total[...] += product

    def emit(group, shifted, total, parity, at):
        summed = jnp.zeros((E, C), jnp.float32)
        squared = jnp.zeros((E, C), jnp.float32)
        counted = jnp.zeros((E, C), jnp.float32)
        for b in range(GROUP):
            k = group * GROUP + b
            bx, by, bz = place_of(k)
            valid = jnp.where(k < count, 1.0, 0.0)
            near = columns_ref[bx, pl.ds(pl.multiple_of(bz * E, E), E), :] * valid
            near = pltpu.roll(near, C - by * E, axis=1)
            counted += jnp.where(lane % 16 < E, near, 0.0)
            for x in range(E):
                live = jnp.concatenate(
                    [
                        jnp.broadcast_to(near[:, x * 16 + y : x * 16 + y + 1], (E, C))
                        for y in range(E)
                    ],
                    axis=0,
                )
                block = total[b * 256 + (x // 2) * 64 : b * 256 + (x // 2) * 64 + 64,
                              (x % 2) * C : (x % 2 + 1) * C]
                wide = (block * live).astype(jnp.bfloat16).astype(jnp.float32)
                kept = wide
                if x == 0:
                    kept = wide * jnp.where(bx == 0, 0.0, 1.0)
                    face_low = block
                if x == E - 1:
                    kept = wide * jnp.where(bx == 0, 1.0, 0.0)
                    face_ref[k] = jnp.where(bx == 0, face_low, block)
                summed += jnp.sum(kept.reshape(E, E, C), axis=0)
                squared += jnp.sum((kept * kept).reshape(E, E, C), axis=0)
                stage[parity, 0, at + b, x * 64 : (x + 1) * 64, :] = jnp.where(
                    live > 0.5, wide, ABSENT
                ).astype(jnp.bfloat16)
                stage[parity, 1, at + b, x * 64 : (x + 1) * 64, :] = shifted[
                    1, 1, (x + 1) % 2, b, (x + 1) // 2, 0:4
                ].reshape(64, C)
        sums_ref[0] += summed
        sums_ref[1] += squared
        sums_ref[2] += counted

    extra = [
        pltpu.make_async_copy(y_low_ref, margins.at[0], sems.at[4]),
        pltpu.make_async_copy(y_high_ref, margins.at[1], sems.at[5]),
        pltpu.make_async_copy(taps_hbm, taps_ref, sems.at[6]),
    ]
    for copy in [chunks[0], chunks[1]] + extra:
        copy.start()
    edge = jnp.zeros((18, 18, E, C), jnp.float32)
    padded[:, :, 0:8, :] = edge
    padded[:, :, 136:144, :] = edge
    side = jnp.zeros((18, 128, C), jnp.float32)
    padded[0, :, 8:136, :] = side
    padded[17, :, 8:136, :] = side
    sums_ref[...] = jnp.zeros_like(sums_ref)
    for i in range(2):
        columns_ref[i] = jnp.transpose(occupied_ref[128 * i : 128 * i + 128, :])
    for i in range(4):
        chunks[i].wait()
        columns = columns_ref[i // 2]

        def mask_plane(j, carry, i=i, columns=columns):
            near = pltpu.roll(columns, 128 - 64 * (i % 2) - 16 * j, axis=1)
            for y in range(16):
                live = jnp.broadcast_to(near[:, y : y + 1], (128, C))
                padded[1 + 4 * i + j, 1 + y, 8:136, :] = (
                    raw[i % 2, j, y].astype(jnp.float32) * live
                )
            return carry

        lax.fori_loop(0, 4, mask_plane, 0)
        if i < 2:
            chunks[i + 2].start()
    for copy in extra:
        copy.wait()
    for side in range(2):
        padded[1:17, 17 * side, 8:136, :] = (
            margins[side].reshape(16, 128, C).astype(jnp.float32)
        )
    pair_taps(weight_ref, taps_ref, lambda dy, dz, dx: 9 * dx + 3 * dy + dz)

    @pl.when(steps > 0)
    def _():
        prepare(0, shifted_a)

    def outgoing(step):
        rows = pl.ds(step * 2 * GROUP, 2 * GROUP)
        return [
            pltpu.make_async_copy(
                stage.at[step % 2, i], ref.at[rows], out_sems.at[step % 2, i]
            )
            for i, ref in enumerate((conv_ref, centre_ref))
        ]

    def drain(step):
        for copy in outgoing(step):
            copy.wait()

    def pair(step, carry):
        @pl.when(step >= 2)
        def _():
            drain(step - 2)

        prepare(2 * step + 1, shifted_b)
        multiply(shifted_a, total_a)
        emit(2 * step, shifted_a, total_a, step % 2, 0)
        multiply(shifted_b, total_b)
        emit(2 * step + 1, shifted_b, total_b, step % 2, GROUP)
        prepare(2 * step + 2, shifted_a)

        for copy in outgoing(step):
            copy.start()
        return carry

    lax.fori_loop(0, steps, pair, 0)

    @pl.when(steps >= 2)
    def _():
        drain(steps - 2)

    @pl.when(steps >= 1)
    def _():
        drain(steps - 1)


def convolve(places, count, features, y_low, y_high, occupied, taps):
    any_spec = pl.BlockSpec(memory_space=pl.ANY)
    whole = pl.BlockSpec(memory_space=pltpu.VMEM)
    scalars = pl.BlockSpec(memory_space=pltpu.SMEM)
    return pl.pallas_call(
        conv_kernel,
        in_specs=[scalars, scalars] + [any_spec] * 4 + [whole],
        out_specs=[any_spec] * 2 + [whole] * 2,
        out_shape=[
            jax.ShapeDtypeStruct((32, 512, C), jnp.bfloat16),
            jax.ShapeDtypeStruct((32, 512, C), jnp.bfloat16),
            jax.ShapeDtypeStruct((32, 64, C), jnp.float32),
            jax.ShapeDtypeStruct((3, E, C), jnp.float32),
        ],
        scratch_shapes=[
            pltpu.VMEM((2, 2, 2 * GROUP, 512, C), jnp.bfloat16),
            pltpu.SemaphoreType.DMA((2, 2)),
            pltpu.VMEM((18, 18, 144, C), jnp.float32),
            pltpu.VMEM((2, 4, 16, 128, C), jnp.bfloat16),
            pltpu.VMEM((2, 16, 1, 128, C), jnp.bfloat16),
            pltpu.VMEM((2, C, C), jnp.float32),
            pltpu.VMEM((27, C, C), jnp.bfloat16),
            pltpu.VMEM((3, 12 * C, 2 * C), jnp.bfloat16),
            shifted_scratch(),
            shifted_scratch(),
            pltpu.VMEM((GROUP * 256, 2 * C), jnp.float32),
            pltpu.VMEM((GROUP * 256, 2 * C), jnp.float32),
            pltpu.SemaphoreType.DMA((7,)),
        ],
        compiler_params=pltpu.CompilerParams(vmem_limit_bytes=52 * MIB),
        cost_estimate=pl.CostEstimate(
            flops=2 * 32 * 256 * 4608 * 256, bytes_accessed=30 * MIB, transcendentals=0
        ),
    )(places, count, features, y_low, y_high, taps, occupied)


def face_kernel(
    place_ref,
    count_ref,
    x_low_ref,
    x_high_ref,
    partial_hbm,
    sums_ref,
    occupied_ref,
    taps_ref,
    slots_ref,
    out_ref,
    norm_ref,
    partial_ref,
    buffer,
    sems,
    columns_ref,
    padded,
    shifted,
    added,
    weight_ref,
):
    count = count_ref[0]
    fetch = pltpu.make_async_copy(partial_hbm, partial_ref, sems.at[8])
    fetch.start()
    pair_taps(weight_ref, taps_ref, lambda side, dz, dy: 18 * side + 3 * dy + dz)
    for i in range(2):
        columns_ref[i] = jnp.transpose(occupied_ref[128 * i : 128 * i + 128, :])
    padded[:, 0:8, :] = jnp.zeros((18, E, C), jnp.float32)
    padded[:, 136:144, :] = jnp.zeros((18, E, C), jnp.float32)
    for side, ref in enumerate((x_low_ref, x_high_ref)):
        padded[:, 8:136, :] = ref[0].astype(jnp.float32)
        for dz in range(3):
            shifted[dz] = padded[:, 7 + dz : 135 + dz, :].astype(jnp.bfloat16).reshape(
                9, 2, 128, C
            )
        parts = []
        for dz in range(3):
            for j in range(4):
                parts.append(shifted[dz, j // 2 : j // 2 + 8, j % 2].reshape(1024, C))
        added[side] = jnp.dot(
            jnp.concatenate(parts, axis=1), weight_ref[side], preferred_element_type=jnp.float32
        )

    fetch.wait()

    def outgoing(i):
        rows = pl.ds(i * GROUP, GROUP)
        return pltpu.make_async_copy(buffer.at[rows], out_ref.at[rows], sems.at[i])

    def several(i, carry):
        summed, squared = carry
        for b in range(GROUP):
            k = i * GROUP + b
            place = place_ref[k]
            bx, by, bz = place // 32, place // 16 % 2, place % 16
            valid = jnp.where(k < count, 1.0, 0.0)
            near = columns_ref[bx, pl.ds(pl.multiple_of(bz * E, E), E), :] * valid
            near = pltpu.roll(near, C - bx * 112 - by * E, axis=1)
            live = jnp.concatenate(
                [jnp.broadcast_to(near[:, y : y + 1], (E, C)) for y in range(E)], axis=0
            )
            pieces = []
            for y in range(E):
                start = pl.multiple_of((by * 4 + y // 2) * 128 + bz * E, E)
                pieces.append(added[bx, pl.ds(start, E), (y % 2) * C : (y % 2 + 1) * C])
            block = partial_ref[k] + jnp.concatenate(pieces, axis=0)
            wide = (block * live).astype(jnp.bfloat16).astype(jnp.float32)
            wide = jnp.where(live > 0.5, wide, 0.0)
            buffer[k] = jnp.where(live > 0.5, wide, ABSENT).astype(jnp.bfloat16)
            summed += jnp.sum(wide.reshape(E, E, C), axis=0)
            squared += jnp.sum((wide * wide).reshape(E, E, C), axis=0)
        outgoing(i).start()
        return summed, squared

    rounds = (count + GROUP - 1) // GROUP
    summed, squared = lax.fori_loop(0, rounds, several, (sums_ref[0], sums_ref[1]))
    table = jnp.concatenate(
        [
            jnp.sum(summed, axis=0, keepdims=True),
            jnp.sum(squared, axis=0, keepdims=True),
            jnp.broadcast_to(jnp.sum(sums_ref[2]), (1, C)),
            jnp.zeros((5, C), jnp.float32),
        ],
        axis=0,
    )
    norm_ref[...] = jnp.broadcast_to(table[None], norm_ref.shape)
    wide_lane = lax.broadcasted_iota(jnp.int32, (1, C), 1)
    for i in range(16):
        pair = jnp.where(wide_lane == 0, slots_ref[2 * i], slots_ref[2 * i + 1])
        norm_ref[i, 3:4, :] = pair.astype(jnp.float32)

    def drain(i, carry):
        outgoing(i).wait()
        return carry

    lax.fori_loop(0, rounds, drain, 0)


def correct_faces(places, count, x_low, x_high, partial, sums, occupied, taps, sent):
    any_spec = pl.BlockSpec(memory_space=pl.ANY)
    whole = pl.BlockSpec(memory_space=pltpu.VMEM)
    scalars = pl.BlockSpec(memory_space=pltpu.SMEM)
    return pl.pallas_call(
        face_kernel,
        in_specs=[scalars, scalars, whole, whole, any_spec] + [whole] * 3 + [scalars],
        out_specs=[any_spec, whole],
        out_shape=[
            jax.ShapeDtypeStruct((32, 64, C), jnp.bfloat16),
            jax.ShapeDtypeStruct((16, E, C), jnp.float32),
        ],
        scratch_shapes=[
            pltpu.VMEM((32, 64, C), jnp.float32),
            pltpu.VMEM((32, 64, C), jnp.bfloat16),
            pltpu.SemaphoreType.DMA((9,)),
            pltpu.VMEM((2, C, C), jnp.float32),
            pltpu.VMEM((18, 144, C), jnp.float32),
            pltpu.VMEM((3, 9, 2, 128, C), jnp.bfloat16),
            pltpu.VMEM((2, 1024, 2 * C), jnp.float32),
            pltpu.VMEM((2, 12 * C, 2 * C), jnp.bfloat16),
        ],
        compiler_params=pltpu.CompilerParams(vmem_limit_bytes=32 * MIB),
    )(places, count, x_low, x_high, partial, sums, occupied, taps, sent)


def finish_kernel(
    slot_ref,
    place_ref,
    count_ref,
    conv_hbm,
    centre_hbm,
    face_ref,
    sums_ref,
    gain_ref,
    bias_ref,
    out_ref,
    conv_ref,
    centre_ref,
    buffer,
    in_sems,
    sems,
):
    count = count_ref[0]

    def incoming(group):
        rows = pl.ds(group * GROUP, GROUP)
        return [
            pltpu.make_async_copy(hbm.at[rows], ref.at[rows], in_sems.at[i, group])
            for i, (hbm, ref) in enumerate(((conv_hbm, conv_ref), (centre_hbm, centre_ref)))
        ]

    for group in range(32 // GROUP):

        @pl.when(group * GROUP < count)
        def _():
            for each in incoming(group):
                each.start()

    sums = jnp.sum(sums_ref[...], axis=0)
    mean = sums[0:1] / sums[2:3]
    variance = sums[1:2] / sums[2:3] - mean * mean
    factor = gain_ref[...] / jnp.sqrt(variance + EPSILON)
    bias = bias_ref[...]

    def copy(k):
        return pltpu.make_async_copy(buffer.at[k], out_ref.at[slot_ref[k]], sems.at[k])

    def one(k, carry):
        @pl.when(k % GROUP == 0)
        def _():
            for each in incoming(k // GROUP):
                each.wait()

        bx = place_ref[k] // 32
        for x in range(E):
            conv = conv_ref[k, x * 64 : (x + 1) * 64, :].astype(jnp.float32)
            if x in (0, E - 1):
                own = face_ref[k].astype(jnp.float32)
                conv = jnp.where(bx == (0 if x == 0 else 1), own, conv)
            scaled = factor * (conv - mean) + bias
            silu = scaled * (0.5 + 0.5 * jnp.tanh(0.5 * scaled))
            silu = jnp.where(conv > 0.5 * ABSENT, silu, 0.0)
            centre = centre_ref[k, x * 64 : (x + 1) * 64, :].astype(jnp.float32)
            buffer[k, x * 64 : (x + 1) * 64, :] = (centre + silu).astype(jnp.bfloat16)
        copy(k).start()
        return carry

    def drain(k, carry):
        copy(k).wait()
        return carry

    lax.fori_loop(0, count, one, 0)
    lax.fori_loop(0, count, drain, 0)


def finish(slots, places, count, conv, centre, face, sums, gain, bias):
    whole = pl.BlockSpec(memory_space=pltpu.VMEM)
    scalars = pl.BlockSpec(memory_space=pltpu.SMEM)
    return pl.pallas_call(
        finish_kernel,
        in_specs=[scalars] * 3 + [pl.BlockSpec(memory_space=pl.ANY)] * 2 + [whole] * 4,
        out_specs=pl.BlockSpec(memory_space=pl.ANY),
        scratch_shapes=[
            pltpu.VMEM((32, 512, C), jnp.bfloat16),
            pltpu.VMEM((32, 512, C), jnp.bfloat16),
            pltpu.VMEM((32, 512, C), jnp.bfloat16),
            pltpu.SemaphoreType.DMA((2, 32 // GROUP)),
            pltpu.SemaphoreType.DMA((32,)),
        ],
        out_shape=jax.ShapeDtypeStruct((32, 512, C), jnp.bfloat16),
        compiler_params=pltpu.CompilerParams(vmem_limit_bytes=56 * MIB),
    )(slots, places, count, conv, centre, face, sums, gain, bias)


def pick_kernel(named_ref, in_ref, out_ref, buffer, sems):
    named = named_ref[:, 3, :]
    lane = lax.broadcasted_iota(jnp.int32, (16, C), 1)
    source = 2 * lax.broadcasted_iota(jnp.int32, (16, C), 0) + lane
    reads, writes = [], []
    for i in range(O):
        hit = (named == float(i)) & (lane < 2)
        index = jnp.sum(jnp.where(hit, source, 0))
        reads.append(pltpu.make_async_copy(in_ref.at[index], buffer.at[i], sems.at[0, i]))
        writes.append(pltpu.make_async_copy(buffer.at[i], out_ref.at[i], sems.at[1, i]))
    for read in reads:
        read.start()
    for read, write in zip(reads, writes):
        read.wait()
        write.start()
    for write in writes:
        write.wait()


def pick(named, received):
    return pl.pallas_call(
        pick_kernel,
        in_specs=[pl.BlockSpec(memory_space=pltpu.VMEM), pl.BlockSpec(memory_space=pl.ANY)],
        out_specs=pl.BlockSpec(memory_space=pl.ANY),
        scratch_shapes=[
            pltpu.VMEM((O, 512, C), jnp.bfloat16),
            pltpu.SemaphoreType.DMA((2, O)),
        ],
        out_shape=jax.ShapeDtypeStruct((O, 512, C), jnp.bfloat16),
    )(named, received)


def swap(spread, axis):
    return lax.all_to_all(spread, axis, 0, 0, tiled=True)


def neighbours(low_block, high_block, axis):
    count = lax.axis_size(axis)
    up = [(i, i + 1) for i in range(count - 1)]
    down = [(j, i) for i, j in up]
    return lax.ppermute(high_block, axis, up), lax.ppermute(low_block, axis, down)


def masked_line(line, columns, x, y):
    column = x % E * 16 + y
    live = jnp.broadcast_to(columns[x // E][:, column : column + 1], (128, C))
    return (line.astype(jnp.float32) * live).astype(jnp.bfloat16)


def line_columns(lines_ref):
    return [jnp.transpose(lines_ref[128 * i : 128 * i + 128, :]) for i in range(2)]


def y_edges_kernel(
    active_ref,
    occupancy_ref,
    features_ref,
    lines_ref,
    first_ref,
    last_ref,
    ends_first_ref,
    ends_last_ref,
    raw,
    sems,
):
    copies = [
        pltpu.make_async_copy(features_ref.at[:, 15 * i], raw.at[i], sems.at[i]) for i in range(2)
    ]
    for copy in copies:
        copy.start()
    repeat = jnp.where(
        lax.broadcasted_iota(jnp.int32, (16, C), 1) // E
        == lax.broadcasted_iota(jnp.int32, (16, C), 0),
        1.0,
        0.0,
    ).astype(jnp.bfloat16)
    for bx in range(2):
        spread = jnp.dot(
            jnp.where(active_ref[bx] >= 0, 1.0, 0.0).astype(jnp.bfloat16),
            repeat,
            preferred_element_type=jnp.float32,
        )
        for x in range(bx * E, bx * E + E):
            for by in range(2):
                at = x * 16 + by * E
                lines_ref[at : at + E, :] = (
                    occupancy_ref[at : at + E, :].astype(jnp.float32) * spread[by : by + 1, :]
                )
    columns = line_columns(lines_ref)
    for i, (ref, ends) in enumerate(((first_ref, ends_first_ref), (last_ref, ends_last_ref))):
        copies[i].wait()
        for x in range(16):
            line = masked_line(raw[i, x], columns, x, 15 * i)
            ref[x, 0] = line
            if x in (0, 15):
                ends[x // 15, 0] = line


def x_edges_kernel(
    owner_ref,
    lines_ref,
    features_ref,
    first_ref,
    last_ref,
    place_ref,
    slot_ref,
    count_ref,
    sent_ref,
    raw,
    met,
    sems,
):
    copies = [
        pltpu.make_async_copy(features_ref.at[15 * i], raw.at[i], sems.at[i]) for i in range(2)
    ]
    for copy in copies:
        copy.start()

    for i in range(17):
        met[i] = 0
    for i in range(32):
        sent_ref[i] = -1
    for i in range(48):
        place_ref[i] = 0
        slot_ref[i] = 0

    def route(i, carry):
        owned = owner_ref[i // 32, i // 16 % 2, i % 16]

        @pl.when(owned >= 0)
        def _():
            owner = owned // 16
            slot = 2 * owner + met[owner]
            rank = met[16]
            met[owner] = met[owner] + 1
            met[16] = rank + 1
            place_ref[rank] = i
            slot_ref[rank] = slot
            sent_ref[slot] = owned % 16

        return carry

    lax.fori_loop(0, 64, route, 0)
    count_ref[0] = met[16]
    count_ref[1] = (met[16] + 2 * GROUP - 1) // (2 * GROUP)
    columns = line_columns(lines_ref)
    for i, ref in enumerate((first_ref, last_ref)):
        copies[i].wait()
        for y in range(16):
            ref[0, 1 + y] = masked_line(raw[i, y], columns, 15 * i, y)


def y_edges(owner_map, occupancy, features):
    whole = pl.BlockSpec(memory_space=pltpu.VMEM)
    blocks = [(16, 1), (16, 1), (2, 1), (2, 1)]
    return pl.pallas_call(
        y_edges_kernel,
        in_specs=[whole, whole, pl.BlockSpec(memory_space=pl.ANY)],
        out_specs=[whole] * 5,
        out_shape=[jax.ShapeDtypeStruct((256, 128), jnp.float32)]
        + [jax.ShapeDtypeStruct(block + (128, C), jnp.bfloat16) for block in blocks],
        scratch_shapes=[
            pltpu.VMEM((2, 16, 128, C), jnp.bfloat16),
            pltpu.SemaphoreType.DMA((2,)),
        ],
        compiler_params=pltpu.CompilerParams(vmem_limit_bytes=57 * MIB),
    )(owner_map, occupancy, features)


def x_edges(owner_map, lines, features):
    whole = pl.BlockSpec(memory_space=pltpu.VMEM)
    scalars = pl.BlockSpec(memory_space=pltpu.SMEM)
    return pl.pallas_call(
        x_edges_kernel,
        in_specs=[scalars, whole, pl.BlockSpec(memory_space=pl.ANY)],
        out_specs=[whole] * 2 + [scalars] * 4,
        out_shape=[jax.ShapeDtypeStruct((1, 18, 128, C), jnp.bfloat16)] * 2
        + [jax.ShapeDtypeStruct((n,), jnp.int32) for n in (48, 48, 2, 32)],
        scratch_shapes=[
            pltpu.VMEM((2, 16, 128, C), jnp.bfloat16),
            pltpu.SMEM((17,), jnp.int32),
            pltpu.SemaphoreType.DMA((2,)),
        ],
        compiler_params=pltpu.CompilerParams(vmem_limit_bytes=57 * MIB),
    )(owner_map, lines, features)


def widen_kernel(first_ref, last_ref, low_ref, high_ref, first_out, last_out, sems):
    copies = []
    for i, out in enumerate((first_out, last_out)):
        for j, ref in enumerate((low_ref, high_ref)):
            copies.append(
                pltpu.make_async_copy(ref.at[i], out.at[0, 17 * j : 17 * j + 1], sems.at[i, j])
            )
    for copy in copies:
        copy.start()
    for copy in copies:
        copy.wait()


def widen(first, last, low, high):
    any_spec = pl.BlockSpec(memory_space=pl.ANY)
    return pl.pallas_call(
        widen_kernel,
        in_specs=[any_spec] * 2 + [pl.BlockSpec(memory_space=pltpu.VMEM)] * 2,
        out_specs=[any_spec] * 2,
        out_shape=[jax.ShapeDtypeStruct((1, 18, 128, C), jnp.bfloat16)] * 2,
        scratch_shapes=[pltpu.SemaphoreType.DMA((2, 2))],
        input_output_aliases={0: 0, 1: 1},
    )(first, last, low, high)


def on_device(features, occupancy, owner_map, kernel, norm_gain, norm_bias):
    lines, y_first, y_last, ends_first, ends_last = y_edges(
        owner_map, occupancy.reshape(256, 128), features
    )
    line_low, line_high = neighbours(ends_first, ends_last, "gy")
    y_low, y_high = neighbours(y_first, y_last, "gy")
    x_first, x_last, places, slot_of, counts, sent = x_edges(owner_map, lines, features)
    x_low, x_high = neighbours(*widen(x_first, x_last, line_low, line_high), "gx")
    conv, centre, partial, sums = convolve(places, counts, features, y_low, y_high, lines, kernel)
    face_conv, spread = correct_faces(
        places, counts, x_low, x_high, partial, sums, lines, kernel, sent
    )
    arrived = swap(spread, "gx")
    totals = swap(jnp.broadcast_to(jnp.sum(arrived, axis=0)[None], (8, E, C)), "gy")
    result = finish(
        slot_of,
        places,
        counts,
        conv,
        centre,
        face_conv,
        totals,
        norm_gain.reshape(1, C),
        norm_bias.reshape(1, C),
    )
    received = swap(result.reshape(16, 2, 512, C), "gx").reshape(32, 512, C)
    return pick(arrived, received).reshape(O, 1, 512, C)


def solution(mesh):
    in_specs = (P("gx", "gy", None, None), P("gx", "gy", None), P("gx", "gy", None), P(), P(), P())
    out_specs = P("gx", "gy", None, None)
    return jax.shard_map(
        on_device, mesh=mesh, in_specs=in_specs, out_specs=out_specs, check_vma=False
    )
```

```python
import functools

import jax
import jax.numpy as jnp
from jax import lax
from jax.experimental import pallas as pl
from jax.experimental.pallas import tpu as pltpu
from jax.sharding import PartitionSpec as P

O = 16
SLOTS, SENT, COUNT = 48, 96, 128
E = 8
C = 128
GROUP = 4
ABSENT = -1e30
EPSILON = 1e-05
MIB = 1 << 20


def pair_taps(weight_ref, taps_ref, index):
    blank = jnp.zeros((C, C), jnp.bfloat16)
    for a in range(weight_ref.shape[0]):
        for dz in range(3):
            for j in range(4):
                at = (dz * 4 + j) * C
                weight_ref[a, at : at + C, 0:C] = (
                    taps_ref[index(a, dz, j)] if j < 3 else blank
                )
                weight_ref[a, at : at + C, C : 2 * C] = (
                    taps_ref[index(a, dz, j - 1)] if j > 0 else blank
                )


def shifted_scratch():
    return pltpu.VMEM((2, 3, 2, GROUP, 5, 5, 16, C), jnp.bfloat16)


def conv_kernel(
    route_ref,
    features_ref,
    y_low_ref,
    y_high_ref,
    taps_hbm,
    occupied_ref,
    conv_ref,
    centre_ref,
    face_ref,
    sums_ref,
    stage,
    out_sems,
    padded,
    raw,
    margins,
    columns_ref,
    taps_ref,
    weight_ref,
    shifted_a,
    shifted_b,
    total_a,
    total_b,
    sems,
):
    count, steps = route_ref[COUNT], route_ref[COUNT + 1]
    chunks = [
        pltpu.make_async_copy(
            features_ref.at[4 * i : 4 * i + 4], raw.at[i % 2], sems.at[i]
        )
        for i in range(4)
    ]
    lane = lax.broadcasted_iota(jnp.int32, (E, C), 1)

    def place_of(k):
        place = route_ref[k]
        return place // 32, place // 16 % 2, place % 16

    def prepare(group, shifted):
        for b in range(GROUP):
            bx, by, bz = place_of(group * GROUP + b)
            for dz in range(3):
                for xx in range(10):
                    lines = [
                        padded[bx * E + xx, by * E + yy, pl.ds(bz * E + 7 + dz, E), :]
                        for yy in range(10)
                    ]
                    for parity in range(2):
                        for yp in range(5 - parity):
                            pair = jnp.concatenate(
                                [lines[2 * yp + parity], lines[2 * yp + parity + 1]], axis=0
                            )
                            shifted[parity, dz, xx % 2, b, xx // 2, yp] = pair.astype(jnp.bfloat16)

    def multiply(shifted, total):
        for dy in range(3):
            parity, first = dy % 2, dy // 2
            parts = []
            for dz in range(3):
                for j in range(4):
                    part = shifted[
                        parity, dz, j % 2, :, j // 2 : j // 2 + 4, first : first + 4, :, :
                    ]
                    parts.append(part.reshape(GROUP * 256, C))
            product = jnp.dot(
                jnp.concatenate(parts, axis=1),
                weight_ref[dy],
                preferred_element_type=jnp.float32,
            )
            if dy == 0:
                total[...] = product
            else:
                total[...] += product

    def emit(group, shifted, total, parity, at):
        summed = jnp.zeros((E, C), jnp.float32)
        squared = jnp.zeros((E, C), jnp.float32)
        counted = jnp.zeros((E, C), jnp.float32)
        for b in range(GROUP):
            k = group * GROUP + b
            bx, by, bz = place_of(k)
            valid = jnp.where(k < count, 1.0, 0.0)
            near = columns_ref[bx, pl.ds(pl.multiple_of(bz * E, E), E), :] * valid
            near = pltpu.roll(near, C - by * E, axis=1)
            counted += jnp.where(lane % 16 < E, near, 0.0)
            for x in range(E):
                live = jnp.concatenate(
                    [
                        jnp.broadcast_to(near[:, x * 16 + y : x * 16 + y + 1], (E, C))
                        for y in range(E)
                    ],
                    axis=0,
                )
                block = total[b * 256 + (x // 2) * 64 : b * 256 + (x // 2) * 64 + 64,
                              (x % 2) * C : (x % 2 + 1) * C]
                wide = (block * live).astype(jnp.bfloat16).astype(jnp.float32)
                kept = wide
                if x == 0:
                    kept = wide * jnp.where(bx == 0, 0.0, 1.0)
                    face_low = block
                if x == E - 1:
                    kept = wide * jnp.where(bx == 0, 1.0, 0.0)
                    face_ref[k] = jnp.where(bx == 0, face_low, block)
                summed += jnp.sum(kept.reshape(E, E, C), axis=0)
                squared += jnp.sum((kept * kept).reshape(E, E, C), axis=0)
                stage[parity, 0, at + b, x * 64 : (x + 1) * 64, :] = jnp.where(
                    live > 0.5, wide, ABSENT
                ).astype(jnp.bfloat16)
                stage[parity, 1, at + b, x * 64 : (x + 1) * 64, :] = shifted[
                    1, 1, (x + 1) % 2, b, (x + 1) // 2, 0:4
                ].reshape(64, C)
        sums_ref[0] += summed
        sums_ref[1] += squared
        sums_ref[2] += counted

    extra = [
        pltpu.make_async_copy(y_low_ref, margins.at[0], sems.at[4]),
        pltpu.make_async_copy(y_high_ref, margins.at[1], sems.at[5]),
        pltpu.make_async_copy(taps_hbm, taps_ref, sems.at[6]),
    ]
    for copy in [chunks[0], chunks[1]] + extra:
        copy.start()
    edge = jnp.zeros((18, 18, E, C), jnp.float32)
    padded[:, :, 0:8, :] = edge
    padded[:, :, 136:144, :] = edge
    side = jnp.zeros((18, 128, C), jnp.float32)
    padded[0, :, 8:136, :] = side
    padded[17, :, 8:136, :] = side
    sums_ref[...] = jnp.zeros_like(sums_ref)
    for i in range(2):
        columns_ref[i] = jnp.transpose(occupied_ref[128 * i : 128 * i + 128, :])
    for i in range(4):
        chunks[i].wait()
        columns = columns_ref[i // 2]

        def mask_plane(j, carry, i=i, columns=columns):
            near = pltpu.roll(columns, 128 - 64 * (i % 2) - 16 * j, axis=1)
            for y in range(16):
                live = jnp.broadcast_to(near[:, y : y + 1], (128, C))
                padded[1 + 4 * i + j, 1 + y, 8:136, :] = (
                    raw[i % 2, j, y].astype(jnp.float32) * live
                )
            return carry

        lax.fori_loop(0, 4, mask_plane, 0)
        if i < 2:
            chunks[i + 2].start()
    for copy in extra:
        copy.wait()
    for side in range(2):
        padded[1:17, 17 * side, 8:136, :] = (
            margins[side].reshape(16, 128, C).astype(jnp.float32)
        )
    pair_taps(weight_ref, taps_ref, lambda dy, dz, dx: 9 * dx + 3 * dy + dz)

    @pl.when(steps > 0)
    def _():
        prepare(0, shifted_a)

    def outgoing(step):
        rows = pl.ds(step * 2 * GROUP, 2 * GROUP)
        return [
            pltpu.make_async_copy(
                stage.at[step % 2, i], ref.at[rows], out_sems.at[step % 2, i]
            )
            for i, ref in enumerate((conv_ref, centre_ref))
        ]

    def drain(step):
        for copy in outgoing(step):
            copy.wait()

    def pair(step, carry):
        @pl.when(step >= 2)
        def _():
            drain(step - 2)

        prepare(2 * step + 1, shifted_b)
        multiply(shifted_a, total_a)
        emit(2 * step, shifted_a, total_a, step % 2, 0)
        multiply(shifted_b, total_b)
        emit(2 * step + 1, shifted_b, total_b, step % 2, GROUP)
        prepare(2 * step + 2, shifted_a)

        for copy in outgoing(step):
            copy.start()
        return carry

    lax.fori_loop(0, steps, pair, 0)

    @pl.when(steps >= 2)
    def _():
        drain(steps - 2)

    @pl.when(steps >= 1)
    def _():
        drain(steps - 1)


def convolve(routes, features, y_low, y_high, occupied, taps):
    any_spec = pl.BlockSpec(memory_space=pl.ANY)
    whole = pl.BlockSpec(memory_space=pltpu.VMEM)
    scalars = pl.BlockSpec(memory_space=pltpu.SMEM)
    return pl.pallas_call(
        conv_kernel,
        in_specs=[scalars] + [any_spec] * 4 + [whole],
        out_specs=[any_spec] * 2 + [whole] * 2,
        out_shape=[
            jax.ShapeDtypeStruct((32, 512, C), jnp.bfloat16),
            jax.ShapeDtypeStruct((32, 512, C), jnp.bfloat16),
            jax.ShapeDtypeStruct((32, 64, C), jnp.float32),
            jax.ShapeDtypeStruct((3, E, C), jnp.float32),
        ],
        scratch_shapes=[
            pltpu.VMEM((2, 2, 2 * GROUP, 512, C), jnp.bfloat16),
            pltpu.SemaphoreType.DMA((2, 2)),
            pltpu.VMEM((18, 18, 144, C), jnp.float32),
            pltpu.VMEM((2, 4, 16, 128, C), jnp.bfloat16),
            pltpu.VMEM((2, 16, 1, 128, C), jnp.bfloat16),
            pltpu.VMEM((2, C, C), jnp.float32),
            pltpu.VMEM((27, C, C), jnp.bfloat16),
            pltpu.VMEM((3, 12 * C, 2 * C), jnp.bfloat16),
            shifted_scratch(),
            shifted_scratch(),
            pltpu.VMEM((GROUP * 256, 2 * C), jnp.float32),
            pltpu.VMEM((GROUP * 256, 2 * C), jnp.float32),
            pltpu.SemaphoreType.DMA((7,)),
        ],
        compiler_params=pltpu.CompilerParams(vmem_limit_bytes=49 * MIB),
        cost_estimate=pl.CostEstimate(
            flops=2 * 32 * 256 * 4608 * 256, bytes_accessed=30 * MIB, transcendentals=0
        ),
    )(routes, features, y_low, y_high, taps, occupied)


def face_kernel(
    route_ref,
    x_low_ref,
    x_high_ref,
    partial_hbm,
    sums_ref,
    occupied_ref,
    taps_ref,
    out_ref,
    norm_ref,
    partial_ref,
    buffer,
    sems,
    columns_ref,
    padded,
    shifted,
    added,
    weight_ref,
):
    count = route_ref[COUNT]
    fetch = pltpu.make_async_copy(partial_hbm, partial_ref, sems.at[8])
    fetch.start()
    pair_taps(weight_ref, taps_ref, lambda side, dz, dy: 18 * side + 3 * dy + dz)
    for i in range(2):
        columns_ref[i] = jnp.transpose(occupied_ref[128 * i : 128 * i + 128, :])
    padded[:, 0:8, :] = jnp.zeros((18, E, C), jnp.float32)
    padded[:, 136:144, :] = jnp.zeros((18, E, C), jnp.float32)
    for side, ref in enumerate((x_low_ref, x_high_ref)):
        padded[:, 8:136, :] = ref[0].astype(jnp.float32)
        for dz in range(3):
            shifted[dz] = padded[:, 7 + dz : 135 + dz, :].astype(jnp.bfloat16).reshape(
                9, 2, 128, C
            )
        parts = []
        for dz in range(3):
            for j in range(4):
                parts.append(shifted[dz, j // 2 : j // 2 + 8, j % 2].reshape(1024, C))
        added[side] = jnp.dot(
            jnp.concatenate(parts, axis=1), weight_ref[side], preferred_element_type=jnp.float32
        )

    fetch.wait()

    def outgoing(i):
        rows = pl.ds(i * GROUP, GROUP)
        return pltpu.make_async_copy(buffer.at[rows], out_ref.at[rows], sems.at[i])

    def several(i, carry):
        summed, squared = carry
        for b in range(GROUP):
            k = i * GROUP + b
            place = route_ref[k]
            bx, by, bz = place // 32, place // 16 % 2, place % 16
            valid = jnp.where(k < count, 1.0, 0.0)
            near = columns_ref[bx, pl.ds(pl.multiple_of(bz * E, E), E), :] * valid
            near = pltpu.roll(near, C - bx * 112 - by * E, axis=1)
            live = jnp.concatenate(
                [jnp.broadcast_to(near[:, y : y + 1], (E, C)) for y in range(E)], axis=0
            )
            pieces = []
            for y in range(E):
                start = pl.multiple_of((by * 4 + y // 2) * 128 + bz * E, E)
                pieces.append(added[bx, pl.ds(start, E), (y % 2) * C : (y % 2 + 1) * C])
            block = partial_ref[k] + jnp.concatenate(pieces, axis=0)
            wide = (block * live).astype(jnp.bfloat16).astype(jnp.float32)
            wide = jnp.where(live > 0.5, wide, 0.0)
            buffer[k] = jnp.where(live > 0.5, wide, ABSENT).astype(jnp.bfloat16)
            summed += jnp.sum(wide.reshape(E, E, C), axis=0)
            squared += jnp.sum((wide * wide).reshape(E, E, C), axis=0)
        outgoing(i).start()
        return summed, squared

    rounds = (count + GROUP - 1) // GROUP
    summed, squared = lax.fori_loop(0, rounds, several, (sums_ref[0], sums_ref[1]))
    sums = [
        jnp.sum(summed, axis=0, keepdims=True),
        jnp.sum(squared, axis=0, keepdims=True),
        jnp.broadcast_to(jnp.sum(sums_ref[2]), (1, C)),
    ]
    first_lane = lax.broadcasted_iota(jnp.int32, (1, C), 1) == 0
    for i in range(16):
        pair = jnp.where(first_lane, route_ref[SENT + 2 * i], route_ref[SENT + 2 * i + 1])
        table = jnp.concatenate(sums + [pair.astype(jnp.float32)], axis=0)
        norm_ref[8 * i : 8 * i + 8] = jnp.broadcast_to(table[None], (8, 4, C))

    def drain(i, carry):
        outgoing(i).wait()
        return carry

    lax.fori_loop(0, rounds, drain, 0)


def correct_faces(routes, x_low, x_high, partial, sums, occupied, taps):
    any_spec = pl.BlockSpec(memory_space=pl.ANY)
    whole = pl.BlockSpec(memory_space=pltpu.VMEM)
    scalars = pl.BlockSpec(memory_space=pltpu.SMEM)
    return pl.pallas_call(
        face_kernel,
        in_specs=[scalars, whole, whole, any_spec] + [whole] * 3,
        out_specs=[any_spec, whole],
        out_shape=[
            jax.ShapeDtypeStruct((32, 64, C), jnp.bfloat16),
            jax.ShapeDtypeStruct((128, 4, C), jnp.float32),
        ],
        scratch_shapes=[
            pltpu.VMEM((32, 64, C), jnp.float32),
            pltpu.VMEM((32, 64, C), jnp.bfloat16),
            pltpu.SemaphoreType.DMA((9,)),
            pltpu.VMEM((2, C, C), jnp.float32),
            pltpu.VMEM((18, 144, C), jnp.float32),
            pltpu.VMEM((3, 9, 2, 128, C), jnp.bfloat16),
            pltpu.VMEM((2, 1024, 2 * C), jnp.float32),
            pltpu.VMEM((2, 12 * C, 2 * C), jnp.bfloat16),
        ],
        compiler_params=pltpu.CompilerParams(vmem_limit_bytes=32 * MIB),
    )(routes, x_low, x_high, partial, sums, occupied, taps)


def finish_kernel(
    route_ref,
    conv_hbm,
    centre_hbm,
    face_ref,
    sums_ref,
    gain_ref,
    bias_ref,
    out_ref,
    conv_ref,
    centre_ref,
    buffer,
    in_sems,
    sems,
):
    count = route_ref[COUNT]

    def incoming(group):
        rows = pl.ds(group * GROUP, GROUP)
        return [
            pltpu.make_async_copy(hbm.at[rows], ref.at[rows], in_sems.at[i, group])
            for i, (hbm, ref) in enumerate(((conv_hbm, conv_ref), (centre_hbm, centre_ref)))
        ]

    for group in range(32 // GROUP):

        @pl.when(group * GROUP < count)
        def _():
            for each in incoming(group):
                each.start()

    sums = jnp.sum(sums_ref[...], axis=0)
    mean = sums[0:1] / sums[2:3]
    variance = sums[1:2] / sums[2:3] - mean * mean
    factor = gain_ref[...] / jnp.sqrt(variance + EPSILON)
    bias = bias_ref[...]

    def copy(k):
        return pltpu.make_async_copy(buffer.at[k], out_ref.at[route_ref[SLOTS + k]], sems.at[k])

    def one(k, carry):
        @pl.when(k % GROUP == 0)
        def _():
            for each in incoming(k // GROUP):
                each.wait()

        bx = route_ref[k] // 32
        for x in range(E):
            conv = conv_ref[k, x * 64 : (x + 1) * 64, :].astype(jnp.float32)
            if x in (0, E - 1):
                own = face_ref[k].astype(jnp.float32)
                conv = jnp.where(bx == (0 if x == 0 else 1), own, conv)
            scaled = factor * (conv - mean) + bias
            silu = scaled * (0.5 + 0.5 * jnp.tanh(0.5 * scaled))
            silu = jnp.where(conv > 0.5 * ABSENT, silu, 0.0)
            centre = centre_ref[k, x * 64 : (x + 1) * 64, :].astype(jnp.float32)
            buffer[k, x * 64 : (x + 1) * 64, :] = (centre + silu).astype(jnp.bfloat16)
        copy(k).start()
        return carry

    def drain(k, carry):
        copy(k).wait()
        return carry

    lax.fori_loop(0, count, one, 0)
    lax.fori_loop(0, count, drain, 0)


def finish(routes, conv, centre, face, sums, gain, bias):
    whole = pl.BlockSpec(memory_space=pltpu.VMEM)
    scalars = pl.BlockSpec(memory_space=pltpu.SMEM)
    return pl.pallas_call(
        finish_kernel,
        in_specs=[scalars] + [pl.BlockSpec(memory_space=pl.ANY)] * 2 + [whole] * 4,
        out_specs=pl.BlockSpec(memory_space=pl.ANY),
        scratch_shapes=[
            pltpu.VMEM((32, 512, C), jnp.bfloat16),
            pltpu.VMEM((32, 512, C), jnp.bfloat16),
            pltpu.VMEM((32, 512, C), jnp.bfloat16),
            pltpu.SemaphoreType.DMA((2, 32 // GROUP)),
            pltpu.SemaphoreType.DMA((32,)),
        ],
        out_shape=jax.ShapeDtypeStruct((32, 512, C), jnp.bfloat16),
        compiler_params=pltpu.CompilerParams(vmem_limit_bytes=56 * MIB),
    )(routes, conv, centre, face, sums, gain, bias)


def pick_kernel(named_ref, in_ref, out_ref, buffer, sems):
    named = named_ref[:, 3, :]
    lane = lax.broadcasted_iota(jnp.int32, (128, C), 1)
    device = lax.broadcasted_iota(jnp.int32, (128, C), 0)
    source = 2 * (device // 8) + lane
    beside = (lane < 2) & (device % 8 == lax.axis_index("gy"))
    named = jnp.where(beside, named, -1.0)
    reads, writes = [], []
    for i in range(O):
        index = jnp.sum(jnp.where(named == float(i), source, 0))
        reads.append(pltpu.make_async_copy(in_ref.at[index], buffer.at[i], sems.at[0, i]))
        reads[i].start()
        writes.append(pltpu.make_async_copy(buffer.at[i], out_ref.at[i], sems.at[1, i]))
    for read, write in zip(reads, writes):
        read.wait()
        write.start()
    for write in writes:
        write.wait()


def pick(named, received):
    return pl.pallas_call(
        pick_kernel,
        in_specs=[pl.BlockSpec(memory_space=pltpu.VMEM), pl.BlockSpec(memory_space=pl.ANY)],
        out_specs=pl.BlockSpec(memory_space=pl.ANY),
        scratch_shapes=[
            pltpu.VMEM((O, 512, C), jnp.bfloat16),
            pltpu.SemaphoreType.DMA((2, O)),
        ],
        out_shape=jax.ShapeDtypeStruct((O, 512, C), jnp.bfloat16),
    )(named, received)


def swap(spread, axis):
    return lax.all_to_all(spread, axis, 0, 0, tiled=True)


def neighbours(low_block, high_block, axis):
    count = lax.axis_size(axis)
    up = [(i, i + 1) for i in range(count - 1)]
    down = [(j, i) for i, j in up]
    return lax.ppermute(high_block, axis, up), lax.ppermute(low_block, axis, down)


def masked_line(line, columns, x, y):
    column = x % E * 16 + y
    live = jnp.broadcast_to(columns[x // E][:, column : column + 1], (128, C))
    return (line.astype(jnp.float32) * live).astype(jnp.bfloat16)


def line_columns(lines_ref):
    return [jnp.transpose(lines_ref[128 * i : 128 * i + 128, :]) for i in range(2)]


def y_edges_kernel(
    active_ref,
    occupancy_ref,
    features_ref,
    lines_ref,
    first_ref,
    last_ref,
    raw,
    sems,
):
    copies = [
        pltpu.make_async_copy(features_ref.at[:, 15 * i], raw.at[i], sems.at[i]) for i in range(2)
    ]
    for copy in copies:
        copy.start()
    repeat = jnp.where(
        lax.broadcasted_iota(jnp.int32, (16, C), 1) // E
        == lax.broadcasted_iota(jnp.int32, (16, C), 0),
        1.0,
        0.0,
    ).astype(jnp.bfloat16)
    for bx in range(2):
        spread = jnp.dot(
            jnp.where(active_ref[bx] >= 0, 1.0, 0.0).astype(jnp.bfloat16),
            repeat,
            preferred_element_type=jnp.float32,
        )
        for x in range(bx * E, bx * E + E):
            for by in range(2):
                at = x * 16 + by * E
                lines_ref[at : at + E, :] = (
                    occupancy_ref[at : at + E, :].astype(jnp.float32) * spread[by : by + 1, :]
                )
    columns = line_columns(lines_ref)
    for i, ref in enumerate((first_ref, last_ref)):
        copies[i].wait()
        for x in range(16):
            ref[x, 0] = masked_line(raw[i, x], columns, x, 15 * i)


def x_edges_kernel(
    lines_ref, low_ref, high_ref, features_ref, first_ref, last_ref, raw, ends, sems
):
    copies = [
        pltpu.make_async_copy(features_ref.at[15 * i], raw.at[i], sems.at[i]) for i in range(2)
    ]
    for i in range(2):
        for j, ref in enumerate((low_ref, high_ref)):
            copies.append(
                pltpu.make_async_copy(ref.at[15 * i], ends.at[i, j], sems.at[2 + 2 * i + j])
            )
    for copy in copies:
        copy.start()
    columns = line_columns(lines_ref)
    for i, ref in enumerate((first_ref, last_ref)):
        for j in range(2):
            copies[2 + 2 * i + j].wait()
            ref[0, 17 * j : 17 * j + 1] = ends[i, j]
        copies[i].wait()
        for y in range(16):
            ref[0, 1 + y] = masked_line(raw[i, y], columns, 15 * i, y)


def routes_kernel(owner_ref, route_ref, met):
    for i in range(17):
        met[i] = 0
    for i in range(COUNT):
        route_ref[i] = 0 if i < SENT else -1

    def route(i, carry):
        owned = owner_ref[i // 32, i // 16 % 2, i % 16]

        @pl.when(owned >= 0)
        def _():
            owner = owned // 16
            slot = 2 * owner + met[owner]
            rank = met[16]
            met[owner] = met[owner] + 1
            met[16] = rank + 1
            route_ref[rank] = i
            route_ref[SLOTS + rank] = slot
            route_ref[SENT + slot] = owned % 16

        return carry

    lax.fori_loop(0, 64, route, 0)
    route_ref[COUNT] = met[16]
    route_ref[COUNT + 1] = (met[16] + 2 * GROUP - 1) // (2 * GROUP)


def find_routes(owner_map):
    scalars = pl.BlockSpec(memory_space=pltpu.SMEM)
    return pl.pallas_call(
        routes_kernel,
        in_specs=[scalars],
        out_specs=scalars,
        out_shape=jax.ShapeDtypeStruct((COUNT + 2,), jnp.int32),
        scratch_shapes=[pltpu.SMEM((17,), jnp.int32)],
    )(owner_map)


def y_edges(owner_map, occupancy, features):
    whole = pl.BlockSpec(memory_space=pltpu.VMEM)
    return pl.pallas_call(
        y_edges_kernel,
        in_specs=[whole, whole, pl.BlockSpec(memory_space=pl.ANY)],
        out_specs=[whole] * 3,
        out_shape=[jax.ShapeDtypeStruct((256, 128), jnp.float32)]
        + [jax.ShapeDtypeStruct((16, 1, 128, C), jnp.bfloat16)] * 2,
        scratch_shapes=[
            pltpu.VMEM((2, 16, 128, C), jnp.bfloat16),
            pltpu.SemaphoreType.DMA((2,)),
        ],
        compiler_params=pltpu.CompilerParams(vmem_limit_bytes=53 * MIB),
    )(owner_map, occupancy, features)


def x_edges(lines, y_low, y_high, features):
    whole = pl.BlockSpec(memory_space=pltpu.VMEM)
    return pl.pallas_call(
        x_edges_kernel,
        in_specs=[whole] + [pl.BlockSpec(memory_space=pl.ANY)] * 3,
        out_specs=[whole] * 2,
        out_shape=[jax.ShapeDtypeStruct((1, 18, 128, C), jnp.bfloat16)] * 2,
        scratch_shapes=[
            pltpu.VMEM((2, 16, 128, C), jnp.bfloat16),
            pltpu.VMEM((2, 2, 1, 128, C), jnp.bfloat16),
            pltpu.SemaphoreType.DMA((6,)),
        ],
        compiler_params=pltpu.CompilerParams(vmem_limit_bytes=51 * MIB),
    )(lines, y_low, y_high, features)


def on_device(features, occupancy, owner_map, kernel, norm_gain, norm_bias):
    lines, y_first, y_last = y_edges(owner_map, occupancy.reshape(256, 128), features)
    y_low, y_high = neighbours(y_first, y_last, "gy")
    routes = find_routes(owner_map)
    x_low, x_high = neighbours(*x_edges(lines, y_low, y_high, features), "gx")
    conv, centre, partial, sums = convolve(routes, features, y_low, y_high, lines, kernel)
    face_conv, spread = correct_faces(routes, x_low, x_high, partial, sums, lines, kernel)
    totals = swap(spread, ("gx", "gy"))
    result = finish(
        routes, conv, centre, face_conv, totals, norm_gain.reshape(1, C), norm_bias.reshape(1, C)
    )
    received = swap(result.reshape(16, 2, 512, C), "gx").reshape(32, 512, C)
    return pick(totals, received).reshape(O, 1, 512, C)


def solution(mesh):
    in_specs = (P("gx", "gy", None, None), P("gx", "gy", None), P("gx", "gy", None), P(), P(), P())
    out_specs = P("gx", "gy", None, None)
    return jax.shard_map(
        on_device, mesh=mesh, in_specs=in_specs, out_specs=out_specs, check_vma=False
    )
```

```python
import functools

import jax
import jax.numpy as jnp
from jax import lax
from jax.experimental import pallas as pl
from jax.experimental.pallas import tpu as pltpu
from jax.sharding import PartitionSpec as P

O = 16
SLOTS, SENT, COUNT = 48, 96, 128
E = 8
C = 128
GROUP = 4
ABSENT = -1e30
EPSILON = 1e-05
MIB = 1 << 20


def pair_taps(weight_ref, taps_ref, index):
    blank = jnp.zeros((C, C), jnp.bfloat16)
    for a in range(weight_ref.shape[0]):
        for dz in range(3):
            for j in range(4):
                at = (dz * 4 + j) * C
                weight_ref[a, at : at + C, 0:C] = (
                    taps_ref[index(a, dz, j)] if j < 3 else blank
                )
                weight_ref[a, at : at + C, C : 2 * C] = (
                    taps_ref[index(a, dz, j - 1)] if j > 0 else blank
                )


def shifted_scratch():
    return pltpu.VMEM((2, 3, 2, GROUP, 5, 5, 16, C), jnp.bfloat16)


def conv_kernel(
    route_ref,
    features_ref,
    y_low_ref,
    y_high_ref,
    taps_hbm,
    occupied_ref,
    conv_ref,
    centre_ref,
    face_ref,
    sums_ref,
    stage,
    out_sems,
    padded,
    raw,
    margins,
    columns_ref,
    taps_ref,
    weight_ref,
    shifted_a,
    shifted_b,
    total_a,
    total_b,
    sems,
):
    count, steps = route_ref[COUNT], route_ref[COUNT + 1]
    chunks = [
        pltpu.make_async_copy(
            features_ref.at[4 * i : 4 * i + 4], raw.at[i % 2], sems.at[i]
        )
        for i in range(4)
    ]
    lane = lax.broadcasted_iota(jnp.int32, (E, C), 1)

    def place_of(k):
        place = route_ref[k]
        return place // 32, place // 16 % 2, place % 16

    def prepare(group, shifted):
        for b in range(GROUP):
            bx, by, bz = place_of(group * GROUP + b)
            for dz in range(3):
                for xx in range(10):
                    lines = [
                        padded[bx * E + xx, by * E + yy, pl.ds(bz * E + 7 + dz, E), :]
                        for yy in range(10)
                    ]
                    for parity in range(2):
                        for yp in range(5 - parity):
                            pair = jnp.concatenate(
                                [lines[2 * yp + parity], lines[2 * yp + parity + 1]], axis=0
                            )
                            shifted[parity, dz, xx % 2, b, xx // 2, yp] = pair.astype(jnp.bfloat16)

    def multiply(shifted, total):
        for dy in range(3):
            parity, first = dy % 2, dy // 2
            parts = []
            for dz in range(3):
                for j in range(4):
                    part = shifted[
                        parity, dz, j % 2, :, j // 2 : j // 2 + 4, first : first + 4, :, :
                    ]
                    parts.append(part.reshape(GROUP * 256, C))
            product = jnp.dot(
                jnp.concatenate(parts, axis=1),
                weight_ref[dy],
                preferred_element_type=jnp.float32,
            )
            if dy == 0:
                total[...] = product
            else:
                total[...] += product

    def emit(group, shifted, total, parity, at):
        summed = jnp.zeros((E, C), jnp.float32)
        squared = jnp.zeros((E, C), jnp.float32)
        counted = jnp.zeros((E, C), jnp.float32)
        for b in range(GROUP):
            k = group * GROUP + b
            bx, by, bz = place_of(k)
            valid = jnp.where(k < count, 1.0, 0.0)
            near = columns_ref[bx, pl.ds(pl.multiple_of(bz * E, E), E), :] * valid
            near = pltpu.roll(near, C - by * E, axis=1)
            counted += jnp.where(lane % 16 < E, near, 0.0)
            for x in range(E):
                live = jnp.concatenate(
                    [
                        jnp.broadcast_to(near[:, x * 16 + y : x * 16 + y + 1], (E, C))
                        for y in range(E)
                    ],
                    axis=0,
                )
                block = total[b * 256 + (x // 2) * 64 : b * 256 + (x // 2) * 64 + 64,
                              (x % 2) * C : (x % 2 + 1) * C]
                wide = (block * live).astype(jnp.bfloat16).astype(jnp.float32)
                kept = wide
                if x == 0:
                    kept = wide * jnp.where(bx == 0, 0.0, 1.0)
                    face_low = block
                if x == E - 1:
                    kept = wide * jnp.where(bx == 0, 1.0, 0.0)
                    face_ref[k] = jnp.where(bx == 0, face_low, block)
                summed += jnp.sum(kept.reshape(E, E, C), axis=0)
                squared += jnp.sum((kept * kept).reshape(E, E, C), axis=0)
                stage[parity, 0, at + b, x * 64 : (x + 1) * 64, :] = jnp.where(
                    live > 0.5, wide, ABSENT
                ).astype(jnp.bfloat16)
                stage[parity, 1, at + b, x * 64 : (x + 1) * 64, :] = shifted[
                    1, 1, (x + 1) % 2, b, (x + 1) // 2, 0:4
                ].reshape(64, C)
        sums_ref[0] += summed
        sums_ref[1] += squared
        sums_ref[2] += counted

    extra = [
        pltpu.make_async_copy(y_low_ref, margins.at[0], sems.at[4]),
        pltpu.make_async_copy(y_high_ref, margins.at[1], sems.at[5]),
        pltpu.make_async_copy(taps_hbm, taps_ref, sems.at[6]),
    ]
    for copy in [chunks[0], chunks[1]] + extra:
        copy.start()
    edge = jnp.zeros((18, 18, E, C), jnp.float32)
    padded[:, :, 0:8, :] = edge
    padded[:, :, 136:144, :] = edge
    side = jnp.zeros((18, 128, C), jnp.float32)
    padded[0, :, 8:136, :] = side
    padded[17, :, 8:136, :] = side
    sums_ref[...] = jnp.zeros_like(sums_ref)
    for i in range(2):
        columns_ref[i] = jnp.transpose(occupied_ref[128 * i : 128 * i + 128, :])
    for i in range(4):
        chunks[i].wait()
        columns = columns_ref[i // 2]

        def mask_plane(j, carry, i=i, columns=columns):
            near = pltpu.roll(columns, 128 - 64 * (i % 2) - 16 * j, axis=1)
            near = near.astype(jnp.bfloat16)
            for y in range(16):
                live = jnp.broadcast_to(near[:, y : y + 1], (128, C))
                padded[1 + 4 * i + j, 1 + y, 8:136, :] = (
                    (raw[i % 2, j, y] * live).astype(jnp.float32)
                )
            return carry

        lax.fori_loop(0, 4, mask_plane, 0)
        if i < 2:
            chunks[i + 2].start()
    for copy in extra:
        copy.wait()
    for side in range(2):
        padded[1:17, 17 * side, 8:136, :] = (
            margins[side].reshape(16, 128, C).astype(jnp.float32)
        )
    pair_taps(weight_ref, taps_ref, lambda dy, dz, dx: 9 * dx + 3 * dy + dz)

    @pl.when(steps > 0)
    def _():
        prepare(0, shifted_a)

    def outgoing(step):
        rows = pl.ds(step * 2 * GROUP, 2 * GROUP)
        return [
            pltpu.make_async_copy(
                stage.at[step % 2, i], ref.at[rows], out_sems.at[step % 2, i]
            )
            for i, ref in enumerate((conv_ref, centre_ref))
        ]

    def drain(step):
        for copy in outgoing(step):
            copy.wait()

    def pair(step, carry):
        @pl.when(step >= 2)
        def _():
            drain(step - 2)

        prepare(2 * step + 1, shifted_b)
        multiply(shifted_a, total_a)
        emit(2 * step, shifted_a, total_a, step % 2, 0)
        multiply(shifted_b, total_b)
        emit(2 * step + 1, shifted_b, total_b, step % 2, GROUP)
        prepare(2 * step + 2, shifted_a)

        for copy in outgoing(step):
            copy.start()
        return carry

    lax.fori_loop(0, steps, pair, 0)

    @pl.when(steps >= 2)
    def _():
        drain(steps - 2)

    @pl.when(steps >= 1)
    def _():
        drain(steps - 1)


def convolve(routes, features, y_low, y_high, occupied, taps):
    any_spec = pl.BlockSpec(memory_space=pl.ANY)
    whole = pl.BlockSpec(memory_space=pltpu.VMEM)
    scalars = pl.BlockSpec(memory_space=pltpu.SMEM)
    return pl.pallas_call(
        conv_kernel,
        in_specs=[scalars] + [any_spec] * 4 + [whole],
        out_specs=[any_spec] * 2 + [whole] * 2,
        out_shape=[
            jax.ShapeDtypeStruct((32, 512, C), jnp.bfloat16),
            jax.ShapeDtypeStruct((32, 512, C), jnp.bfloat16),
            jax.ShapeDtypeStruct((32, 64, C), jnp.float32),
            jax.ShapeDtypeStruct((3, E, C), jnp.float32),
        ],
        scratch_shapes=[
            pltpu.VMEM((2, 2, 2 * GROUP, 512, C), jnp.bfloat16),
            pltpu.SemaphoreType.DMA((2, 2)),
            pltpu.VMEM((18, 18, 144, C), jnp.float32),
            pltpu.VMEM((2, 4, 16, 128, C), jnp.bfloat16),
            pltpu.VMEM((2, 16, 1, 128, C), jnp.bfloat16),
            pltpu.VMEM((2, C, C), jnp.float32),
            pltpu.VMEM((27, C, C), jnp.bfloat16),
            pltpu.VMEM((3, 12 * C, 2 * C), jnp.bfloat16),
            shifted_scratch(),
            shifted_scratch(),
            pltpu.VMEM((GROUP * 256, 2 * C), jnp.float32),
            pltpu.VMEM((GROUP * 256, 2 * C), jnp.float32),
            pltpu.SemaphoreType.DMA((7,)),
        ],
        compiler_params=pltpu.CompilerParams(vmem_limit_bytes=49 * MIB),
        cost_estimate=pl.CostEstimate(
            flops=2 * 32 * 256 * 4608 * 256, bytes_accessed=30 * MIB, transcendentals=0
        ),
    )(routes, features, y_low, y_high, taps, occupied)


def face_kernel(
    route_ref,
    x_low_ref,
    x_high_ref,
    corner_low_ref,
    corner_high_ref,
    partial_hbm,
    sums_ref,
    occupied_ref,
    taps_ref,
    out_ref,
    norm_ref,
    partial_ref,
    buffer,
    sems,
    columns_ref,
    padded,
    shifted,
    added,
    weight_ref,
):
    count = route_ref[COUNT]
    fetch = pltpu.make_async_copy(partial_hbm, partial_ref, sems.at[8])
    fetch.start()
    pair_taps(weight_ref, taps_ref, lambda side, dz, dy: 18 * side + 3 * dy + dz)
    for i in range(2):
        columns_ref[i] = jnp.transpose(occupied_ref[128 * i : 128 * i + 128, :])
    padded[:, 0:8, :] = jnp.zeros((18, E, C), jnp.float32)
    padded[:, 136:144, :] = jnp.zeros((18, E, C), jnp.float32)
    halos = ((x_low_ref, corner_low_ref), (x_high_ref, corner_high_ref))
    for side, (ref, corner_ref) in enumerate(halos):
        padded[1:17, 8:136, :] = ref[0].astype(jnp.float32)
        padded[0:1, 8:136, :] = corner_ref[0].astype(jnp.float32)
        padded[17:18, 8:136, :] = corner_ref[1].astype(jnp.float32)
        for dz in range(3):
            shifted[dz] = padded[:, 7 + dz : 135 + dz, :].astype(jnp.bfloat16).reshape(
                9, 2, 128, C
            )
        parts = []
        for dz in range(3):
            for j in range(4):
                parts.append(shifted[dz, j // 2 : j // 2 + 8, j % 2].reshape(1024, C))
        added[side] = jnp.dot(
            jnp.concatenate(parts, axis=1), weight_ref[side], preferred_element_type=jnp.float32
        )

    fetch.wait()

    def outgoing(i):
        rows = pl.ds(i * GROUP, GROUP)
        return pltpu.make_async_copy(buffer.at[rows], out_ref.at[rows], sems.at[i])

    def several(i, carry):
        summed, squared = carry
        for b in range(GROUP):
            k = i * GROUP + b
            place = route_ref[k]
            bx, by, bz = place // 32, place // 16 % 2, place % 16
            valid = jnp.where(k < count, 1.0, 0.0)
            near = columns_ref[bx, pl.ds(pl.multiple_of(bz * E, E), E), :] * valid
            near = pltpu.roll(near, C - bx * 112 - by * E, axis=1)
            live = jnp.concatenate(
                [jnp.broadcast_to(near[:, y : y + 1], (E, C)) for y in range(E)], axis=0
            )
            pieces = []
            for y in range(E):
                start = pl.multiple_of((by * 4 + y // 2) * 128 + bz * E, E)
                pieces.append(added[bx, pl.ds(start, E), (y % 2) * C : (y % 2 + 1) * C])
            block = partial_ref[k] + jnp.concatenate(pieces, axis=0)
            wide = (block * live).astype(jnp.bfloat16).astype(jnp.float32)
            wide = jnp.where(live > 0.5, wide, 0.0)
            buffer[k] = jnp.where(live > 0.5, wide, ABSENT).astype(jnp.bfloat16)
            summed += jnp.sum(wide.reshape(E, E, C), axis=0)
            squared += jnp.sum((wide * wide).reshape(E, E, C), axis=0)
        outgoing(i).start()
        return summed, squared

    rounds = (count + GROUP - 1) // GROUP
    summed, squared = lax.fori_loop(0, rounds, several, (sums_ref[0], sums_ref[1]))
    sums = [
        jnp.sum(summed, axis=0, keepdims=True),
        jnp.sum(squared, axis=0, keepdims=True),
        jnp.broadcast_to(jnp.sum(sums_ref[2]), (1, C)),
    ]
    first_lane = lax.broadcasted_iota(jnp.int32, (1, C), 1) == 0
    for i in range(16):
        pair = jnp.where(first_lane, route_ref[SENT + 2 * i], route_ref[SENT + 2 * i + 1])
        table = jnp.concatenate(sums + [pair.astype(jnp.float32)], axis=0)
        norm_ref[8 * i : 8 * i + 8] = jnp.broadcast_to(table[None], (8, 4, C))

    def drain(i, carry):
        outgoing(i).wait()
        return carry

    lax.fori_loop(0, rounds, drain, 0)


def correct_faces(routes, x_low, x_high, corner_low, corner_high, partial, sums, occupied, taps):
    any_spec = pl.BlockSpec(memory_space=pl.ANY)
    whole = pl.BlockSpec(memory_space=pltpu.VMEM)
    scalars = pl.BlockSpec(memory_space=pltpu.SMEM)
    return pl.pallas_call(
        face_kernel,
        in_specs=[scalars] + [whole] * 4 + [any_spec] + [whole] * 3,
        out_specs=[any_spec, whole],
        out_shape=[
            jax.ShapeDtypeStruct((32, 64, C), jnp.bfloat16),
            jax.ShapeDtypeStruct((128, 4, C), jnp.float32),
        ],
        scratch_shapes=[
            pltpu.VMEM((32, 64, C), jnp.float32),
            pltpu.VMEM((32, 64, C), jnp.bfloat16),
            pltpu.SemaphoreType.DMA((9,)),
            pltpu.VMEM((2, C, C), jnp.float32),
            pltpu.VMEM((18, 144, C), jnp.float32),
            pltpu.VMEM((3, 9, 2, 128, C), jnp.bfloat16),
            pltpu.VMEM((2, 1024, 2 * C), jnp.float32),
            pltpu.VMEM((2, 12 * C, 2 * C), jnp.bfloat16),
        ],
        compiler_params=pltpu.CompilerParams(vmem_limit_bytes=32 * MIB),
    )(routes, x_low, x_high, corner_low, corner_high, partial, sums, occupied, taps)


def finish_kernel(
    route_ref,
    conv_hbm,
    centre_hbm,
    face_ref,
    sums_ref,
    gain_ref,
    bias_ref,
    out_ref,
    conv_ref,
    centre_ref,
    buffer,
    in_sems,
    sems,
):
    count = route_ref[COUNT]

    def incoming(group):
        rows = pl.ds(group * GROUP, GROUP)
        return [
            pltpu.make_async_copy(hbm.at[rows], ref.at[rows], in_sems.at[i, group])
            for i, (hbm, ref) in enumerate(((conv_hbm, conv_ref), (centre_hbm, centre_ref)))
        ]

    for group in range(32 // GROUP):

        @pl.when(group * GROUP < count)
        def _():
            for each in incoming(group):
                each.start()

    sums = jnp.sum(sums_ref[...], axis=0)
    mean = sums[0:1] / sums[2:3]
    variance = sums[1:2] / sums[2:3] - mean * mean
    factor = 0.5 * (gain_ref[...] / jnp.sqrt(variance + EPSILON))
    bias = 0.5 * bias_ref[...]

    def copy(k):
        return pltpu.make_async_copy(buffer.at[k], out_ref.at[route_ref[SLOTS + k]], sems.at[k])

    def one(k, carry):
        @pl.when(k % GROUP == 0)
        def _():
            for each in incoming(k // GROUP):
                each.wait()

        bx = route_ref[k] // 32
        for x in range(E):
            conv = conv_ref[k, x * 64 : (x + 1) * 64, :].astype(jnp.float32)
            if x in (0, E - 1):
                own = face_ref[k].astype(jnp.float32)
                conv = jnp.where(bx == (0 if x == 0 else 1), own, conv)
            halved = factor * (conv - mean) + bias
            silu = halved + halved * jnp.tanh(halved)
            silu = jnp.where(conv > 0.5 * ABSENT, silu, 0.0)
            centre = centre_ref[k, x * 64 : (x + 1) * 64, :].astype(jnp.float32)
            buffer[k, x * 64 : (x + 1) * 64, :] = (centre + silu).astype(jnp.bfloat16)
        copy(k).start()
        return carry

    def drain(k, carry):
        copy(k).wait()
        return carry

    lax.fori_loop(0, count, one, 0)
    lax.fori_loop(0, count, drain, 0)


def finish(routes, conv, centre, face, sums, gain, bias):
    whole = pl.BlockSpec(memory_space=pltpu.VMEM)
    scalars = pl.BlockSpec(memory_space=pltpu.SMEM)
    return pl.pallas_call(
        finish_kernel,
        in_specs=[scalars] + [pl.BlockSpec(memory_space=pl.ANY)] * 2 + [whole] * 4,
        out_specs=pl.BlockSpec(memory_space=pl.ANY),
        scratch_shapes=[
            pltpu.VMEM((32, 512, C), jnp.bfloat16),
            pltpu.VMEM((32, 512, C), jnp.bfloat16),
            pltpu.VMEM((32, 512, C), jnp.bfloat16),
            pltpu.SemaphoreType.DMA((2, 32 // GROUP)),
            pltpu.SemaphoreType.DMA((32,)),
        ],
        out_shape=jax.ShapeDtypeStruct((32, 512, C), jnp.bfloat16),
        compiler_params=pltpu.CompilerParams(vmem_limit_bytes=56 * MIB),
    )(routes, conv, centre, face, sums, gain, bias)


def pick_kernel(named_ref, in_ref, out_ref, buffer, sems):
    named = named_ref[:, 3, :]
    lane = lax.broadcasted_iota(jnp.int32, (128, C), 1)
    device = lax.broadcasted_iota(jnp.int32, (128, C), 0)
    source = 2 * (device // 8) + lane
    beside = (lane < 2) & (device % 8 == lax.axis_index("gy"))
    named = jnp.where(beside, named, -1.0)
    reads, writes = [], []
    for i in range(O):
        index = jnp.sum(jnp.where(named == float(i), source, 0))
        reads.append(pltpu.make_async_copy(in_ref.at[index], buffer.at[i], sems.at[0, i]))
        reads[i].start()
        writes.append(pltpu.make_async_copy(buffer.at[i], out_ref.at[i], sems.at[1, i]))
    for read, write in zip(reads, writes):
        read.wait()
        write.start()
    for write in writes:
        write.wait()


def pick(named, received):
    return pl.pallas_call(
        pick_kernel,
        in_specs=[pl.BlockSpec(memory_space=pltpu.VMEM), pl.BlockSpec(memory_space=pl.ANY)],
        out_specs=pl.BlockSpec(memory_space=pl.ANY),
        scratch_shapes=[
            pltpu.VMEM((O, 512, C), jnp.bfloat16),
            pltpu.SemaphoreType.DMA((2, O)),
        ],
        out_shape=jax.ShapeDtypeStruct((O, 512, C), jnp.bfloat16),
    )(named, received)


def swap(spread, axis):
    return lax.all_to_all(spread, axis, 0, 0, tiled=True)


def neighbours(low_block, high_block, axis):
    count = lax.axis_size(axis)
    up = [(i, i + 1) for i in range(count - 1)]
    down = [(j, i) for i, j in up]
    return lax.ppermute(high_block, axis, up), lax.ppermute(low_block, axis, down)


def masked_line(line, columns, x, y):
    column = x % E * 16 + y
    live = jnp.broadcast_to(columns[x // E][:, column : column + 1], (128, C))
    return (line.astype(jnp.float32) * live).astype(jnp.bfloat16)


def line_columns(lines_ref):
    return [jnp.transpose(lines_ref[128 * i : 128 * i + 128, :]) for i in range(2)]


def edges_kernel(
    active_ref,
    occupancy_ref,
    features_ref,
    lines_ref,
    y_first_ref,
    y_last_ref,
    x_first_ref,
    x_last_ref,
    raw,
    sems,
):
    copies = [
        pltpu.make_async_copy(features_ref.at[:, 15 * i], raw.at[i], sems.at[i]) for i in range(2)
    ] + [
        pltpu.make_async_copy(features_ref.at[15 * i], raw.at[2 + i], sems.at[2 + i])
        for i in range(2)
    ]
    for copy in copies:
        copy.start()
    repeat = jnp.where(
        lax.broadcasted_iota(jnp.int32, (16, C), 1) // E
        == lax.broadcasted_iota(jnp.int32, (16, C), 0),
        1.0,
        0.0,
    ).astype(jnp.bfloat16)
    for bx in range(2):
        spread = jnp.dot(
            jnp.where(active_ref[bx] >= 0, 1.0, 0.0).astype(jnp.bfloat16),
            repeat,
            preferred_element_type=jnp.float32,
        )
        for x in range(bx * E, bx * E + E):
            for by in range(2):
                at = x * 16 + by * E
                lines_ref[at : at + E, :] = (
                    occupancy_ref[at : at + E, :].astype(jnp.float32) * spread[by : by + 1, :]
                )
    columns = line_columns(lines_ref)
    for i, ref in enumerate((y_first_ref, y_last_ref)):
        copies[i].wait()
        for x in range(16):
            ref[x, 0] = masked_line(raw[i, x], columns, x, 15 * i)
    for i, ref in enumerate((x_first_ref, x_last_ref)):
        copies[2 + i].wait()
        for y in range(16):
            ref[0, y] = masked_line(raw[2 + i, y], columns, 15 * i, y)


def corners_kernel(low_ref, high_ref, first_ref, last_ref, sems):
    copies = [
        pltpu.make_async_copy(ref.at[15 * i], out.at[j], sems.at[i, j])
        for i, out in enumerate((first_ref, last_ref))
        for j, ref in enumerate((low_ref, high_ref))
    ]
    for copy in copies:
        copy.start()
    for copy in copies:
        copy.wait()


def corners(y_low, y_high):
    return pl.pallas_call(
        corners_kernel,
        in_specs=[pl.BlockSpec(memory_space=pl.ANY)] * 2,
        out_specs=[pl.BlockSpec(memory_space=pltpu.VMEM)] * 2,
        out_shape=[jax.ShapeDtypeStruct((2, 1, 128, C), jnp.bfloat16)] * 2,
        scratch_shapes=[pltpu.SemaphoreType.DMA((2, 2))],
    )(y_low, y_high)


def routes_kernel(owner_ref, route_ref, met):
    for i in range(17):
        met[i] = 0
    for i in range(COUNT):
        route_ref[i] = 0 if i < SENT else -1

    def route(i, carry):
        owned = owner_ref[i // 32, i // 16 % 2, i % 16]

        @pl.when(owned >= 0)
        def _():
            owner = owned // 16
            slot = 2 * owner + met[owner]
            rank = met[16]
            met[owner] = met[owner] + 1
            met[16] = rank + 1
            route_ref[rank] = i
            route_ref[SLOTS + rank] = slot
            route_ref[SENT + slot] = owned % 16

        return carry

    lax.fori_loop(0, 64, route, 0)
    route_ref[COUNT] = met[16]
    route_ref[COUNT + 1] = (met[16] + 2 * GROUP - 1) // (2 * GROUP)


def find_routes(owner_map):
    scalars = pl.BlockSpec(memory_space=pltpu.SMEM)
    return pl.pallas_call(
        routes_kernel,
        in_specs=[scalars],
        out_specs=scalars,
        out_shape=jax.ShapeDtypeStruct((COUNT + 2,), jnp.int32),
        scratch_shapes=[pltpu.SMEM((17,), jnp.int32)],
    )(owner_map)


def edges(owner_map, occupancy, features):
    whole = pl.BlockSpec(memory_space=pltpu.VMEM)
    return pl.pallas_call(
        edges_kernel,
        in_specs=[whole, whole, pl.BlockSpec(memory_space=pl.ANY)],
        out_specs=[whole] * 5,
        out_shape=[jax.ShapeDtypeStruct((256, 128), jnp.float32)]
        + [jax.ShapeDtypeStruct((16, 1, 128, C), jnp.bfloat16)] * 2
        + [jax.ShapeDtypeStruct((1, 16, 128, C), jnp.bfloat16)] * 2,
        scratch_shapes=[
            pltpu.VMEM((4, 16, 128, C), jnp.bfloat16),
            pltpu.SemaphoreType.DMA((4,)),
        ],
        compiler_params=pltpu.CompilerParams(vmem_limit_bytes=53 * MIB),
    )(owner_map, occupancy, features)


def on_device(features, occupancy, owner_map, kernel, norm_gain, norm_bias):
    lines, y_first, y_last, x_first, x_last = edges(
        owner_map, occupancy.reshape(256, 128), features
    )
    y_low, y_high = neighbours(y_first, y_last, "gy")
    x_low, x_high = neighbours(x_first, x_last, "gx")
    routes = find_routes(owner_map)
    corner_low, corner_high = neighbours(*corners(y_low, y_high), "gx")
    conv, centre, partial, sums = convolve(routes, features, y_low, y_high, lines, kernel)
    face_conv, spread = correct_faces(
        routes, x_low, x_high, corner_low, corner_high, partial, sums, lines, kernel
    )
    totals = swap(spread, ("gx", "gy"))
    result = finish(
        routes, conv, centre, face_conv, totals, norm_gain.reshape(1, C), norm_bias.reshape(1, C)
    )
    received = swap(result.reshape(16, 2, 512, C), "gx").reshape(32, 512, C)
    return pick(totals, received).reshape(O, 1, 512, C)


def solution(mesh):
    in_specs = (P("gx", "gy", None, None), P("gx", "gy", None), P("gx", "gy", None), P(), P(), P())
    out_specs = P("gx", "gy", None, None)
    return jax.shard_map(
        on_device, mesh=mesh, in_specs=in_specs, out_specs=out_specs, check_vma=False
    )
```

```python
import functools

import jax
import jax.numpy as jnp
from jax import lax
from jax.experimental import pallas as pl
from jax.experimental.pallas import tpu as pltpu
from jax.sharding import PartitionSpec as P

O = 16
SLOTS, SENT, COUNT = 48, 96, 128
E = 8
C = 128
GROUP = 4
ABSENT = -1e30
EPSILON = 1e-05
MIB = 1 << 20


def pair_taps(weight_ref, taps_ref, index):
    blank = jnp.zeros((C, C), jnp.bfloat16)
    for a in range(weight_ref.shape[0]):
        for dz in range(3):
            for j in range(4):
                at = (dz * 4 + j) * C
                weight_ref[a, at : at + C, 0:C] = (
                    taps_ref[index(a, dz, j)] if j < 3 else blank
                )
                weight_ref[a, at : at + C, C : 2 * C] = (
                    taps_ref[index(a, dz, j - 1)] if j > 0 else blank
                )


def shifted_scratch():
    return pltpu.VMEM((2, 3, 2, GROUP, 5, 5, 16, C), jnp.bfloat16)


def conv_kernel(
    route_ref,
    features_ref,
    y_low_ref,
    y_high_ref,
    taps_hbm,
    occupied_ref,
    conv_ref,
    centre_ref,
    face_ref,
    sums_ref,
    stage,
    out_sems,
    padded,
    raw,
    margins,
    columns_ref,
    taps_ref,
    weight_ref,
    shifted_a,
    shifted_b,
    total_a,
    total_b,
    sems,
):
    count, steps = route_ref[COUNT], route_ref[COUNT + 1]
    chunks = [
        pltpu.make_async_copy(
            features_ref.at[4 * i : 4 * i + 4], raw.at[i % 2], sems.at[i]
        )
        for i in range(4)
    ]
    lane = lax.broadcasted_iota(jnp.int32, (E, C), 1)

    def place_of(k):
        place = route_ref[k]
        return place // 32, place // 16 % 2, place % 16

    def prepare(group, shifted):
        for b in range(GROUP):
            bx, by, bz = place_of(group * GROUP + b)
            for dz in range(3):
                for xx in range(10):
                    lines = [
                        padded[bx * E + xx, by * E + yy, pl.ds(bz * E + 7 + dz, E), :]
                        for yy in range(10)
                    ]
                    for parity in range(2):
                        for yp in range(5 - parity):
                            pair = jnp.concatenate(
                                [lines[2 * yp + parity], lines[2 * yp + parity + 1]], axis=0
                            )
                            shifted[parity, dz, xx % 2, b, xx // 2, yp] = pair.astype(jnp.bfloat16)

    def multiply(shifted, total):
        for dy in range(3):
            parity, first = dy % 2, dy // 2
            parts = []
            for dz in range(3):
                for j in range(4):
                    part = shifted[
                        parity, dz, j % 2, :, j // 2 : j // 2 + 4, first : first + 4, :, :
                    ]
                    parts.append(part.reshape(GROUP * 256, C))
            product = jnp.dot(
                jnp.concatenate(parts, axis=1),
                weight_ref[dy],
                preferred_element_type=jnp.float32,
            )
            if dy == 0:
                total[...] = product
            else:
                total[...] += product

    def emit(group, shifted, total, parity, at):
        summed = jnp.zeros((E, C), jnp.float32)
        squared = jnp.zeros((E, C), jnp.float32)
        counted = jnp.zeros((E, C), jnp.float32)
        for b in range(GROUP):
            k = group * GROUP + b
            bx, by, bz = place_of(k)
            valid = jnp.where(k < count, 1.0, 0.0)
            near = columns_ref[bx, pl.ds(pl.multiple_of(bz * E, E), E), :] * valid
            near = pltpu.roll(near, C - by * E, axis=1)
            counted += jnp.where(lane % 16 < E, near, 0.0)
            for x in range(E):
                live = jnp.concatenate(
                    [
                        jnp.broadcast_to(near[:, x * 16 + y : x * 16 + y + 1], (E, C))
                        for y in range(E)
                    ],
                    axis=0,
                )
                block = total[b * 256 + (x // 2) * 64 : b * 256 + (x // 2) * 64 + 64,
                              (x % 2) * C : (x % 2 + 1) * C]
                wide = (block * live).astype(jnp.bfloat16).astype(jnp.float32)
                kept = wide
                if x == 0:
                    kept = wide * jnp.where(bx == 0, 0.0, 1.0)
                    face_low = block
                if x == E - 1:
                    kept = wide * jnp.where(bx == 0, 1.0, 0.0)
                    face_ref[k] = jnp.where(bx == 0, face_low, block)
                summed += jnp.sum(kept.reshape(E, E, C), axis=0)
                squared += jnp.sum((kept * kept).reshape(E, E, C), axis=0)
                stage[parity, 0, at + b, x * 64 : (x + 1) * 64, :] = jnp.where(
                    live > 0.5, wide, ABSENT
                ).astype(jnp.bfloat16)
                stage[parity, 1, at + b, x * 64 : (x + 1) * 64, :] = shifted[
                    1, 1, (x + 1) % 2, b, (x + 1) // 2, 0:4
                ].reshape(64, C)
        sums_ref[0] += summed
        sums_ref[1] += squared
        sums_ref[2] += counted

    extra = [
        pltpu.make_async_copy(y_low_ref, margins.at[0], sems.at[4]),
        pltpu.make_async_copy(y_high_ref, margins.at[1], sems.at[5]),
        pltpu.make_async_copy(taps_hbm, taps_ref, sems.at[6]),
    ]
    for copy in [chunks[0], chunks[1]] + extra:
        copy.start()
    edge = jnp.zeros((18, 18, E, C), jnp.float32)
    padded[:, :, 0:8, :] = edge
    padded[:, :, 136:144, :] = edge
    side = jnp.zeros((18, 128, C), jnp.float32)
    padded[0, :, 8:136, :] = side
    padded[17, :, 8:136, :] = side
    sums_ref[...] = jnp.zeros_like(sums_ref)
    for i in range(2):
        columns_ref[i] = jnp.transpose(occupied_ref[128 * i : 128 * i + 128, :])
    for i in range(4):
        chunks[i].wait()
        columns = columns_ref[i // 2]

        def mask_plane(j, carry, i=i, columns=columns):
            near = pltpu.roll(columns, 128 - 64 * (i % 2) - 16 * j, axis=1)
            near = near.astype(jnp.bfloat16)
            for y in range(16):
                live = jnp.broadcast_to(near[:, y : y + 1], (128, C))
                padded[1 + 4 * i + j, 1 + y, 8:136, :] = (
                    (raw[i % 2, j, y] * live).astype(jnp.float32)
                )
            return carry

        lax.fori_loop(0, 4, mask_plane, 0)
        if i < 2:
            chunks[i + 2].start()
    for copy in extra:
        copy.wait()
    for side in range(2):
        padded[1:17, 17 * side, 8:136, :] = (
            margins[side].reshape(16, 128, C).astype(jnp.float32)
        )
    pair_taps(weight_ref, taps_ref, lambda dy, dz, dx: 9 * dx + 3 * dy + dz)

    @pl.when(steps > 0)
    def _():
        prepare(0, shifted_a)

    def outgoing(step):
        rows = pl.ds(step * 2 * GROUP, 2 * GROUP)
        return [
            pltpu.make_async_copy(
                stage.at[step % 2, i], ref.at[rows], out_sems.at[step % 2, i]
            )
            for i, ref in enumerate((conv_ref, centre_ref))
        ]

    def drain(step):
        for copy in outgoing(step):
            copy.wait()

    def pair(step, carry):
        @pl.when(step >= 2)
        def _():
            drain(step - 2)

        prepare(2 * step + 1, shifted_b)
        multiply(shifted_a, total_a)
        emit(2 * step, shifted_a, total_a, step % 2, 0)
        multiply(shifted_b, total_b)
        emit(2 * step + 1, shifted_b, total_b, step % 2, GROUP)
        prepare(2 * step + 2, shifted_a)

        for copy in outgoing(step):
            copy.start()
        return carry

    lax.fori_loop(0, steps, pair, 0)

    @pl.when(steps >= 2)
    def _():
        drain(steps - 2)

    @pl.when(steps >= 1)
    def _():
        drain(steps - 1)


def convolve(routes, features, y_low, y_high, occupied, taps):
    any_spec = pl.BlockSpec(memory_space=pl.ANY)
    whole = pl.BlockSpec(memory_space=pltpu.VMEM)
    scalars = pl.BlockSpec(memory_space=pltpu.SMEM)
    return pl.pallas_call(
        conv_kernel,
        in_specs=[scalars] + [any_spec] * 4 + [whole],
        out_specs=[any_spec] * 2 + [whole] * 2,
        out_shape=[
            jax.ShapeDtypeStruct((32, 512, C), jnp.bfloat16),
            jax.ShapeDtypeStruct((32, 512, C), jnp.bfloat16),
            jax.ShapeDtypeStruct((32, 64, C), jnp.float32),
            jax.ShapeDtypeStruct((3, E, C), jnp.float32),
        ],
        scratch_shapes=[
            pltpu.VMEM((2, 2, 2 * GROUP, 512, C), jnp.bfloat16),
            pltpu.SemaphoreType.DMA((2, 2)),
            pltpu.VMEM((18, 18, 144, C), jnp.float32),
            pltpu.VMEM((2, 4, 16, 128, C), jnp.bfloat16),
            pltpu.VMEM((2, 16, 1, 128, C), jnp.bfloat16),
            pltpu.VMEM((2, C, C), jnp.float32),
            pltpu.VMEM((27, C, C), jnp.bfloat16),
            pltpu.VMEM((3, 12 * C, 2 * C), jnp.bfloat16),
            shifted_scratch(),
            shifted_scratch(),
            pltpu.VMEM((GROUP * 256, 2 * C), jnp.float32),
            pltpu.VMEM((GROUP * 256, 2 * C), jnp.float32),
            pltpu.SemaphoreType.DMA((7,)),
        ],
        compiler_params=pltpu.CompilerParams(vmem_limit_bytes=49 * MIB),
        cost_estimate=pl.CostEstimate(
            flops=2 * 32 * 256 * 4608 * 256, bytes_accessed=30 * MIB, transcendentals=0
        ),
    )(routes, features, y_low, y_high, taps, occupied)


def face_kernel(
    route_ref,
    x_low_ref,
    x_high_ref,
    partial_hbm,
    sums_ref,
    occupied_ref,
    taps_ref,
    out_ref,
    norm_ref,
    partial_ref,
    buffer,
    sems,
    columns_ref,
    padded,
    shifted,
    added,
    weight_ref,
):
    count = route_ref[COUNT]
    fetch = pltpu.make_async_copy(partial_hbm, partial_ref, sems.at[8])
    fetch.start()
    pair_taps(weight_ref, taps_ref, lambda side, dz, dy: 18 * side + 3 * dy + dz)
    for i in range(2):
        columns_ref[i] = jnp.transpose(occupied_ref[128 * i : 128 * i + 128, :])
    padded[:, 0:8, :] = jnp.zeros((18, E, C), jnp.float32)
    padded[:, 136:144, :] = jnp.zeros((18, E, C), jnp.float32)
    for side, ref in enumerate((x_low_ref, x_high_ref)):
        padded[:, 8:136, :] = ref[0].astype(jnp.float32)
        for dz in range(3):
            shifted[dz] = padded[:, 7 + dz : 135 + dz, :].astype(jnp.bfloat16).reshape(
                9, 2, 128, C
            )
        parts = []
        for dz in range(3):
            for j in range(4):
                parts.append(shifted[dz, j // 2 : j // 2 + 8, j % 2].reshape(1024, C))
        added[side] = jnp.dot(
            jnp.concatenate(parts, axis=1), weight_ref[side], preferred_element_type=jnp.float32
        )

    fetch.wait()

    def outgoing(i):
        rows = pl.ds(i * GROUP, GROUP)
        return pltpu.make_async_copy(buffer.at[rows], out_ref.at[rows], sems.at[i])

    def several(i, carry):
        summed, squared = carry
        for b in range(GROUP):
            k = i * GROUP + b
            place = route_ref[k]
            bx, by, bz = place // 32, place // 16 % 2, place % 16
            valid = jnp.where(k < count, 1.0, 0.0)
            near = columns_ref[bx, pl.ds(pl.multiple_of(bz * E, E), E), :] * valid
            near = pltpu.roll(near, C - bx * 112 - by * E, axis=1)
            live = jnp.concatenate(
                [jnp.broadcast_to(near[:, y : y + 1], (E, C)) for y in range(E)], axis=0
            )
            pieces = []
            for y in range(E):
                start = pl.multiple_of((by * 4 + y // 2) * 128 + bz * E, E)
                pieces.append(added[bx, pl.ds(start, E), (y % 2) * C : (y % 2 + 1) * C])
            block = partial_ref[k] + jnp.concatenate(pieces, axis=0)
            wide = (block * live).astype(jnp.bfloat16).astype(jnp.float32)
            wide = jnp.where(live > 0.5, wide, 0.0)
            buffer[k] = jnp.where(live > 0.5, wide, ABSENT).astype(jnp.bfloat16)
            summed += jnp.sum(wide.reshape(E, E, C), axis=0)
            squared += jnp.sum((wide * wide).reshape(E, E, C), axis=0)
        outgoing(i).start()
        return summed, squared

    rounds = (count + GROUP - 1) // GROUP
    summed, squared = lax.fori_loop(0, rounds, several, (sums_ref[0], sums_ref[1]))
    sums = [
        jnp.sum(summed, axis=0, keepdims=True),
        jnp.sum(squared, axis=0, keepdims=True),
        jnp.broadcast_to(jnp.sum(sums_ref[2]), (1, C)),
    ]
    first_lane = lax.broadcasted_iota(jnp.int32, (1, C), 1) == 0
    for i in range(16):
        pair = jnp.where(first_lane, route_ref[SENT + 2 * i], route_ref[SENT + 2 * i + 1])
        table = jnp.concatenate(sums + [pair.astype(jnp.float32)], axis=0)
        norm_ref[8 * i : 8 * i + 8] = jnp.broadcast_to(table[None], (8, 4, C))

    def drain(i, carry):
        outgoing(i).wait()
        return carry

    lax.fori_loop(0, rounds, drain, 0)


def correct_faces(routes, x_low, x_high, partial, sums, occupied, taps):
    any_spec = pl.BlockSpec(memory_space=pl.ANY)
    whole = pl.BlockSpec(memory_space=pltpu.VMEM)
    scalars = pl.BlockSpec(memory_space=pltpu.SMEM)
    return pl.pallas_call(
        face_kernel,
        in_specs=[scalars, whole, whole, any_spec] + [whole] * 3,
        out_specs=[any_spec, whole],
        out_shape=[
            jax.ShapeDtypeStruct((32, 64, C), jnp.bfloat16),
            jax.ShapeDtypeStruct((128, 4, C), jnp.float32),
        ],
        scratch_shapes=[
            pltpu.VMEM((32, 64, C), jnp.float32),
            pltpu.VMEM((32, 64, C), jnp.bfloat16),
            pltpu.SemaphoreType.DMA((9,)),
            pltpu.VMEM((2, C, C), jnp.float32),
            pltpu.VMEM((18, 144, C), jnp.float32),
            pltpu.VMEM((3, 9, 2, 128, C), jnp.bfloat16),
            pltpu.VMEM((2, 1024, 2 * C), jnp.float32),
            pltpu.VMEM((2, 12 * C, 2 * C), jnp.bfloat16),
        ],
        compiler_params=pltpu.CompilerParams(vmem_limit_bytes=32 * MIB),
    )(routes, x_low, x_high, partial, sums, occupied, taps)


def finish_kernel(
    route_ref,
    conv_hbm,
    centre_hbm,
    face_ref,
    sums_ref,
    gain_ref,
    bias_ref,
    out_ref,
    conv_ref,
    centre_ref,
    buffer,
    in_sems,
    sems,
):
    count = route_ref[COUNT]

    def incoming(group):
        rows = pl.ds(group * GROUP, GROUP)
        return [
            pltpu.make_async_copy(hbm.at[rows], ref.at[rows], in_sems.at[i, group])
            for i, (hbm, ref) in enumerate(((conv_hbm, conv_ref), (centre_hbm, centre_ref)))
        ]

    for group in range(32 // GROUP):

        @pl.when(group * GROUP < count)
        def _():
            for each in incoming(group):
                each.start()

    sums = jnp.sum(sums_ref[...], axis=0)
    mean = sums[0:1] / sums[2:3]
    variance = sums[1:2] / sums[2:3] - mean * mean
    factor = 0.5 * (gain_ref[...] / jnp.sqrt(variance + EPSILON))
    bias = 0.5 * bias_ref[...]

    def copy(k):
        return pltpu.make_async_copy(buffer.at[k], out_ref.at[route_ref[SLOTS + k]], sems.at[k])

    def one(k, carry):
        @pl.when(k % GROUP == 0)
        def _():
            for each in incoming(k // GROUP):
                each.wait()

        bx = route_ref[k] // 32
        for x in range(E):
            conv = conv_ref[k, x * 64 : (x + 1) * 64, :].astype(jnp.float32)
            if x in (0, E - 1):
                own = face_ref[k].astype(jnp.float32)
                conv = jnp.where(bx == (0 if x == 0 else 1), own, conv)
            halved = factor * (conv - mean) + bias
            silu = halved + halved * jnp.tanh(halved)
            silu = jnp.where(conv > 0.5 * ABSENT, silu, 0.0)
            centre = centre_ref[k, x * 64 : (x + 1) * 64, :].astype(jnp.float32)
            buffer[k, x * 64 : (x + 1) * 64, :] = (centre + silu).astype(jnp.bfloat16)
        copy(k).start()
        return carry

    def drain(k, carry):
        copy(k).wait()
        return carry

    lax.fori_loop(0, count, one, 0)
    lax.fori_loop(0, count, drain, 0)


def finish(routes, conv, centre, face, sums, gain, bias):
    whole = pl.BlockSpec(memory_space=pltpu.VMEM)
    scalars = pl.BlockSpec(memory_space=pltpu.SMEM)
    return pl.pallas_call(
        finish_kernel,
        in_specs=[scalars] + [pl.BlockSpec(memory_space=pl.ANY)] * 2 + [whole] * 4,
        out_specs=pl.BlockSpec(memory_space=pl.ANY),
        scratch_shapes=[
            pltpu.VMEM((32, 512, C), jnp.bfloat16),
            pltpu.VMEM((32, 512, C), jnp.bfloat16),
            pltpu.VMEM((32, 512, C), jnp.bfloat16),
            pltpu.SemaphoreType.DMA((2, 32 // GROUP)),
            pltpu.SemaphoreType.DMA((32,)),
        ],
        out_shape=jax.ShapeDtypeStruct((32, 512, C), jnp.bfloat16),
        compiler_params=pltpu.CompilerParams(vmem_limit_bytes=56 * MIB),
    )(routes, conv, centre, face, sums, gain, bias)


def pick_kernel(named_ref, in_ref, out_ref, buffer, sems):
    named = named_ref[:, 3, :]
    lane = lax.broadcasted_iota(jnp.int32, (128, C), 1)
    device = lax.broadcasted_iota(jnp.int32, (128, C), 0)
    source = 2 * (device // 8) + lane
    beside = (lane < 2) & (device % 8 == lax.axis_index("gy"))
    named = jnp.where(beside, named, -1.0)
    reads, writes = [], []
    for i in range(O):
        index = jnp.sum(jnp.where(named == float(i), source, 0))
        reads.append(pltpu.make_async_copy(in_ref.at[index], buffer.at[i], sems.at[0, i]))
        reads[i].start()
        writes.append(pltpu.make_async_copy(buffer.at[i], out_ref.at[i], sems.at[1, i]))
    for read, write in zip(reads, writes):
        read.wait()
        write.start()
    for write in writes:
        write.wait()


def pick(named, received):
    return pl.pallas_call(
        pick_kernel,
        in_specs=[pl.BlockSpec(memory_space=pltpu.VMEM), pl.BlockSpec(memory_space=pl.ANY)],
        out_specs=pl.BlockSpec(memory_space=pl.ANY),
        scratch_shapes=[
            pltpu.VMEM((O, 512, C), jnp.bfloat16),
            pltpu.SemaphoreType.DMA((2, O)),
        ],
        out_shape=jax.ShapeDtypeStruct((O, 512, C), jnp.bfloat16),
    )(named, received)


def swap(spread, axis):
    return lax.all_to_all(spread, axis, 0, 0, tiled=True)


def neighbours(low_block, high_block, axis):
    count = lax.axis_size(axis)
    up = [(i, i + 1) for i in range(count - 1)]
    down = [(j, i) for i, j in up]
    return lax.ppermute(high_block, axis, up), lax.ppermute(low_block, axis, down)


def masked_line(line, columns, x, y):
    column = x % E * 16 + y
    live = jnp.broadcast_to(columns[x // E][:, column : column + 1], (128, C))
    return (line.astype(jnp.float32) * live).astype(jnp.bfloat16)


def line_columns(lines_ref):
    return [jnp.transpose(lines_ref[128 * i : 128 * i + 128, :]) for i in range(2)]


def y_edges_kernel(
    active_ref,
    occupancy_ref,
    features_ref,
    lines_ref,
    first_ref,
    last_ref,
    raw,
    sems,
):
    copies = [
        pltpu.make_async_copy(features_ref.at[:, 15 * i], raw.at[i], sems.at[i]) for i in range(2)
    ]
    for copy in copies:
        copy.start()
    repeat = jnp.where(
        lax.broadcasted_iota(jnp.int32, (16, C), 1) // E
        == lax.broadcasted_iota(jnp.int32, (16, C), 0),
        1.0,
        0.0,
    ).astype(jnp.bfloat16)
    for bx in range(2):
        spread = jnp.dot(
            jnp.where(active_ref[bx] >= 0, 1.0, 0.0).astype(jnp.bfloat16),
            repeat,
            preferred_element_type=jnp.float32,
        )
        for x in range(bx * E, bx * E + E):
            for by in range(2):
                at = x * 16 + by * E
                lines_ref[at : at + E, :] = (
                    occupancy_ref[at : at + E, :].astype(jnp.float32) * spread[by : by + 1, :]
                )
    columns = line_columns(lines_ref)
    for i, ref in enumerate((first_ref, last_ref)):
        copies[i].wait()
        for x in range(16):
            ref[x, 0] = masked_line(raw[i, x], columns, x, 15 * i)


def x_edges_kernel(
    lines_ref, low_ref, high_ref, features_ref, first_ref, last_ref, raw, ends, sems
):
    copies = [
        pltpu.make_async_copy(features_ref.at[15 * i], raw.at[i], sems.at[i]) for i in range(2)
    ]
    for i in range(2):
        for j, ref in enumerate((low_ref, high_ref)):
            copies.append(
                pltpu.make_async_copy(ref.at[15 * i], ends.at[i, j], sems.at[2 + 2 * i + j])
            )
    for copy in copies:
        copy.start()
    columns = line_columns(lines_ref)
    for i, ref in enumerate((first_ref, last_ref)):
        for j in range(2):
            copies[2 + 2 * i + j].wait()
            ref[0, 17 * j : 17 * j + 1] = ends[i, j]
        copies[i].wait()
        for y in range(16):
            ref[0, 1 + y] = masked_line(raw[i, y], columns, 15 * i, y)


def routes_kernel(owner_ref, route_ref, met):
    for i in range(17):
        met[i] = 0
    for i in range(COUNT):
        route_ref[i] = 0 if i < SENT else -1

    def route(i, carry):
        owned = owner_ref[i // 32, i // 16 % 2, i % 16]

        @pl.when(owned >= 0)
        def _():
            owner = owned // 16
            slot = 2 * owner + met[owner]
            rank = met[16]
            met[owner] = met[owner] + 1
            met[16] = rank + 1
            route_ref[rank] = i
            route_ref[SLOTS + rank] = slot
            route_ref[SENT + slot] = owned % 16

        return carry

    lax.fori_loop(0, 64, route, 0)
    route_ref[COUNT] = met[16]
    route_ref[COUNT + 1] = (met[16] + 2 * GROUP - 1) // (2 * GROUP)


def find_routes(owner_map):
    scalars = pl.BlockSpec(memory_space=pltpu.SMEM)
    return pl.pallas_call(
        routes_kernel,
        in_specs=[scalars],
        out_specs=scalars,
        out_shape=jax.ShapeDtypeStruct((COUNT + 2,), jnp.int32),
        scratch_shapes=[pltpu.SMEM((17,), jnp.int32)],
    )(owner_map)


def y_edges(owner_map, occupancy, features):
    whole = pl.BlockSpec(memory_space=pltpu.VMEM)
    return pl.pallas_call(
        y_edges_kernel,
        in_specs=[whole, whole, pl.BlockSpec(memory_space=pl.ANY)],
        out_specs=[whole] * 3,
        out_shape=[jax.ShapeDtypeStruct((256, 128), jnp.float32)]
        + [jax.ShapeDtypeStruct((16, 1, 128, C), jnp.bfloat16)] * 2,
        scratch_shapes=[
            pltpu.VMEM((2, 16, 128, C), jnp.bfloat16),
            pltpu.SemaphoreType.DMA((2,)),
        ],
        compiler_params=pltpu.CompilerParams(vmem_limit_bytes=53 * MIB),
    )(owner_map, occupancy, features)


def x_edges(lines, y_low, y_high, features):
    whole = pl.BlockSpec(memory_space=pltpu.VMEM)
    return pl.pallas_call(
        x_edges_kernel,
        in_specs=[whole] + [pl.BlockSpec(memory_space=pl.ANY)] * 3,
        out_specs=[whole] * 2,
        out_shape=[jax.ShapeDtypeStruct((1, 18, 128, C), jnp.bfloat16)] * 2,
        scratch_shapes=[
            pltpu.VMEM((2, 16, 128, C), jnp.bfloat16),
            pltpu.VMEM((2, 2, 1, 128, C), jnp.bfloat16),
            pltpu.SemaphoreType.DMA((6,)),
        ],
        compiler_params=pltpu.CompilerParams(vmem_limit_bytes=51 * MIB),
    )(lines, y_low, y_high, features)


def on_device(features, occupancy, owner_map, kernel, norm_gain, norm_bias):
    lines, y_first, y_last = y_edges(owner_map, occupancy.reshape(256, 128), features)
    y_low, y_high = neighbours(y_first, y_last, "gy")
    routes = find_routes(owner_map)
    x_low, x_high = neighbours(*x_edges(lines, y_low, y_high, features), "gx")
    conv, centre, partial, sums = convolve(routes, features, y_low, y_high, lines, kernel)
    face_conv, spread = correct_faces(routes, x_low, x_high, partial, sums, lines, kernel)
    totals = swap(spread, ("gx", "gy"))
    result = finish(
        routes, conv, centre, face_conv, totals, norm_gain.reshape(1, C), norm_bias.reshape(1, C)
    )
    received = swap(result.reshape(16, 2, 512, C), "gx").reshape(32, 512, C)
    return pick(totals, received).reshape(O, 1, 512, C)


def solution(mesh):
    in_specs = (P("gx", "gy", None, None), P("gx", "gy", None), P("gx", "gy", None), P(), P(), P())
    out_specs = P("gx", "gy", None, None)
    return jax.shard_map(
        on_device, mesh=mesh, in_specs=in_specs, out_specs=out_specs, check_vma=False
    )
```

```python
import functools

import jax
import jax.numpy as jnp
from jax import lax
from jax.experimental import pallas as pl
from jax.experimental.pallas import tpu as pltpu
from jax.sharding import PartitionSpec as P

O = 16
SLOTS, SENT, COUNT = 48, 96, 128
E = 8
C = 128
GROUP = 4
ABSENT = -1e30
EPSILON = 1e-05
MIB = 1 << 20


def pair_taps(weight_ref, taps_ref, index):
    blank = jnp.zeros((C, C), jnp.bfloat16)
    for a in range(weight_ref.shape[0]):
        for dz in range(3):
            for j in range(4):
                at = (dz * 4 + j) * C
                weight_ref[a, at : at + C, 0:C] = (
                    taps_ref[index(a, dz, j)] if j < 3 else blank
                )
                weight_ref[a, at : at + C, C : 2 * C] = (
                    taps_ref[index(a, dz, j - 1)] if j > 0 else blank
                )


def shifted_scratch():
    return pltpu.VMEM((2, 3, 2, GROUP, 5, 5, 16, C), jnp.bfloat16)


def conv_kernel(
    route_ref,
    features_ref,
    y_low_ref,
    y_high_ref,
    taps_hbm,
    occupied_ref,
    conv_ref,
    centre_ref,
    face_ref,
    sums_ref,
    stage,
    out_sems,
    padded,
    raw,
    margins,
    columns_ref,
    taps_ref,
    weight_ref,
    shifted_a,
    shifted_b,
    total_a,
    total_b,
    sems,
):
    count, steps = route_ref[COUNT], route_ref[COUNT + 1]
    chunks = [
        pltpu.make_async_copy(
            features_ref.at[4 * i : 4 * i + 4], raw.at[i % 2], sems.at[i]
        )
        for i in range(4)
    ]
    lane = lax.broadcasted_iota(jnp.int32, (E, C), 1)

    def place_of(k):
        place = route_ref[k]
        return place // 32, place // 16 % 2, place % 16

    def prepare(group, shifted):
        for b in range(GROUP):
            bx, by, bz = place_of(group * GROUP + b)
            for dz in range(3):
                for xx in range(10):
                    lines = [
                        padded[bx * E + xx, by * E + yy, pl.ds(bz * E + 7 + dz, E), :]
                        for yy in range(10)
                    ]
                    for parity in range(2):
                        for yp in range(5 - parity):
                            pair = jnp.concatenate(
                                [lines[2 * yp + parity], lines[2 * yp + parity + 1]], axis=0
                            )
                            shifted[parity, dz, xx % 2, b, xx // 2, yp] = pair.astype(jnp.bfloat16)

    def multiply(shifted, total):
        for dy in range(3):
            parity, first = dy % 2, dy // 2
            parts = []
            for dz in range(3):
                for j in range(4):
                    part = shifted[
                        parity, dz, j % 2, :, j // 2 : j // 2 + 4, first : first + 4, :, :
                    ]
                    parts.append(part.reshape(GROUP * 256, C))
            product = jnp.dot(
                jnp.concatenate(parts, axis=1),
                weight_ref[dy],
                preferred_element_type=jnp.float32,
            )
            if dy == 0:
                total[...] = product
            else:
                total[...] += product

    def emit(group, shifted, total, parity, at):
        summed = jnp.zeros((E, C), jnp.float32)
        squared = jnp.zeros((E, C), jnp.float32)
        counted = jnp.zeros((E, C), jnp.float32)
        for b in range(GROUP):
            k = group * GROUP + b
            bx, by, bz = place_of(k)
            valid = jnp.where(k < count, 1.0, 0.0)
            near = columns_ref[bx, pl.ds(pl.multiple_of(bz * E, E), E), :] * valid
            near = pltpu.roll(near, C - by * E, axis=1)
            counted += jnp.where(lane % 16 < E, near, 0.0)
            for x in range(E):
                live = jnp.concatenate(
                    [
                        jnp.broadcast_to(near[:, x * 16 + y : x * 16 + y + 1], (E, C))
                        for y in range(E)
                    ],
                    axis=0,
                )
                block = total[b * 256 + (x // 2) * 64 : b * 256 + (x // 2) * 64 + 64,
                              (x % 2) * C : (x % 2 + 1) * C]
                wide = (block * live).astype(jnp.bfloat16).astype(jnp.float32)
                kept = wide
                if x == 0:
                    kept = wide * jnp.where(bx == 0, 0.0, 1.0)
                    face_low = block
                if x == E - 1:
                    kept = wide * jnp.where(bx == 0, 1.0, 0.0)
                    face_ref[k] = jnp.where(bx == 0, face_low, block)
                summed += jnp.sum(kept.reshape(E, E, C), axis=0)
                squared += jnp.sum((kept * kept).reshape(E, E, C), axis=0)
                stage[parity, 0, at + b, x * 64 : (x + 1) * 64, :] = jnp.where(
                    live > 0.5, wide, ABSENT
                ).astype(jnp.bfloat16)
                stage[parity, 1, at + b, x * 64 : (x + 1) * 64, :] = shifted[
                    1, 1, (x + 1) % 2, b, (x + 1) // 2, 0:4
                ].reshape(64, C)
        sums_ref[0] += summed
        sums_ref[1] += squared
        sums_ref[2] += counted

    extra = [
        pltpu.make_async_copy(y_low_ref, margins.at[0], sems.at[4]),
        pltpu.make_async_copy(y_high_ref, margins.at[1], sems.at[5]),
        pltpu.make_async_copy(taps_hbm, taps_ref, sems.at[6]),
    ]
    for copy in [chunks[0], chunks[1]] + extra:
        copy.start()
    edge = jnp.zeros((18, 18, E, C), jnp.float32)
    padded[:, :, 0:8, :] = edge
    padded[:, :, 136:144, :] = edge
    side = jnp.zeros((18, 128, C), jnp.float32)
    padded[0, :, 8:136, :] = side
    padded[17, :, 8:136, :] = side
    sums_ref[...] = jnp.zeros_like(sums_ref)
    for i in range(2):
        columns_ref[i] = jnp.transpose(occupied_ref[128 * i : 128 * i + 128, :])
    eye = jnp.where(
        lax.broadcasted_iota(jnp.int32, (C, C), 0) == lax.broadcasted_iota(jnp.int32, (C, C), 1),
        1.0,
        0.0,
    )
    ones = jnp.ones((C, C), jnp.bfloat16)
    for i in range(4):
        chunks[i].wait()
        columns = columns_ref[i // 2]

        def mask_plane(j, carry, i=i, columns=columns):
            near = pltpu.roll(columns, 128 - 64 * (i % 2) - 16 * j, axis=1)
            near = near.astype(jnp.bfloat16)
            for y in range(16):
                if y % 3 == 1:
                    line = occupied_ref[pl.ds((4 * i + j) * 16 + y, 1), :]
                    live = jnp.dot(
                        (eye * line).astype(jnp.bfloat16),
                        ones,
                        preferred_element_type=jnp.float32,
                    ).astype(jnp.bfloat16)
                else:
                    live = jnp.broadcast_to(near[:, y : y + 1], (128, C))
                padded[1 + 4 * i + j, 1 + y, 8:136, :] = (
                    (raw[i % 2, j, y] * live).astype(jnp.float32)
                )
            return carry

        lax.fori_loop(0, 4, mask_plane, 0)
        if i < 2:
            chunks[i + 2].start()
    for copy in extra:
        copy.wait()
    for side in range(2):
        padded[1:17, 17 * side, 8:136, :] = (
            margins[side].reshape(16, 128, C).astype(jnp.float32)
        )
    pair_taps(weight_ref, taps_ref, lambda dy, dz, dx: 9 * dx + 3 * dy + dz)

    @pl.when(steps > 0)
    def _():
        prepare(0, shifted_a)

    def outgoing(step):
        rows = pl.ds(step * 2 * GROUP, 2 * GROUP)
        return [
            pltpu.make_async_copy(
                stage.at[step % 2, i], ref.at[rows], out_sems.at[step % 2, i]
            )
            for i, ref in enumerate((conv_ref, centre_ref))
        ]

    def drain(step):
        for copy in outgoing(step):
            copy.wait()

    def pair(step, carry):
        @pl.when(step >= 2)
        def _():
            drain(step - 2)

        prepare(2 * step + 1, shifted_b)
        multiply(shifted_a, total_a)
        emit(2 * step, shifted_a, total_a, step % 2, 0)
        multiply(shifted_b, total_b)
        emit(2 * step + 1, shifted_b, total_b, step % 2, GROUP)
        prepare(2 * step + 2, shifted_a)

        for copy in outgoing(step):
            copy.start()
        return carry

    lax.fori_loop(0, steps, pair, 0)

    @pl.when(steps >= 2)
    def _():
        drain(steps - 2)

    @pl.when(steps >= 1)
    def _():
        drain(steps - 1)


def convolve(routes, features, y_low, y_high, occupied, taps):
    any_spec = pl.BlockSpec(memory_space=pl.ANY)
    whole = pl.BlockSpec(memory_space=pltpu.VMEM)
    scalars = pl.BlockSpec(memory_space=pltpu.SMEM)
    return pl.pallas_call(
        conv_kernel,
        in_specs=[scalars] + [any_spec] * 4 + [whole],
        out_specs=[any_spec] * 2 + [whole] * 2,
        out_shape=[
            jax.ShapeDtypeStruct((32, 512, C), jnp.bfloat16),
            jax.ShapeDtypeStruct((32, 512, C), jnp.bfloat16),
            jax.ShapeDtypeStruct((32, 64, C), jnp.float32),
            jax.ShapeDtypeStruct((3, E, C), jnp.float32),
        ],
        scratch_shapes=[
            pltpu.VMEM((2, 2, 2 * GROUP, 512, C), jnp.bfloat16),
            pltpu.SemaphoreType.DMA((2, 2)),
            pltpu.VMEM((18, 18, 144, C), jnp.float32),
            pltpu.VMEM((2, 4, 16, 128, C), jnp.bfloat16),
            pltpu.VMEM((2, 16, 1, 128, C), jnp.bfloat16),
            pltpu.VMEM((2, C, C), jnp.float32),
            pltpu.VMEM((27, C, C), jnp.bfloat16),
            pltpu.VMEM((3, 12 * C, 2 * C), jnp.bfloat16),
            shifted_scratch(),
            shifted_scratch(),
            pltpu.VMEM((GROUP * 256, 2 * C), jnp.float32),
            pltpu.VMEM((GROUP * 256, 2 * C), jnp.float32),
            pltpu.SemaphoreType.DMA((7,)),
        ],
        compiler_params=pltpu.CompilerParams(vmem_limit_bytes=49 * MIB),
        cost_estimate=pl.CostEstimate(
            flops=2 * 32 * 256 * 4608 * 256, bytes_accessed=30 * MIB, transcendentals=0
        ),
    )(routes, features, y_low, y_high, taps, occupied)


def face_kernel(
    route_ref,
    x_low_ref,
    x_high_ref,
    partial_hbm,
    sums_ref,
    occupied_ref,
    taps_ref,
    out_ref,
    norm_ref,
    partial_ref,
    buffer,
    sems,
    columns_ref,
    padded,
    shifted,
    added,
    weight_ref,
):
    count = route_ref[COUNT]
    fetch = pltpu.make_async_copy(partial_hbm, partial_ref, sems.at[8])
    fetch.start()
    pair_taps(weight_ref, taps_ref, lambda side, dz, dy: 18 * side + 3 * dy + dz)
    for i in range(2):
        columns_ref[i] = jnp.transpose(occupied_ref[128 * i : 128 * i + 128, :])
    padded[:, 0:8, :] = jnp.zeros((18, E, C), jnp.float32)
    padded[:, 136:144, :] = jnp.zeros((18, E, C), jnp.float32)
    for side, ref in enumerate((x_low_ref, x_high_ref)):
        padded[:, 8:136, :] = ref[0].astype(jnp.float32)
        for dz in range(3):
            shifted[dz] = padded[:, 7 + dz : 135 + dz, :].astype(jnp.bfloat16).reshape(
                9, 2, 128, C
            )
        parts = []
        for dz in range(3):
            for j in range(4):
                parts.append(shifted[dz, j // 2 : j // 2 + 8, j % 2].reshape(1024, C))
        added[side] = jnp.dot(
            jnp.concatenate(parts, axis=1), weight_ref[side], preferred_element_type=jnp.float32
        )

    fetch.wait()

    def outgoing(i):
        rows = pl.ds(i * GROUP, GROUP)
        return pltpu.make_async_copy(buffer.at[rows], out_ref.at[rows], sems.at[i])

    def several(i, carry):
        summed, squared = carry
        for b in range(GROUP):
            k = i * GROUP + b
            place = route_ref[k]
            bx, by, bz = place // 32, place // 16 % 2, place % 16
            valid = jnp.where(k < count, 1.0, 0.0)
            near = columns_ref[bx, pl.ds(pl.multiple_of(bz * E, E), E), :] * valid
            near = pltpu.roll(near, C - bx * 112 - by * E, axis=1)
            live = jnp.concatenate(
                [jnp.broadcast_to(near[:, y : y + 1], (E, C)) for y in range(E)], axis=0
            )
            pieces = []
            for y in range(E):
                start = pl.multiple_of((by * 4 + y // 2) * 128 + bz * E, E)
                pieces.append(added[bx, pl.ds(start, E), (y % 2) * C : (y % 2 + 1) * C])
            block = partial_ref[k] + jnp.concatenate(pieces, axis=0)
            wide = (block * live).astype(jnp.bfloat16).astype(jnp.float32)
            wide = jnp.where(live > 0.5, wide, 0.0)
            buffer[k] = jnp.where(live > 0.5, wide, ABSENT).astype(jnp.bfloat16)
            summed += jnp.sum(wide.reshape(E, E, C), axis=0)
            squared += jnp.sum((wide * wide).reshape(E, E, C), axis=0)
        outgoing(i).start()
        return summed, squared

    rounds = (count + GROUP - 1) // GROUP
    summed, squared = lax.fori_loop(0, rounds, several, (sums_ref[0], sums_ref[1]))
    sums = [
        jnp.sum(summed, axis=0, keepdims=True),
        jnp.sum(squared, axis=0, keepdims=True),
        jnp.broadcast_to(jnp.sum(sums_ref[2]), (1, C)),
    ]
    first_lane = lax.broadcasted_iota(jnp.int32, (1, C), 1) == 0
    for i in range(16):
        pair = jnp.where(first_lane, route_ref[SENT + 2 * i], route_ref[SENT + 2 * i + 1])
        table = jnp.concatenate(sums + [pair.astype(jnp.float32)], axis=0)
        norm_ref[8 * i : 8 * i + 8] = jnp.broadcast_to(table[None], (8, 4, C))

    def drain(i, carry):
        outgoing(i).wait()
        return carry

    lax.fori_loop(0, rounds, drain, 0)


def correct_faces(routes, x_low, x_high, partial, sums, occupied, taps):
    any_spec = pl.BlockSpec(memory_space=pl.ANY)
    whole = pl.BlockSpec(memory_space=pltpu.VMEM)
    scalars = pl.BlockSpec(memory_space=pltpu.SMEM)
    return pl.pallas_call(
        face_kernel,
        in_specs=[scalars, whole, whole, any_spec] + [whole] * 3,
        out_specs=[any_spec, whole],
        out_shape=[
            jax.ShapeDtypeStruct((32, 64, C), jnp.bfloat16),
            jax.ShapeDtypeStruct((128, 4, C), jnp.float32),
        ],
        scratch_shapes=[
            pltpu.VMEM((32, 64, C), jnp.float32),
            pltpu.VMEM((32, 64, C), jnp.bfloat16),
            pltpu.SemaphoreType.DMA((9,)),
            pltpu.VMEM((2, C, C), jnp.float32),
            pltpu.VMEM((18, 144, C), jnp.float32),
            pltpu.VMEM((3, 9, 2, 128, C), jnp.bfloat16),
            pltpu.VMEM((2, 1024, 2 * C), jnp.float32),
            pltpu.VMEM((2, 12 * C, 2 * C), jnp.bfloat16),
        ],
        compiler_params=pltpu.CompilerParams(vmem_limit_bytes=32 * MIB),
    )(routes, x_low, x_high, partial, sums, occupied, taps)


def finish_kernel(
    route_ref,
    conv_hbm,
    centre_hbm,
    face_ref,
    sums_ref,
    gain_ref,
    bias_ref,
    out_ref,
    conv_ref,
    centre_ref,
    buffer,
    in_sems,
    sems,
):
    count = route_ref[COUNT]

    def incoming(group):
        rows = pl.ds(group * GROUP, GROUP)
        return [
            pltpu.make_async_copy(hbm.at[rows], ref.at[rows], in_sems.at[i, group])
            for i, (hbm, ref) in enumerate(((conv_hbm, conv_ref), (centre_hbm, centre_ref)))
        ]

    for group in range(32 // GROUP):

        @pl.when(group * GROUP < count)
        def _():
            for each in incoming(group):
                each.start()

    sums = jnp.sum(sums_ref[...], axis=0)
    mean = sums[0:1] / sums[2:3]
    variance = sums[1:2] / sums[2:3] - mean * mean
    factor = 0.5 * (gain_ref[...] / jnp.sqrt(variance + EPSILON))
    bias = 0.5 * bias_ref[...]

    def copy(k):
        return pltpu.make_async_copy(buffer.at[k], out_ref.at[route_ref[SLOTS + k]], sems.at[k])

    def one(k, carry):
        @pl.when(k % GROUP == 0)
        def _():
            for each in incoming(k // GROUP):
                each.wait()

        bx = route_ref[k] // 32
        for x in range(E):
            conv = conv_ref[k, x * 64 : (x + 1) * 64, :].astype(jnp.float32)
            if x in (0, E - 1):
                own = face_ref[k].astype(jnp.float32)
                conv = jnp.where(bx == (0 if x == 0 else 1), own, conv)
            halved = factor * (conv - mean) + bias
            silu = halved + halved * jnp.tanh(halved)
            silu = jnp.where(conv > 0.5 * ABSENT, silu, 0.0)
            centre = centre_ref[k, x * 64 : (x + 1) * 64, :].astype(jnp.float32)
            buffer[k, x * 64 : (x + 1) * 64, :] = (centre + silu).astype(jnp.bfloat16)
        copy(k).start()
        return carry

    def drain(k, carry):
        copy(k).wait()
        return carry

    lax.fori_loop(0, count, one, 0)
    lax.fori_loop(0, count, drain, 0)


def finish(routes, conv, centre, face, sums, gain, bias):
    whole = pl.BlockSpec(memory_space=pltpu.VMEM)
    scalars = pl.BlockSpec(memory_space=pltpu.SMEM)
    return pl.pallas_call(
        finish_kernel,
        in_specs=[scalars] + [pl.BlockSpec(memory_space=pl.ANY)] * 2 + [whole] * 4,
        out_specs=pl.BlockSpec(memory_space=pl.ANY),
        scratch_shapes=[
            pltpu.VMEM((32, 512, C), jnp.bfloat16),
            pltpu.VMEM((32, 512, C), jnp.bfloat16),
            pltpu.VMEM((32, 512, C), jnp.bfloat16),
            pltpu.SemaphoreType.DMA((2, 32 // GROUP)),
            pltpu.SemaphoreType.DMA((32,)),
        ],
        out_shape=jax.ShapeDtypeStruct((32, 512, C), jnp.bfloat16),
        compiler_params=pltpu.CompilerParams(vmem_limit_bytes=56 * MIB),
    )(routes, conv, centre, face, sums, gain, bias)


def pick_kernel(named_ref, in_ref, out_ref, buffer, sems):
    named = named_ref[:, 3, :]
    lane = lax.broadcasted_iota(jnp.int32, (128, C), 1)
    device = lax.broadcasted_iota(jnp.int32, (128, C), 0)
    source = 2 * (device // 8) + lane
    beside = (lane < 2) & (device % 8 == lax.axis_index("gy"))
    named = jnp.where(beside, named, -1.0)
    reads, writes = [], []
    for i in range(O):
        index = jnp.sum(jnp.where(named == float(i), source, 0))
        reads.append(pltpu.make_async_copy(in_ref.at[index], buffer.at[i], sems.at[0, i]))
        reads[i].start()
        writes.append(pltpu.make_async_copy(buffer.at[i], out_ref.at[i], sems.at[1, i]))
    for read, write in zip(reads, writes):
        read.wait()
        write.start()
    for write in writes:
        write.wait()


def pick(named, received):
    return pl.pallas_call(
        pick_kernel,
        in_specs=[pl.BlockSpec(memory_space=pltpu.VMEM), pl.BlockSpec(memory_space=pl.ANY)],
        out_specs=pl.BlockSpec(memory_space=pl.ANY),
        scratch_shapes=[
            pltpu.VMEM((O, 512, C), jnp.bfloat16),
            pltpu.SemaphoreType.DMA((2, O)),
        ],
        out_shape=jax.ShapeDtypeStruct((O, 512, C), jnp.bfloat16),
    )(named, received)


def swap(spread, axis):
    return lax.all_to_all(spread, axis, 0, 0, tiled=True)


def neighbours(low_block, high_block, axis):
    count = lax.axis_size(axis)
    up = [(i, i + 1) for i in range(count - 1)]
    down = [(j, i) for i, j in up]
    return lax.ppermute(high_block, axis, up), lax.ppermute(low_block, axis, down)


def masked_line(line, columns, x, y):
    column = x % E * 16 + y
    live = jnp.broadcast_to(columns[x // E][:, column : column + 1], (128, C))
    return (line.astype(jnp.float32) * live).astype(jnp.bfloat16)


def line_columns(lines_ref):
    return [jnp.transpose(lines_ref[128 * i : 128 * i + 128, :]) for i in range(2)]


def y_edges_kernel(
    active_ref,
    occupancy_ref,
    features_ref,
    lines_ref,
    first_ref,
    last_ref,
    raw,
    sems,
):
    copies = [
        pltpu.make_async_copy(features_ref.at[:, 15 * i], raw.at[i], sems.at[i]) for i in range(2)
    ]
    for copy in copies:
        copy.start()
    repeat = jnp.where(
        lax.broadcasted_iota(jnp.int32, (16, C), 1) // E
        == lax.broadcasted_iota(jnp.int32, (16, C), 0),
        1.0,
        0.0,
    ).astype(jnp.bfloat16)
    for bx in range(2):
        spread = jnp.dot(
            jnp.where(active_ref[bx] >= 0, 1.0, 0.0).astype(jnp.bfloat16),
            repeat,
            preferred_element_type=jnp.float32,
        )
        for x in range(bx * E, bx * E + E):
            for by in range(2):
                at = x * 16 + by * E
                lines_ref[at : at + E, :] = (
                    occupancy_ref[at : at + E, :].astype(jnp.float32) * spread[by : by + 1, :]
                )
    columns = line_columns(lines_ref)
    for i, ref in enumerate((first_ref, last_ref)):
        copies[i].wait()
        for x in range(16):
            ref[x, 0] = masked_line(raw[i, x], columns, x, 15 * i)


def x_edges_kernel(
    lines_ref, low_ref, high_ref, features_ref, first_ref, last_ref, raw, ends, sems
):
    copies = [
        pltpu.make_async_copy(features_ref.at[15 * i], raw.at[i], sems.at[i]) for i in range(2)
    ]
    for i in range(2):
        for j, ref in enumerate((low_ref, high_ref)):
            copies.append(
                pltpu.make_async_copy(ref.at[15 * i], ends.at[i, j], sems.at[2 + 2 * i + j])
            )
    for copy in copies:
        copy.start()
    columns = line_columns(lines_ref)
    for i, ref in enumerate((first_ref, last_ref)):
        for j in range(2):
            copies[2 + 2 * i + j].wait()
            ref[0, 17 * j : 17 * j + 1] = ends[i, j]
        copies[i].wait()
        for y in range(16):
            ref[0, 1 + y] = masked_line(raw[i, y], columns, 15 * i, y)


def routes_kernel(owner_ref, route_ref, met):
    for i in range(17):
        met[i] = 0
    for i in range(COUNT):
        route_ref[i] = 0 if i < SENT else -1

    def route(i, carry):
        owned = owner_ref[i // 32, i // 16 % 2, i % 16]

        @pl.when(owned >= 0)
        def _():
            owner = owned // 16
            slot = 2 * owner + met[owner]
            rank = met[16]
            met[owner] = met[owner] + 1
            met[16] = rank + 1
            route_ref[rank] = i
            route_ref[SLOTS + rank] = slot
            route_ref[SENT + slot] = owned % 16

        return carry

    lax.fori_loop(0, 64, route, 0)
    route_ref[COUNT] = met[16]
    route_ref[COUNT + 1] = (met[16] + 2 * GROUP - 1) // (2 * GROUP)


def find_routes(owner_map):
    scalars = pl.BlockSpec(memory_space=pltpu.SMEM)
    return pl.pallas_call(
        routes_kernel,
        in_specs=[scalars],
        out_specs=scalars,
        out_shape=jax.ShapeDtypeStruct((COUNT + 2,), jnp.int32),
        scratch_shapes=[pltpu.SMEM((17,), jnp.int32)],
    )(owner_map)


def y_edges(owner_map, occupancy, features):
    whole = pl.BlockSpec(memory_space=pltpu.VMEM)
    return pl.pallas_call(
        y_edges_kernel,
        in_specs=[whole, whole, pl.BlockSpec(memory_space=pl.ANY)],
        out_specs=[whole] * 3,
        out_shape=[jax.ShapeDtypeStruct((256, 128), jnp.float32)]
        + [jax.ShapeDtypeStruct((16, 1, 128, C), jnp.bfloat16)] * 2,
        scratch_shapes=[
            pltpu.VMEM((2, 16, 128, C), jnp.bfloat16),
            pltpu.SemaphoreType.DMA((2,)),
        ],
        compiler_params=pltpu.CompilerParams(vmem_limit_bytes=53 * MIB),
    )(owner_map, occupancy, features)


def x_edges(lines, y_low, y_high, features):
    whole = pl.BlockSpec(memory_space=pltpu.VMEM)
    return pl.pallas_call(
        x_edges_kernel,
        in_specs=[whole] + [pl.BlockSpec(memory_space=pl.ANY)] * 3,
        out_specs=[whole] * 2,
        out_shape=[jax.ShapeDtypeStruct((1, 18, 128, C), jnp.bfloat16)] * 2,
        scratch_shapes=[
            pltpu.VMEM((2, 16, 128, C), jnp.bfloat16),
            pltpu.VMEM((2, 2, 1, 128, C), jnp.bfloat16),
            pltpu.SemaphoreType.DMA((6,)),
        ],
        compiler_params=pltpu.CompilerParams(vmem_limit_bytes=51 * MIB),
    )(lines, y_low, y_high, features)


def on_device(features, occupancy, owner_map, kernel, norm_gain, norm_bias):
    lines, y_first, y_last = y_edges(owner_map, occupancy.reshape(256, 128), features)
    y_low, y_high = neighbours(y_first, y_last, "gy")
    routes = find_routes(owner_map)
    x_low, x_high = neighbours(*x_edges(lines, y_low, y_high, features), "gx")
    conv, centre, partial, sums = convolve(routes, features, y_low, y_high, lines, kernel)
    face_conv, spread = correct_faces(routes, x_low, x_high, partial, sums, lines, kernel)
    totals = swap(spread, ("gx", "gy"))
    result = finish(
        routes, conv, centre, face_conv, totals, norm_gain.reshape(1, C), norm_bias.reshape(1, C)
    )
    received = swap(result.reshape(16, 2, 512, C), "gx").reshape(32, 512, C)
    return pick(totals, received).reshape(O, 1, 512, C)


def solution(mesh):
    in_specs = (P("gx", "gy", None, None), P("gx", "gy", None), P("gx", "gy", None), P(), P(), P())
    out_specs = P("gx", "gy", None, None)
    return jax.shard_map(
        on_device, mesh=mesh, in_specs=in_specs, out_specs=out_specs, check_vma=False
    )
```
